128 devices in a mesh: ctx: 16 (over x, y), exp: 8 (over z, core).
Axes of the slice: x: 4, y: 4, z: 4, core: 2. Of those that a mesh axis runs over, the one named last changes fastest.
Arguments:
- queries: bfloat16 [8, 2048, 2304], P('exp', 'ctx'), may hold values from -6 to 6
- key_vectors: bfloat16 [8, 2048, 2304], P('exp', 'ctx'), may hold values from -0.3125 to 0.3125
- values: bfloat16 [8, 2048, 2304], P('exp', 'ctx'), may hold values from -6 to 6
- log_decay: bfloat16 [8, 2048, 2304], P('exp', 'ctx')
- starts: int32 [8, 2048], P('exp', 'ctx'), may hold values 0 or 1
- residual_in: bfloat16 [8, 2048, 2304], P('exp', 'ctx'), may hold values from -6 to 6
- out_grad: bfloat16 [8, 2048, 2304], P('exp', 'ctx'), may hold values from -6 to 6
- expert_ids: int32 [8, 2048, 8], P('exp', 'ctx'), may hold values from 0 to 127, as said below
- slot_index: int32 [8, 2048, 8], P('exp', 'ctx'), may hold values from 0 to 127, as said below
- router: bfloat16 [2304, 128], replicated, may hold values from -0.125 to 0.125
- hidden_saved: bfloat16 [128, 1536, 512], P(('ctx', 'exp')), may hold values from -16 to 16
- w_down: bfloat16 [128, 512, 2304], P(('ctx', 'exp')), may hold values from -0.09375 to 0.09375
- momentum: bfloat16 [128, 512, 2304], P(('ctx', 'exp')), may hold values from -1.75 to 1.75
Outputs:
- grad_queries: bfloat16 [8, 2048, 2304], P('exp', 'ctx')
- grad_keys: bfloat16 [8, 2048, 2304], P('exp', 'ctx')
- grad_values: bfloat16 [8, 2048, 2304], P('exp', 'ctx')
- grad_decay: bfloat16 [8, 2048, 2304], P('exp', 'ctx')
- grad_residual: bfloat16 [8, 2048, 2304], P('exp', 'ctx')
- new_weights: bfloat16 [128, 512, 2304], P(('ctx', 'exp'))
- new_momentum: bfloat16 [128, 512, 2304], P(('ctx', 'exp'))
The draws below stay inside these ranges and needn't reach their ends.
Inputs may be any that keep to these rules, and one draw needn't show every extreme that they name: `expert_ids`: each token's 8 experts are distinct; loads differ strongly between experts. slot_index[s, t, j] counts the routes to the same expert that come earlier, in order of token and then of j, among the tokens of the same device (the 128 tokens of one block of one sequence); routes with a slot of 12 or more are dropped, and some are in every draw.
All inputs are finite; a program needn't handle non-finite values. No bound on the sum of `starts` on one device may be relied on, other than what follows from the above.
Results may differ from the reference program's by a relative error of at most 0.019.
Values may be sent and summed in bfloat16 or wider, within the bound.
A program may use at most 192 MiB of HBM per device.

```python
import math
import jax
import jax.numpy as jnp
from jax import lax

TOK_DEV = 128
D = 2304
HEADS = 18
HD = 128
FF = 512
TOP = 8
SEQUENCE_LENGTH = 2048
SEQUENCE_COUNT = 8
EXPERTS = 128
SLOTS = 12
CAP = 1536


def route_table(key):
    popular = jax.random.randint(jax.random.fold_in(key, 11), (EXPERTS,), 0, 3) * 6000
    hot_expert = jax.random.randint(jax.random.fold_in(key, 12), (), 0, EXPERTS)
    popular = jnp.where(jnp.arange(EXPERTS) == hot_expert, 80000, popular)
    noise_draw = jax.random.randint(jax.random.fold_in(key, 13), (SEQUENCE_COUNT, SEQUENCE_LENGTH, EXPERTS), 0, 65536)
    scores = (noise_draw + popular[None, None, :]) * EXPERTS + jnp.arange(EXPERTS, dtype=jnp.int32)
    ranked, chosen_ids = lax.top_k(scores, TOP)
    return chosen_ids.astype(jnp.int32)


def draw_expert_ids(key, part):
    return route_table(key)


def draw_slot_index(key, part):
    chosen_ids = route_table(key)
    block_count = SEQUENCE_LENGTH // TOK_DEV
    flat_ids = chosen_ids.reshape(SEQUENCE_COUNT, block_count, TOK_DEV * TOP)
    onehot = (flat_ids[..., None] == jnp.arange(EXPERTS, dtype=jnp.int32)).astype(jnp.int32)
    before = jnp.cumsum(onehot, axis=2, dtype=jnp.int32) - onehot
    slot_rank = jnp.sum(before * onehot, axis=-1)
    return slot_rank.reshape(SEQUENCE_COUNT, SEQUENCE_LENGTH, TOP).astype(jnp.int32)


def draw_log_decay(key, part):
    key = jax.random.fold_in(key, 5)
    random_subkeys = jax.random.split(key, 6)
    slow_share = 0.5
    fast_rate = jnp.exp(jax.random.uniform(random_subkeys[0], (D,), jnp.float32, math.log(1.0 / 50.0), math.log(1.0 / 30.0)))
    slow_rate = jnp.exp(jax.random.uniform(random_subkeys[1], (D,), jnp.float32, math.log(0.05 / SEQUENCE_LENGTH), math.log(0.5 / SEQUENCE_LENGTH)))
    slow_pick = jax.random.uniform(random_subkeys[2], (D,), jnp.float32) < slow_share
    channel_speed = jnp.where(slow_pick, slow_rate, fast_rate)
    jaggedness = jax.random.uniform(random_subkeys[3], (SEQUENCE_COUNT, SEQUENCE_LENGTH, D), jnp.float32, 0.5, 2.0)
    spike_mask = jax.random.uniform(random_subkeys[4], (SEQUENCE_COUNT, SEQUENCE_LENGTH, 1), jnp.float32) < 2.0 / SEQUENCE_LENGTH
    spike_depth = jax.random.uniform(random_subkeys[5], (SEQUENCE_COUNT, SEQUENCE_LENGTH, 1), jnp.float32, 0.2, 0.7)
    return (-channel_speed * jaggedness - jnp.where(spike_mask, spike_depth, 0.0)).astype(jnp.bfloat16)


def with_ends(drawn, own_key, least, top_value):
    extent = drawn.shape
    place = [jax.random.randint(jax.random.fold_in(own_key, axis), (), 0, extent[axis]) for axis in range(len(extent))]
    drawn = drawn.at[tuple(place)].set(least)
    longest = extent.index(max(extent))
    place[longest] = (place[longest] + 1) % extent[longest]
    return drawn.at[tuple(place)].set(top_value)


def steps_of(key, shape, cuts, least, top_value):
    factor_of = 1.0
    for dim, shards_of in cuts:
        draws = jax.random.uniform(jax.random.fold_in(jax.random.fold_in(key, 6), dim), (shards_of,), jnp.float32, least / len(cuts), top_value / len(cuts))
        factor_of = factor_of * jnp.repeat(jnp.exp(draws), shape[dim] // shards_of).reshape((-1,) + (1,) * (len(shape) - 1 - dim))
    return factor_of


def bell_draw(own_key, extent, spread, limit, cuts=(), held_as=jnp.bfloat16):
    result = spread * jax.random.normal(own_key, extent, jnp.float32)
    if cuts:
        result = result * steps_of(own_key, extent, cuts, -0.22, 0.18)
    return jnp.clip(result, -limit, limit).astype(held_as)


def setup_inputs(seed: int = 0) -> dict:
    key_of = jax.random.split(jax.random.key(seed), 14)
    queries = bell_draw(key_of[0], (SEQUENCE_COUNT, SEQUENCE_LENGTH, D), 1.0, 6.0, ((0, 8), (1, 16)))
    key_vectors = bell_draw(key_of[1], (SEQUENCE_COUNT, SEQUENCE_LENGTH, D), 0.05, 0.3125, ((0, 8), (1, 16)))
    values = bell_draw(key_of[2], (SEQUENCE_COUNT, SEQUENCE_LENGTH, D), 1.0, 6.0, ((0, 8), (1, 16)))
    log_decay = draw_log_decay(jax.random.fold_in(key_of[13], 71), 0)
    starts = with_ends((jax.random.randint(key_of[4], (SEQUENCE_COUNT, SEQUENCE_LENGTH), 0, SEQUENCE_LENGTH // 4) < 1).astype(jnp.int32), jax.random.fold_in(key_of[4], 1), 0, 1)
    residual_in = bell_draw(key_of[5], (SEQUENCE_COUNT, SEQUENCE_LENGTH, D), 1.0, 6.0, ((0, 8), (1, 16)))
    out_grad = bell_draw(key_of[6], (SEQUENCE_COUNT, SEQUENCE_LENGTH, D), 1.0, 6.0, ((0, 8), (1, 16)))
    expert_ids = draw_expert_ids(jax.random.fold_in(key_of[13], 71), 0)
    slot_index = draw_slot_index(jax.random.fold_in(key_of[13], 71), 0)
    router = bell_draw(key_of[9], (D, EXPERTS), D ** -0.5, 0.125)
    hidden_saved = bell_draw(key_of[10], (EXPERTS, CAP, FF), 3.0, 16.0, ((0, 128),))
    w_down = bell_draw(key_of[11], (EXPERTS, FF, D), (9 * FF) ** -0.5, 0.09375, ((0, 128),))
    momentum = bell_draw(key_of[12], (EXPERTS, FF, D), 0.3, 1.75, ((0, 128),))
    return {"queries": queries, "key_vectors": key_vectors, "values": values, "log_decay": log_decay, "starts": starts, "residual_in": residual_in, "out_grad": out_grad, "expert_ids": expert_ids, "slot_index": slot_index, "router": router, "hidden_saved": hidden_saved, "w_down": w_down, "momentum": momentum}


NORM_EPS = 1e-06
LION_RATE = 0.001
BETA_ONE = 0.9
BETA_TWO = 0.99
WEIGHT_DECAY = 0.1
HIGHEST_PRECISION = lax.Precision.HIGHEST

def summary(key_block, value_block, decay_block, start_block):
    cumul = jnp.cumsum(decay_block, axis=0)
    segment = jnp.cumsum(start_block, dtype=jnp.int32)
    last_cum = cumul[-1]
    tail_mask = (segment == segment[-1]).astype(jnp.float32)
    key_end = key_block * jnp.exp(last_cum[None] - cumul) * tail_mask[:, None, None]
    fresh = jnp.einsum('shd,she->hde', key_end, value_block, precision=HIGHEST_PRECISION)
    passing = jnp.exp(last_cum) * (segment[-1] == 0).astype(jnp.float32)
    return (passing, fresh)

def block_forward(query_block, key_block, value_block, decay_block, start_block, in_state):
    length = query_block.shape[0]
    scaling = query_block.shape[2] ** (-0.5)
    cumul = jnp.cumsum(decay_block, axis=0)
    segment = jnp.cumsum(start_block, dtype=jnp.int32)
    position = jnp.arange(length, dtype=jnp.int32)
    allowed = (segment[:, None] == segment[None, :]) & (position[:, None] >= position[None, :])
    carried = (segment == 0).astype(jnp.float32)
    q_dec = query_block * jnp.exp(cumul)
    k_dec = key_block * jnp.exp(-cumul)
    scores = jnp.einsum('thd,shd->hts', q_dec, k_dec, precision=HIGHEST_PRECISION)
    scores = jnp.where(allowed[None], scores, 0.0)
    within = jnp.einsum('hts,she->the', scores, value_block, precision=HIGHEST_PRECISION)
    q_carried = q_dec * carried[:, None, None]
    inbound = jnp.einsum('thd,hde->the', q_carried, in_state, precision=HIGHEST_PRECISION)
    passing, fresh = summary(key_block, value_block, decay_block, start_block)
    return (scaling * (within + inbound), passing, fresh, q_carried)

def compose(earlier, later_pair):
    return (later_pair[0] * earlier[0], later_pair[0][..., None] * earlier[1] + later_pair[1])

def expert_step(saved, weight, moment, gathered, route_weight):
    produced = jnp.dot(saved, weight, preferred_element_type=jnp.float32).astype(jnp.bfloat16)
    scaled = (route_weight.astype(jnp.float32)[:, None] * gathered.astype(jnp.float32)).astype(jnp.bfloat16)
    gradient = lax.dot_general(saved, scaled, (((0,), (0,)), ((), ())), preferred_element_type=jnp.float32)
    weight_float = weight.astype(jnp.float32)
    moment_float = moment.astype(jnp.float32)
    direction = jnp.sign(BETA_ONE * moment_float + (1.0 - BETA_ONE) * gradient)
    new_weight = (weight_float - LION_RATE * (direction + WEIGHT_DECAY * weight_float)).astype(jnp.bfloat16)
    new_moment = (BETA_TWO * moment_float + (1.0 - BETA_TWO) * gradient).astype(jnp.bfloat16)
    return (produced, new_weight, new_moment)

def attention(query_all, key_all, value_all, decay_all, starts):
    block_count = SEQUENCE_LENGTH // TOK_DEV

    def split_blocks(array):
        return array.reshape(SEQUENCE_COUNT, block_count, TOK_DEV, HEADS, HD).swapaxes(0, 1)
    start_blocks = starts.reshape(SEQUENCE_COUNT, block_count, TOK_DEV).swapaxes(0, 1)

    def block_step(in_state, block_items):
        query_block, key_block, value_block, decay_block, start_block = block_items
        outputs, passing, fresh, q_carried = jax.vmap(block_forward)(query_block, key_block, value_block, decay_block, start_block, in_state)
        return (passing[..., None] * in_state + fresh, outputs)
    zero_state = jnp.zeros((SEQUENCE_COUNT, HEADS, HD, HD), jnp.float32)
    block_items = (split_blocks(query_all), split_blocks(key_all), split_blocks(value_all), split_blocks(decay_all), start_blocks)
    final_state, outputs = lax.scan(block_step, zero_state, block_items)
    return outputs.swapaxes(0, 1).reshape(SEQUENCE_COUNT, SEQUENCE_LENGTH, D)

def reference(queries, key_vectors, values, log_decay, starts, residual_in, out_grad, expert_ids, slot_index, router, hidden_saved, w_down, momentum):

    def run_attention(query_all, key_all, value_all, decay_all):
        return attention(query_all, key_all, value_all, decay_all, starts)
    attended, pullback = jax.vjp(run_attention, queries.astype(jnp.float32), key_vectors.astype(jnp.float32), values.astype(jnp.float32), log_decay.astype(jnp.float32))
    tokens = SEQUENCE_COUNT * SEQUENCE_LENGTH
    attn_round = attended.astype(jnp.bfloat16).reshape(tokens, D)
    mixed = residual_in.reshape(tokens, D).astype(jnp.float32) + attn_round.astype(jnp.float32)
    inverse = lax.rsqrt(lax.optimization_barrier(jnp.mean(mixed * mixed, axis=-1, keepdims=True)) + NORM_EPS)
    normed = (mixed * inverse).astype(jnp.bfloat16)
    logits = jnp.dot(normed, router, preferred_element_type=jnp.float32)
    choose = expert_ids.reshape(tokens, TOP)
    slot_flat = slot_index.reshape(tokens, TOP)
    chosen = jnp.take_along_axis(logits, choose, axis=1)
    gate_values = jax.nn.sigmoid(chosen)
    gate_total = lax.optimization_barrier(jnp.sum(gate_values, axis=1, keepdims=True))
    weights = gate_values / gate_total
    keep_mask = slot_flat < SLOTS
    token_order = jnp.arange(tokens, dtype=jnp.int32)
    source = token_order % SEQUENCE_LENGTH // TOK_DEV * SEQUENCE_COUNT + token_order // SEQUENCE_LENGTH
    route_place = jnp.where(keep_mask, choose * CAP + source[:, None] * SLOTS + slot_flat, EXPERTS * CAP).astype(jnp.int32)
    flat_place = route_place.reshape(-1)
    owner_token = jnp.broadcast_to(token_order[:, None], (tokens, TOP)).reshape(-1)
    slot_table = jnp.full((EXPERTS * CAP,), tokens, jnp.int32).at[flat_place].set(owner_token, mode='drop').reshape(EXPERTS, CAP)
    weight_table = jnp.zeros((EXPERTS * CAP,), jnp.bfloat16).at[flat_place].set(weights.astype(jnp.bfloat16).reshape(-1), mode='drop').reshape(EXPERTS, CAP)
    grad_rows = out_grad.reshape(tokens, D)
    padded = jnp.concatenate([grad_rows, jnp.zeros((1, D), jnp.bfloat16)], axis=0)

    def per_expert(expert_items):
        saved, weight, moment, row_index, route_weight = expert_items
        gathered = padded[row_index]
        produced, new_weight, new_moment = expert_step(saved, weight, moment, gathered, route_weight)
        slot_score = lax.optimization_barrier(jnp.sum(gathered.astype(jnp.float32) * produced.astype(jnp.float32), axis=-1))
        return (slot_score, new_weight, new_moment)
    slot_scores, new_weights, new_momentum = lax.map(per_expert, (hidden_saved, w_down, momentum, slot_table, weight_table))
    picked = slot_scores.reshape(-1)[jnp.minimum(flat_place, EXPERTS * CAP - 1)]
    prob_grad = jnp.where(keep_mask, picked.reshape(tokens, TOP), 0.0)
    mix_sum = lax.optimization_barrier(jnp.sum(weights * prob_grad, axis=1, keepdims=True))
    chosen_grad = (prob_grad - mix_sum) / gate_total * gate_values * (1.0 - gate_values)
    onehot = (choose[:, :, None] == jnp.arange(EXPERTS, dtype=jnp.int32)).astype(jnp.float32)
    logit_grad = lax.optimization_barrier(jnp.sum(onehot * chosen_grad[:, :, None], axis=1)).astype(jnp.bfloat16)
    normed_grad = lax.dot_general(logit_grad, router, (((1,), (1,)), ((), ())), preferred_element_type=jnp.float32)
    mixed_grad = grad_rows.astype(jnp.float32) + inverse * normed_grad - mixed * inverse * inverse * inverse * lax.optimization_barrier(jnp.mean(normed_grad * mixed, axis=-1, keepdims=True))
    grad_residual = mixed_grad.astype(jnp.bfloat16)
    cotangent = grad_residual.astype(jnp.float32).reshape(SEQUENCE_COUNT, SEQUENCE_LENGTH, D)
    grad_q, grad_k, grad_v, grad_g = pullback(cotangent)
    return (grad_q.astype(jnp.bfloat16), grad_k.astype(jnp.bfloat16), grad_v.astype(jnp.bfloat16), grad_g.astype(jnp.bfloat16), grad_residual.reshape(SEQUENCE_COUNT, SEQUENCE_LENGTH, D), new_weights, new_momentum)
```

```python
import jax
import jax.numpy as jnp
from jax import lax
from jax.sharding import PartitionSpec as P

HEADS = 18
HD = 128
TOP = 8
NORM_EPS = 1e-06
LION_RATE = 0.001
BETA_ONE = 0.9
BETA_TWO = 0.99
WEIGHT_DECAY = 0.1
BF = jnp.bfloat16
F32 = jnp.float32


def mm(spec, a, b):
    return jnp.einsum(spec, a.astype(BF), b.astype(BF), preferred_element_type=F32)


def split(x):
    hi = x.astype(BF)
    lo = (x - hi.astype(F32)).astype(BF)
    return hi, lo


def heads(array):
    return array[0].reshape(array.shape[1], HEADS, HD).swapaxes(0, 1)


def unheads(array):
    return array.swapaxes(0, 1).reshape(1, array.shape[1], HEADS * HD)


def to_groups(state, count):
    return state.reshape(HEADS, count, HD // count, HD).swapaxes(0, 1)


def from_groups(parts, count):
    return parts.swapaxes(0, 1).reshape(HEADS, HD, HD)


def exchange(x, axis):
    return lax.all_to_all(x, axis, split_axis=0, concat_axis=0, tiled=True)


def scan_states(blocks, passing, reverse):
    count = blocks.shape[0]
    state = jnp.zeros(blocks.shape[1:], F32)
    out = [None] * count
    order = range(count - 1, -1, -1) if reverse else range(count)
    for j in order:
        out[j] = state.astype(BF)
        state = passing[j][:, None, :] * state + blocks[j].astype(F32)
    return jnp.stack(out)


def local(
    queries, key_vectors, values, log_decay, starts, residual_in, out_grad,
    expert_ids, slot_index, router, hidden_saved, w_down, momentum,
):
    tok = queries.shape[1]
    width = queries.shape[2]
    n_ctx = lax.axis_size("ctx")
    n_dev = lax.axis_size(("ctx", "exp"))
    scaling = HD ** (-0.5)
    n_exp = router.shape[1]
    slots = hidden_saved.shape[1] // n_dev
    ids = expert_ids[0]
    rank = slot_index[0]
    keep = rank < slots
    place = jnp.where(keep, ids * slots + rank, -1)
    rows = jnp.arange(n_exp * slots, dtype=jnp.int32)
    hit = jnp.zeros((n_exp * slots, tok), F32)
    for j in range(TOP):
        hit = hit + (rows[:, None] == place[None, :, j]).astype(F32)
    grad_rows = out_grad[0]
    outgoing = jnp.dot(hit.astype(BF), grad_rows, preferred_element_type=F32).astype(BF)
    incoming = exchange(outgoing.reshape(n_exp, slots, width), ("ctx", "exp"))
    start_row = starts[0]
    segment = jnp.cumsum(start_row, dtype=jnp.int32)
    position = jnp.arange(tok, dtype=jnp.int32)
    lower = position[:, None] >= position[None, :]
    allowed = (segment[:, None] == segment[None, :]) & lower
    carried = (segment == 0).astype(F32)[None, :, None]
    tail = (segment == segment[-1]).astype(F32)[None, :, None]
    q = heads(queries).astype(F32)
    k = heads(key_vectors).astype(F32)
    v = heads(values)
    g = heads(log_decay)
    tri = lower.astype(BF)
    cum = jnp.einsum("ts,hsd->htd", tri, g, preferred_element_type=F32)
    last = cum[:, -1:, :]
    grow = jnp.exp(cum)
    shrink = jnp.exp(-cum)
    end_decay = jnp.exp(last - cum) * tail
    q_dec = (q * grow).astype(BF)
    k_dec = (k * shrink).astype(BF)
    key_end = (k * end_decay).astype(BF)
    q_car = (q_dec * carried).astype(BF)
    fresh = mm("hse,hsd->hed", v, key_end)
    passing = jnp.exp(last[:, 0, :]) * (segment[-1] == 0).astype(F32)
    got = exchange(to_groups(fresh, n_ctx).astype(BF), "ctx")
    passing_all = lax.all_gather(passing.astype(BF), "ctx").astype(F32)
    state = from_groups(exchange(scan_states(got, passing_all, False), "ctx"), n_ctx)
    scores = jnp.where(allowed[None], mm("htd,hsd->hts", q_dec, k_dec), 0.0).astype(BF)
    attended = scaling * (mm("hts,hse->hte", scores, v) + mm("htd,hed->hte", q_car, state))
    attn_round = unheads(attended)[0].astype(BF)
    mixed = residual_in[0].astype(F32) + attn_round.astype(F32)
    inverse = lax.rsqrt(jnp.mean(mixed * mixed, axis=-1, keepdims=True) + NORM_EPS)
    normed = (mixed * inverse).astype(BF)
    logits = jnp.dot(normed, router, preferred_element_type=F32)
    onehot = (ids[:, :, None] == jnp.arange(n_exp, dtype=jnp.int32)).astype(F32)
    chosen = jnp.sum(onehot * logits[:, None, :], axis=-1)
    gate = jax.nn.sigmoid(chosen)
    total = jnp.sum(gate, axis=1, keepdims=True)
    weights = gate / total
    slot_ids = jnp.arange(slots, dtype=jnp.int32)
    slot_hot = (rank[:, :, None] == slot_ids).astype(F32)
    w_hot = slot_hot * weights.astype(BF).astype(F32)[:, :, None]
    w_out = jnp.einsum("tje,tjs->es", onehot, w_hot, precision=lax.Precision.HIGHEST)
    w_in = exchange(w_out.astype(BF), ("ctx", "exp"))
    gathered = incoming.reshape(n_dev * slots, width)
    saved = hidden_saved[0]
    produced = jnp.dot(saved, w_down[0], preferred_element_type=F32).astype(BF)
    slot_score = jnp.sum(gathered.astype(F32) * produced.astype(F32), axis=-1)
    score_back = exchange(slot_score.reshape(n_dev, slots), ("ctx", "exp"))
    scaled = (w_in.reshape(-1, 1).astype(F32) * gathered.astype(F32)).astype(BF)
    gradient = lax.dot_general(saved, scaled, (((0,), (0,)), ((), ())), preferred_element_type=F32)
    wf = w_down[0].astype(F32)
    mf = momentum[0].astype(F32)
    direction = jnp.sign(BETA_ONE * mf + (1.0 - BETA_ONE) * gradient)
    new_weight = (wf - LION_RATE * (direction + WEIGHT_DECAY * wf)).astype(BF)
    new_moment = (BETA_TWO * mf + (1.0 - BETA_TWO) * gradient).astype(BF)
    per_expert = jnp.einsum("tje,es->tjs", onehot, score_back, precision=lax.Precision.HIGHEST)
    prob_grad = jnp.sum(per_expert * slot_hot, axis=-1)
    mix_sum = jnp.sum(weights * prob_grad, axis=1, keepdims=True)
    chosen_grad = (prob_grad - mix_sum) / total * gate * (1.0 - gate)
    logit_grad = jnp.sum(onehot * chosen_grad[:, :, None], axis=1).astype(BF)
    normed_grad = lax.dot_general(logit_grad, router, (((1,), (1,)), ((), ())), preferred_element_type=F32)
    mixed_grad = (
        grad_rows.astype(F32)
        + inverse * normed_grad
        - mixed * inverse * inverse * inverse * jnp.mean(normed_grad * mixed, axis=-1, keepdims=True)
    )
    grad_residual = mixed_grad.astype(BF)
    cot = heads(grad_residual[None])
    adjoint = scaling * mm("hte,htd->hed", cot, q_car)
    got_back = exchange(to_groups(adjoint, n_ctx).astype(BF), "ctx")
    state_grad = from_groups(exchange(scan_states(got_back, passing_all, True), "ctx"), n_ctx)
    d_scores = (scaling * jnp.where(allowed[None], mm("hte,hse->hts", cot, v), 0.0)).astype(BF)
    dq_dec = mm("hts,hsd->htd", d_scores, k_dec) + carried * scaling * mm("hte,hed->htd", cot, state)
    dk_dec = mm("hts,htd->hsd", d_scores, q_dec)
    dk_end = mm("hse,hed->hsd", v, state_grad)
    dv = scaling * mm("hts,hte->hse", scores, cot) + mm("hsd,hed->hse", key_end, state_grad)
    dq = dq_dec * grow
    dk = dk_dec * shrink + dk_end * end_decay
    end_term = dk_end * key_end.astype(F32)
    d_cum = dq_dec * q_dec.astype(F32) - dk_dec * k_dec.astype(F32) - end_term
    d_last = jnp.sum(end_term, axis=1, keepdims=True) + passing[:, None, :] * jnp.sum(
        state.astype(F32) * state_grad.astype(F32), axis=1, keepdims=True
    )
    hi, lo = split(d_cum)
    upper = tri.T
    dg = (
        jnp.einsum("ts,hsd->htd", upper, hi, preferred_element_type=F32)
        + jnp.einsum("ts,hsd->htd", upper, lo, preferred_element_type=F32)
        + d_last
    )
    return (
        unheads(dq).astype(BF),
        unheads(dk).astype(BF),
        unheads(dv).astype(BF),
        unheads(dg).astype(BF),
        grad_residual[None],
        new_weight[None],
        new_moment[None],
    )


def solution(mesh):
    tokens = P("exp", "ctx", None)
    owned = P(("ctx", "exp"), None, None)
    in_specs = (tokens,) * 4 + (P("exp", "ctx"),) + (tokens,) * 4 + (P(),) + (owned,) * 3
    out_specs = (tokens,) * 5 + (owned,) * 2
    return jax.shard_map(local, mesh=mesh, in_specs=in_specs, out_specs=out_specs, check_vma=False)
```

```python
import functools

import jax
import jax.numpy as jnp
from jax import lax
from jax.experimental import pallas as pl
from jax.experimental.pallas import tpu as pltpu
from jax.sharding import PartitionSpec as P

HEADS = 18
HD = 128
TOP = 8
TOK = 128
WIDTH = HEADS * HD
FF = 512
SLOTS = 12
EXPERTS = 128
CAP = EXPERTS * SLOTS
THIRD = WIDTH // 3
SIDE = 4
CTX = 16
GROUP = HEADS * 8
PACK = GROUP + 32
NORM_EPS = 1e-06
LION_RATE = 0.001
BETA_ONE = 0.9
BETA_TWO = 0.99
WEIGHT_DECAY = 0.1
SCALING = HD ** (-0.5)
BF = jnp.bfloat16
F32 = jnp.float32
I32 = jnp.int32
MESH = pl.DeviceIdType.MESH
STRIDE = (32, 8, 2)
AXES = ((0, 1, 2), (1, 2, 0), (2, 0, 1))


def dot(a, b, dims=((1,), (0,))):
    return lax.dot_general(a, b, (dims, ((), ())), preferred_element_type=F32)


NN = ((1,), (0,))
NT = ((1,), (1,))
TN = ((0,), (0,))


def split(x):
    hi = x.astype(BF)
    return hi, (x - hi.astype(F32)).astype(BF)


def iota(shape, dim):
    return lax.broadcasted_iota(I32, shape, dim)


def lower_ones():
    return (iota((TOK, TOK), 0) >= iota((TOK, TOK), 1)).astype(F32).astype(BF)


def segments(starts_ref):
    begin = jnp.broadcast_to(starts_ref[...].astype(F32), (8, TOK)).astype(BF)
    tri = lower_ones()
    row = dot(begin, tri, NT)[0:1]
    col = dot(tri, begin, NT)[:, 0:1]
    return row, col


def head(h):
    return pl.ds(pl.multiple_of(h * HD, HD), HD)


def floor_div(r, by):
    return jnp.floor((r + 0.5) * (1.0 / by))


def row_parts(rows):
    r = iota((rows, 1), 0).astype(F32)
    b = floor_div(r, 48)
    r = r - 48 * b
    a = floor_div(r, SLOTS)
    return b, a, r - SLOTS * a


def mixer(
    og_h, q_h, k_h, v_h, g_h, res_h, router_h, hid_h, w_h, ids_ref, slot_ref, info_ref, starts_ref,
    gres_o, state_o, sgrad_o, grad_o,
    og, q, k, v, g, res, router, hid, w,
    ph1, inf, tab, s2, r2, arr, hp,
    f32buf, fsend, frecv, ssend, srecv, state, asend, arecv, bsend, brecv,
    prow, allowed, carried, mixed, qcar, cot, small, wsend, wmid, wrecv, csend, cmid, crecv, scol, gbuf, cum_s,
    in_sem, out_sem, s1_s, s1_r, i1_s, i1_r, s2_s, s2_r, s3_s, s3_r, f_s, f_r, b_s, b_r,
    w1_s, w1_r, w2_s, w2_r, c1_s, c1_r, c2_s, c2_r, a_s, a_r, e_s, e_r,
):
    ctx, ex = lax.axis_index("ctx"), lax.axis_index("exp")
    here = (lax.div(ctx, SIDE), lax.rem(ctx, SIDE), lax.div(ex, 2), lax.rem(ex, 2))

    def at(coords):
        return (coords[0] * SIDE + coords[1], coords[2] * 2 + coords[3])

    def moved(axis, by, flip=False):
        c = list(here)
        c[axis] = lax.rem(c[axis] + by, SIDE)
        if flip:
            c[3] = 1 - c[3]
        return tuple(c)

    def remote(src, dst, ss, rs, device):
        return pltpu.make_async_remote_copy(
            src_ref=src, dst_ref=dst, send_sem=ss, recv_sem=rs, device_id=device, device_id_type=MESH
        )

    loads = []
    for n, (a, b) in enumerate(
        ((og_h, og), (k_h, k), (v_h, v), (g_h, g), (q_h, q), (res_h, res), (router_h, router), (hid_h, hid), (w_h, w))
    ):
        loads.append(pltpu.make_async_copy(a, b, in_sem.at[n]))
        loads[-1].start()

    barrier = pltpu.get_barrier_semaphore()

    def tell(device):
        pl.semaphore_signal(barrier, inc=1, device_id=device, device_id_type=MESH)

    def tell_ctx(i, _):
        tell((lax.rem(ctx + i, CTX), ex))
        return 0

    def tell_exp(i, _):
        tell((ctx, lax.rem(ex + i, 8)))
        return 0

    lax.fori_loop(1, CTX, tell_ctx, 0)
    lax.fori_loop(1, 8, tell_exp, 0)
    for axis in (0, 1):
        for by in (1, 2, 3):
            tell(at(moved(axis, by, True)))
    pl.semaphore_wait(barrier, CTX - 1 + 7 + 6)

    loads[0].wait()
    sends = []
    locals_ = []
    for by in (1, 3, 2):
        for i in range(3):
            a0 = here[i]
            cp = remote(
                og.at[:, pl.ds(i * THIRD, THIRD)], ph1.at[i, pl.ds(pl.multiple_of(a0 * TOK, TOK), TOK)],
                s1_s.at[i, by], s1_r.at[i, a0], at(moved(i, by)))
            cp.start()
            sends.append(cp)
            cp = remote(info_ref, inf.at[i, a0], i1_s.at[i, by], i1_r.at[i, a0], at(moved(i, by)))
            cp.start()
            sends.append(cp)
    for i in range(3):
        a0 = here[i]
        cp = pltpu.make_async_copy(
            og.at[:, pl.ds(i * THIRD, THIRD)], ph1.at[i, pl.ds(pl.multiple_of(a0 * TOK, TOK), TOK)], s1_r.at[i, a0])
        cp.start()
        cp = pltpu.make_async_copy(info_ref, inf.at[i, a0], i1_r.at[i, a0])
        cp.start()

    for n in (1, 2, 3):
        loads[n].wait()
    seg_row, seg_col = segments(starts_ref)
    last_seg = seg_row[:, TOK - 1:TOK]
    tri = lower_ones()
    allowed[...] = jnp.where(
        (seg_row == seg_col) & (iota((TOK, TOK), 0) >= iota((TOK, TOK), 1)), 1.0, 0.0)
    carried[...] = jnp.broadcast_to(jnp.where(seg_col == 0.0, 1.0, 0.0), (TOK, TOK))
    tail = jnp.broadcast_to(jnp.where(seg_col == last_seg, 1.0, 0.0), (TOK, TOK))
    unbroken = jnp.where(last_seg == 0.0, 1.0, 0.0)
    prow[...] = jnp.zeros_like(prow)

    def own_state(h, _):
        cum = dot(tri, g[:, head(h)])
        cum_s[:, head(h)] = cum
        last = cum[TOK - 1:TOK]
        key_end = (k[:, head(h)].astype(F32) * jnp.exp(last - cum) * tail).astype(BF)
        fresh = dot(v[:, head(h)], key_end, TN)
        f32buf[:, pl.ds(pl.multiple_of(h * 8, 8), 8), :] = fresh.reshape(CTX, 8, HD)
        prow[pl.ds(h, 1), :] = jnp.exp(last) * unbroken
        return 0

    lax.fori_loop(0, HEADS, own_state, 0)
    passing = prow[...].astype(BF)

    def pack(j, _):
        fsend[j, 0:GROUP, :] = f32buf[j].astype(BF)
        fsend[j, GROUP:PACK, :] = passing
        return 0

    lax.fori_loop(0, CTX, pack, 0)

    def ctx_exchange(src, dst, ss, rs):
        def one(i, _):
            t = lax.rem(ctx + i, CTX)
            remote(src.at[t], dst.at[ctx], ss.at[i], rs.at[ctx], (t, ex)).start()
            return 0

        lax.fori_loop(1, CTX, one, 0)
        pltpu.make_async_copy(src.at[ctx], dst.at[ctx], rs.at[ctx]).start()

    def ctx_arrive(src, dst, ss, rs):
        def one(i, _):
            pltpu.make_async_copy(src.at[0], dst.at[i], rs.at[i]).wait()
            return 0

        lax.fori_loop(0, CTX, one, 0)

    def ctx_sent(src, dst, ss, rs):
        def one(i, _):
            pltpu.make_async_copy(src.at[0], dst.at[0], ss.at[i]).wait()
            return 0

        lax.fori_loop(1, CTX, one, 0)

    ctx_exchange(fsend, frecv, f_s, f_r)

    pat_a = floor_div(iota((48, 4 * TOK), 0).astype(F32), SLOTS)
    pat_s = iota((48, 4 * TOK), 0).astype(F32) - SLOTS * pat_a
    pattern = jnp.where(pat_a == floor_div(iota((48, 4 * TOK), 1).astype(F32), TOK), pat_s, -5.0)
    for i, (A, B, C) in enumerate(AXES):
        a0, b0, c0 = here[A], here[B], here[C]
        r = iota((32, TOK), 0).astype(F32)
        bb = floor_div(r, 8)
        cc = floor_div(r - 8 * bb, 2)
        e = bb * STRIDE[B] + cc * STRIDE[C] + (r - 8 * bb - 2 * cc) + (a0 * STRIDE[A]).astype(F32)
        for a in range(SIDE):
            pltpu.make_async_copy(info_ref, inf.at[i, a], i1_r.at[i, a]).wait()
            found = jnp.full((32, TOK), -1.0, F32)
            for j in range(TOP):
                found = jnp.where(inf[i, a, j:j + 1, :] == e, inf[i, a, TOP + j:TOP + j + 1, :], found)
            tab[:, a * TOK:(a + 1) * TOK] = found
            pltpu.make_async_copy(
                og.at[:, pl.ds(0, THIRD)], ph1.at[i, pl.ds(a * TOK, TOK)], s1_r.at[i, a]).wait()

        def select(n, _, i=i, B=B, b0=b0):
            b = lax.rem(b0 + n, SIDE)
            blocks = []
            for m in range(8):
                line = tab[pl.ds(b * 8 + m, 1), :]
                blocks.append(jnp.where(line == pattern, 1.0, 0.0).astype(BF))
            hit = jnp.concatenate(blocks, axis=0)
            s2[i, b] = dot(hit, ph1[i]).astype(BF).reshape(8, 48, THIRD)

            c = list(here)
            c[B] = b
            remote(s2.at[i, b], r2.at[i, b0], s2_s.at[i, n], s2_r.at[i, b0], at(c)).start()
            return 0

        lax.fori_loop(1, SIDE, select, 0)
        blocks = []
        for m in range(8):
            line = tab[pl.ds(b0 * 8 + m, 1), :]
            blocks.append(jnp.where(line == pattern, 1.0, 0.0).astype(BF))
        r2[i, b0] = dot(jnp.concatenate(blocks, axis=0), ph1[i]).astype(BF).reshape(8, 48, THIRD)

    ctx_arrive(fsend, frecv, f_s, f_r)

    def factor(j):
        p = frecv[j, GROUP:PACK, :].astype(F32)
        return jnp.concatenate([jnp.broadcast_to(p[h:h + 1], (8, HD)) for h in range(HEADS)], axis=0)

    def forward(j, acc):
        ssend[j] = acc.astype(BF)
        return factor(j) * acc + frecv[j, 0:GROUP, :].astype(F32)

    lax.fori_loop(0, CTX, forward, jnp.zeros((GROUP, HD), F32))
    ctx_exchange(ssend, srecv, b_s, b_r)

    loads[7].wait()
    pb, pa, ps = row_parts(192)
    for i, (A, B, C) in enumerate(AXES):
        base = (pa * STRIDE[A] + pb * STRIDE[B]) * SLOTS + ps

        def permute(n, _, i=i, C=C, base=base):
            core, c = lax.div(n, SIDE), lax.rem(n, SIDE)
            where = base.astype(I32) + (c * STRIDE[C] + core) * SLOTS
            pick = jnp.where(iota((192, CAP), 1) == where, 1.0, 0.0).astype(BF)
            hp[i, pl.ds(pl.multiple_of(n * 192, 192), 192)] = dot(pick, hid[...]).astype(BF)
            return 0

        lax.fori_loop(0, 8, permute, 0)

    for n in (4, 5, 6):
        loads[n].wait()
    ctx_arrive(ssend, srecv, b_s, b_r)

    def widen(j, _):
        f32buf[j] = srecv[j].astype(F32)
        return 0

    lax.fori_loop(0, CTX, widen, 0)

    def attend(h, _):
        cum = cum_s[:, head(h)]
        q_dec = q[:, head(h)].astype(F32) * jnp.exp(cum)
        k_dec = (k[:, head(h)].astype(F32) * jnp.exp(-cum)).astype(BF)
        scores = (dot(q_dec.astype(BF), k_dec, NT) * allowed[...]).astype(BF)
        q_c = (q_dec * carried[...]).astype(BF)
        qcar[:, head(h)] = q_c
        st = f32buf[:, pl.ds(pl.multiple_of(h * 8, 8), 8), :].reshape(HD, HD).astype(BF)
        state[h] = st
        out = SCALING * (dot(scores, v[:, head(h)]) + dot(q_c, st, NT))
        mixed[:, head(h)] = res[:, head(h)].astype(F32) + out.astype(BF).astype(F32)
        return 0

    lax.fori_loop(0, HEADS, attend, 0)
    state_out = pltpu.make_async_copy(state, state_o, out_sem.at[0])
    state_out.start()

    def square(h, acc):
        m = mixed[:, head(h)]
        return acc + m * m

    sq = lax.fori_loop(0, HEADS, square, jnp.zeros((TOK, HD), F32))
    inverse = lax.rsqrt(jnp.sum(sq, axis=1, keepdims=True) * (1.0 / WIDTH) + NORM_EPS)

    def project(h, acc):
        normed = (mixed[:, head(h)] * inverse).astype(BF)
        return acc + dot(normed, router[head(h), :])

    logits = lax.fori_loop(0, HEADS, project, jnp.zeros((TOK, EXPERTS), F32))
    lanes = iota((TOK, EXPERTS), 1)
    rank = jnp.full((TOK, EXPERTS), -1.0, F32)
    chosen = jnp.zeros((TOK, EXPERTS), F32)
    for j in range(TOP):
        eq = ids_ref[:, j:j + 1] == lanes
        chosen = jnp.where(eq, 1.0, chosen)
        rank = jnp.where(eq, slot_ref[:, j:j + 1].astype(F32), rank)
    gate = chosen * jax.nn.sigmoid(logits)
    total = jnp.sum(gate, axis=1, keepdims=True)
    weights = gate / total
    w_round = weights.astype(BF).astype(F32)
    rows_ = []
    for s in range(SLOTS):
        rows_.append(jnp.sum(jnp.where(rank == float(s), w_round, 0.0), axis=0, keepdims=True))
    w_t = jnp.concatenate(rows_ + [jnp.zeros((4, EXPERTS), F32)], axis=0).astype(BF)
    turn_r, turn_l = iota((EXPERTS, EXPERTS), 0).astype(F32), iota((EXPERTS, EXPERTS), 1).astype(F32)
    turn_e = floor_div(turn_r, CTX)
    turn = jnp.where((turn_r - CTX * turn_e) * 8 + turn_e == turn_l, 1.0, 0.0).astype(BF)
    w_rows = dot(turn, w_t, NT)
    small[...] = jnp.zeros_like(small)
    small[:, 0:16] = w_rows
    wsend[...] = small[...].reshape(8, CTX, EXPERTS)

    def exp_out(src, dst, ss, rs):
        def one(i, _):
            t = lax.rem(ex + i, 8)
            remote(src.at[t], dst.at[:, ex], ss.at[i], rs.at[ex], (ctx, t)).start()
            return 0

        lax.fori_loop(1, 8, one, 0)
        pltpu.make_async_copy(src.at[ex], dst.at[:, ex], rs.at[ex]).start()

    def exp_in(src, dst, ss, rs):
        def one(i, _):
            pltpu.make_async_copy(src.at[0], dst.at[:, i], rs.at[i]).wait()
            return 0

        lax.fori_loop(0, 8, one, 0)

    def exp_sent(src, dst, ss, rs):
        def one(i, _):
            pltpu.make_async_copy(src.at[0], dst.at[:, 0], ss.at[i]).wait()
            return 0

        lax.fori_loop(1, 8, one, 0)

    exp_out(wsend, wmid, w1_s, w1_r)

    for i, (A, B, C) in enumerate(AXES):
        b0, c0 = here[B], here[C]
        slot0 = here[3] * SIDE + c0

        def come(n, _, i=i, b0=b0):
            b = lax.rem(b0 + n, SIDE)
            pltpu.make_async_copy(s2.at[i, 0], r2.at[i, b], s2_r.at[i, b]).wait()
            return 0

        lax.fori_loop(1, SIDE, come, 0)
        for by in (1, 3, 2, 0):
            for flip in (0, 1):
                c = list(here)
                c[C] = lax.rem(c0 + by, SIDE)
                if flip:
                    c[3] = 1 - c[3]
                line = c[C] * 2 + c[3]
                if by == 0 and flip == 0:
                    pltpu.make_async_copy(r2.at[i, :, line], arr.at[i, slot0], s3_r.at[i, slot0]).start()
                else:
                    cp = remote(
                        r2.at[i, :, line], arr.at[i, slot0], s3_s.at[i, by * 2 + flip], s3_r.at[i, slot0], at(c))
                    cp.start()
                    sends.append(cp)

    exp_in(wsend, wmid, w1_s, w1_r)
    ctx_exchange(wmid, wrecv, w2_s, w2_r)

    loads[8].wait()
    small[...] = jnp.zeros_like(small)

    for n in range(8):
        for i, (A, B, C) in enumerate(AXES):
            c0 = here[C]
            step = n // 2
            core = here[3] if n % 2 == 0 else 1 - here[3]
            c = lax.rem(c0 + (0, 1, 3, 2)[step], SIDE)
            piece = core * SIDE + c
            pltpu.make_async_copy(r2.at[i, :, 0], arr.at[i, piece], s3_r.at[i, piece]).wait()
            act = hp[i, pl.ds(pl.multiple_of(piece * 192, 192), 192)]
            part = dot(act, w[:, i * THIRD:(i + 1) * THIRD]).astype(BF).astype(F32)
            part = part * arr[i, piece].reshape(192, THIRD).astype(F32)
            score = jnp.sum(part, axis=1, keepdims=True)
            at_slot = jnp.where(iota((192, EXPERTS), 1) == ps.astype(I32), score, 0.0)
            coord = [None, None, None]
            coord[A], coord[B], coord[C] = pa, pb, c.astype(F32)
            to = (coord[2] * 2 + core.astype(F32)) * CTX + coord[0] * SIDE + coord[1]
            spread = jnp.where(iota((192, EXPERTS), 1) == to.astype(I32), 1.0, 0.0).astype(BF)
            hi, lo = split(at_slot)
            small[...] += dot(spread, hi, TN) + dot(spread, lo, TN)
    csend[...] = small[...].reshape(8, CTX, EXPERTS)
    exp_out(csend, cmid, c1_s, c1_r)
    exp_in(csend, cmid, c1_s, c1_r)
    ctx_exchange(cmid, crecv, c2_s, c2_r)
    ctx_arrive(cmid, crecv, c2_s, c2_r)

    back = jnp.transpose(crecv[...].reshape(EXPERTS, EXPERTS))
    prob = jnp.zeros((TOK, EXPERTS), F32)
    for s in range(SLOTS):
        prob = jnp.where(rank == float(s), back[s:s + 1], prob)
    mix = jnp.sum(weights * prob, axis=1, keepdims=True)
    logit_grad = (chosen * ((prob - mix) / total * gate * (1.0 - gate))).astype(BF)

    def product(h, acc):
        return acc + dot(logit_grad, router[head(h), :], NT) * mixed[:, head(h)]

    mean = jnp.sum(lax.fori_loop(0, HEADS, product, jnp.zeros((TOK, HD), F32)), axis=1, keepdims=True) * (1.0 / WIDTH)
    pull = inverse * inverse * inverse * mean

    def residual(h, _):
        grad = (
            og[:, head(h)].astype(F32)
            + inverse * dot(logit_grad, router[head(h), :], NT)
            - mixed[:, head(h)] * pull
        ).astype(BF)
        cot[:, head(h)] = grad
        adj = SCALING * dot(grad, qcar[:, head(h)], TN)
        f32buf[:, pl.ds(pl.multiple_of(h * 8, 8), 8), :] = adj.reshape(CTX, 8, HD)
        return 0

    lax.fori_loop(0, HEADS, residual, 0)

    def pack_back(j, _):
        asend[j] = f32buf[j].astype(BF)
        return 0

    lax.fori_loop(0, CTX, pack_back, 0)
    ctx_exchange(asend, arecv, a_s, a_r)
    gres_out = pltpu.make_async_copy(cot, gres_o, out_sem.at[1])
    gres_out.start()

    ctx_arrive(wmid, wrecv, w2_s, w2_r)
    w_in = wrecv[...].reshape(EXPERTS, EXPERTS).astype(BF)

    def expert_grad(i):
        A, B, C = AXES[i]

        def column(n, _):
            core, c = lax.div(n, SIDE), lax.rem(n, SIDE)
            src = pa * STRIDE[A] + pb * STRIDE[B]
            src = src.astype(I32) + c * STRIDE[C] + core
            pick = jnp.where(iota((192, EXPERTS), 1) == src, 1.0, 0.0).astype(BF)
            mine = dot(pick, w_in)
            col = jnp.sum(jnp.where(iota((192, EXPERTS), 1) == ps.astype(I32), mine, 0.0), axis=1, keepdims=True)
            scaled = (arr[i, n].reshape(192, THIRD).astype(F32) * col).astype(BF)
            part = dot(hp[i, pl.ds(pl.multiple_of(n * 192, 192), 192)], scaled, TN)

            @pl.when(n == 0)
            def _():
                gbuf[i] = part

            @pl.when(n > 0)
            def _():
                gbuf[i] += part

            return 0

        lax.fori_loop(0, 8, column, 0)
        cp = pltpu.make_async_copy(gbuf.at[i], grad_o.at[:, pl.ds(i * THIRD, THIRD)], out_sem.at[3 + i])
        cp.start()
        return cp

    grads = [expert_grad(0)]
    ctx_arrive(asend, arecv, a_s, a_r)

    def backward(n, acc):
        j = CTX - 1 - n
        bsend[j] = acc.astype(BF)
        return factor(j) * acc + arecv[j].astype(F32)

    lax.fori_loop(0, CTX, backward, jnp.zeros((GROUP, HD), F32))
    ctx_exchange(bsend, brecv, e_s, e_r)
    grads.append(expert_grad(1))
    grads.append(expert_grad(2))
    ctx_arrive(bsend, brecv, e_s, e_r)

    def widen_back(j, _):
        f32buf[j] = brecv[j].astype(F32)
        return 0

    lax.fori_loop(0, CTX, widen_back, 0)
    state_out.wait()

    def gather(h, _):
        state[h] = f32buf[:, pl.ds(pl.multiple_of(h * 8, 8), 8), :].reshape(HD, HD).astype(BF)
        return 0

    lax.fori_loop(0, HEADS, gather, 0)
    sgrad_out = pltpu.make_async_copy(state, sgrad_o, out_sem.at[2])
    sgrad_out.start()

    for cp in sends:
        cp.wait_send()
    for i in range(3):
        for n in (1, 2, 3):
            pltpu.make_async_copy(s2.at[i, 0], r2.at[i, 0], s2_s.at[i, n]).wait()
    ctx_sent(fsend, frecv, f_s, f_r)
    ctx_sent(ssend, srecv, b_s, b_r)
    ctx_sent(asend, arecv, a_s, a_r)
    ctx_sent(bsend, brecv, e_s, e_r)
    exp_sent(wsend, wmid, w1_s, w1_r)
    exp_sent(csend, cmid, c1_s, c1_r)
    ctx_sent(wmid, wrecv, w2_s, w2_r)
    ctx_sent(cmid, crecv, c2_s, c2_r)
    gres_out.wait()
    sgrad_out.wait()
    for cp in grads:
        cp.wait()


def finish(
    q_ref, k_ref, v_ref, g_ref, cot_ref, state_ref, sgrad_ref, starts_ref, w_ref, m_ref, grad_ref,
    dq_o, dk_o, dv_o, dg_o, gres_o, nw_o, nm_o,
):
    seg_row, seg_col = segments(starts_ref)
    last_seg = seg_row[:, TOK - 1:TOK]
    lower = iota((TOK, TOK), 0) >= iota((TOK, TOK), 1)
    tri = lower.astype(F32).astype(BF)
    allowed = jnp.where((seg_row == seg_col) & lower, 1.0, 0.0)
    carried = jnp.where(seg_col == 0.0, 1.0, 0.0)
    tail = jnp.where(seg_col == last_seg, 1.0, 0.0)
    unbroken = jnp.where(last_seg == 0.0, 1.0, 0.0)
    for n in range(state_ref.shape[0]):
        cols = slice(n * HD, (n + 1) * HD)
        v, cot = v_ref[:, cols], cot_ref[:, cols]
        st, sg = state_ref[n], sgrad_ref[n]
        cum = dot(tri, g_ref[:, cols])
        last = cum[TOK - 1:TOK]
        grow, shrink, to_end = jnp.exp(cum), jnp.exp(-cum), jnp.exp(last - cum) * tail
        k = k_ref[:, cols].astype(F32)
        q_dec = (q_ref[:, cols].astype(F32) * grow).astype(BF)
        k_dec = (k * shrink).astype(BF)
        key_end = (k * to_end).astype(BF)
        scores = (SCALING * allowed * dot(q_dec, k_dec, NT)).astype(BF)
        d_scores = (SCALING * allowed * dot(cot, v, NT)).astype(BF)
        dq_dec = dot(d_scores, k_dec) + (SCALING * carried) * dot(cot, st)
        dk_dec = dot(d_scores, q_dec, TN)
        dk_end = dot(v, sg)
        dv_o[:, cols] = (dot(scores, cot, TN) + dot(key_end, sg, NT)).astype(BF)
        dq_o[:, cols] = (dq_dec * grow).astype(BF)
        dk_o[:, cols] = (dk_dec * shrink + dk_end * to_end).astype(BF)
        end_term = dk_end * key_end.astype(F32)
        d_cum = dq_dec * q_dec.astype(F32) - dk_dec * k_dec.astype(F32) - end_term
        d_last = jnp.sum(end_term, axis=0, keepdims=True) + unbroken * jnp.exp(last) * jnp.sum(
            st.astype(F32) * sg.astype(F32), axis=0, keepdims=True)
        hi, lo = split(d_cum)
        dg_o[:, cols] = (dot(tri, hi, TN) + dot(tri, lo, TN) + d_last).astype(BF)
        gres_o[:, cols] = cot
    wf, mf, grad = w_ref[...].astype(F32), m_ref[...].astype(F32), grad_ref[...]
    turn = BETA_ONE * mf + (1.0 - BETA_ONE) * grad
    direction = jnp.where(turn > 0.0, 1.0, jnp.where(turn < 0.0, -1.0, 0.0))
    nw_o[...] = (wf - LION_RATE * (direction + WEIGHT_DECAY * wf)).astype(BF)
    nm_o[...] = (BETA_TWO * mf + (1.0 - BETA_TWO) * grad).astype(BF)


def local(
    queries, key_vectors, values, log_decay, starts, residual_in, out_grad,
    expert_ids, slot_index, router, hidden_saved, w_down, momentum,
):
    any_, vm = pl.BlockSpec(memory_space=pl.ANY), pl.BlockSpec(memory_space=pltpu.VMEM)
    dma = pltpu.SemaphoreType.DMA
    V = pltpu.VMEM
    info = jnp.concatenate([expert_ids[0].T, slot_index[0].T], axis=0).astype(F32)
    scratch = [
        *[V((TOK, WIDTH), BF)] * 6, V((WIDTH, EXPERTS), BF), V((CAP, FF), BF), V((FF, WIDTH), BF),
        V((3, SIDE * TOK, THIRD), BF), V((3, SIDE, 16, TOK), F32), V((32, SIDE * TOK), F32),
        V((3, SIDE, 8, 48, THIRD), BF), V((3, SIDE, 8, 48, THIRD), BF), V((3, 8, SIDE, 48, THIRD), BF),
        V((3, CAP, FF), BF),
        V((CTX, GROUP, HD), F32), V((CTX, PACK, HD), BF), V((CTX, PACK, HD), BF),
        V((CTX, GROUP, HD), BF), V((CTX, GROUP, HD), BF), V((HEADS, HD, HD), BF),
        *[V((CTX, GROUP, HD), BF)] * 4,
        V((32, HD), F32), V((TOK, TOK), F32), V((TOK, TOK), F32), V((TOK, WIDTH), F32),
        V((TOK, WIDTH), BF), V((TOK, WIDTH), BF), V((EXPERTS, EXPERTS), F32),
        V((8, CTX, EXPERTS), F32), V((CTX, 8, EXPERTS), F32), V((CTX, 8, EXPERTS), F32),
        V((8, CTX, EXPERTS), F32), V((CTX, 8, EXPERTS), F32), V((CTX, 8, EXPERTS), F32),
        V((8, 128), F32), V((3, FF, THIRD), F32), V((TOK, WIDTH), F32),
        dma((9,)), dma((6,)),
        dma((3, 4)), dma((3, 4)), dma((3, 4)), dma((3, 4)), dma((3, 4)), dma((3, 4)), dma((3, 8)), dma((3, 8)),
        dma((CTX,)), dma((CTX,)), dma((CTX,)), dma((CTX,)),
        dma((8,)), dma((8,)), dma((CTX,)), dma((CTX,)), dma((8,)), dma((8,)), dma((CTX,)), dma((CTX,)),
        dma((CTX,)), dma((CTX,)), dma((CTX,)), dma((CTX,)),
    ]
    gres, state, sgrad, grad = pl.pallas_call(
        mixer,
        name="dispatch_and_scan",
        out_shape=(
            jax.ShapeDtypeStruct((TOK, WIDTH), BF),
            jax.ShapeDtypeStruct((HEADS, HD, HD), BF),
            jax.ShapeDtypeStruct((HEADS, HD, HD), BF),
            jax.ShapeDtypeStruct((FF, WIDTH), F32),
        ),
        in_specs=[any_] * 9 + [vm] * 4,
        out_specs=(any_,) * 4,
        scratch_shapes=scratch,
        compiler_params=pltpu.CompilerParams(
            collective_id=0, has_side_effects=True, vmem_limit_bytes=62 * 2**20),
    )(
        out_grad[0], queries[0], key_vectors[0], values[0], log_decay[0], residual_in[0], router,
        hidden_saved[0], w_down[0], expert_ids[0], slot_index[0], info, starts,
    )
    per = 2
    tok = pl.BlockSpec((TOK, per * HD), lambda i: (0, i))
    st = pl.BlockSpec((per, HD, HD), lambda i: (i, 0, 0))
    ex = pl.BlockSpec((FF, per * HD), lambda i: (0, i))
    outs = pl.pallas_call(
        finish,
        name="backward_and_step",
        grid=(HEADS // per,),
        out_shape=(jax.ShapeDtypeStruct((TOK, WIDTH), BF),) * 5 + (jax.ShapeDtypeStruct((FF, WIDTH), BF),) * 2,
        in_specs=[tok] * 5 + [st] * 2 + [pl.BlockSpec((1, TOK), lambda i: (0, 0))] + [ex] * 3,
        out_specs=(tok,) * 5 + (ex,) * 2,
        compiler_params=pltpu.CompilerParams(vmem_limit_bytes=40 * 2**20),
    )(
        queries[0], key_vectors[0], values[0], log_decay[0], gres, state, sgrad, starts,
        w_down[0], momentum[0], grad,
    )
    return tuple(x[None] for x in outs)


def solution(mesh):
    tokens = P("exp", "ctx", None)
    owned = P(("ctx", "exp"), None, None)
    in_specs = (tokens,) * 4 + (P("exp", "ctx"),) + (tokens,) * 4 + (P(),) + (owned,) * 3
    out_specs = (tokens,) * 5 + (owned,) * 2
    return jax.shard_map(local, mesh=mesh, in_specs=in_specs, out_specs=out_specs, check_vma=False)
```

```python
import functools

import jax
import jax.numpy as jnp
from jax import lax
from jax.experimental import pallas as pl
from jax.experimental.pallas import tpu as pltpu
from jax.sharding import PartitionSpec as P

HEADS = 18
HD = 128
TOP = 8
TOK = 128
WIDTH = HEADS * HD
FF = 512
SLOTS = 12
EXPERTS = 128
CAP = EXPERTS * SLOTS
THIRD = WIDTH // 3
SIDE = 4
CTX = 16
GROUP = HEADS * 8
PACK = GROUP + 32
NORM_EPS = 1e-06
LION_RATE = 0.001
BETA_ONE = 0.9
BETA_TWO = 0.99
WEIGHT_DECAY = 0.1
SCALING = HD ** (-0.5)
BF = jnp.bfloat16
F32 = jnp.float32
I32 = jnp.int32
UNROLL = 3
PER = 3
MESH = pl.DeviceIdType.MESH
STRIDE = (32, 8, 2)
AXES = ((0, 1, 2), (1, 2, 0), (2, 0, 1))


def dot(a, b, dims=((1,), (0,))):
    return lax.dot_general(a, b, (dims, ((), ())), preferred_element_type=F32)


NN = ((1,), (0,))
NT = ((1,), (1,))
TN = ((0,), (0,))


def split(x):
    hi = x.astype(BF)
    return hi, (x - hi.astype(F32)).astype(BF)


def iota(shape, dim):
    return lax.broadcasted_iota(I32, shape, dim)


def lower_ones():
    return (iota((TOK, TOK), 0) >= iota((TOK, TOK), 1)).astype(F32).astype(BF)


def segments(starts_ref):
    begin = jnp.broadcast_to(starts_ref[...].astype(F32), (8, TOK)).astype(BF)
    tri = lower_ones()
    row = dot(begin, tri, NT)[0:1]
    col = dot(tri, begin, NT)[:, 0:1]
    return row, col


def head(h):
    return pl.ds(pl.multiple_of(h * HD, HD), HD)


def floor_div(r, by):
    return jnp.floor((r + 0.5) * (1.0 / by))


def digits(r, sizes):
    out = []
    for size in reversed(sizes):
        rest = floor_div(r, size)
        out.append(r - size * rest)
        r = rest
    return [r] + out[::-1]


def mixer(
    og_h, q_h, k_h, v_h, g_h, res_h, router_h, hid_h, w_h, ids_ref, slot_ref, starts_ref,
    gres_o, state_o, sgrad_o, grad_o,
    og, q, k, v, g, res, router, hid, w,
    ph1, info, inf, tab, s2, r2, arr, hp,
    f32buf, fsend, frecv, ssend, srecv, state, asend, arecv, bsend, brecv,
    prow, allowed, carried, mixed, qcar, cot, small, wsend, wmid, wrecv, csend, cmid, crecv, gbuf, cum_s,
    in_sem, out_sem, s1_s, s1_r, i1_s, i1_r, s2_s, s2_r, s3_s, s3_r, f_s, f_r, b_s, b_r,
    w1_s, w1_r, w2_s, w2_r, c1_s, c1_r, c2_s, c2_r, a_s, a_r, e_s, e_r,
):
    ctx, ex = lax.axis_index("ctx"), lax.axis_index("exp")
    here = (lax.div(ctx, SIDE), lax.rem(ctx, SIDE), lax.div(ex, 2), lax.rem(ex, 2))

    def at(coords):
        return (coords[0] * SIDE + coords[1], coords[2] * 2 + coords[3])

    def moved(axis, by, flip=False):
        c = list(here)
        c[axis] = lax.rem(c[axis] + by, SIDE)
        if flip:
            c[3] = 1 - c[3]
        return tuple(c)

    def remote(src, dst, ss, rs, device):
        return pltpu.make_async_remote_copy(
            src_ref=src, dst_ref=dst, send_sem=ss, recv_sem=rs, device_id=device, device_id_type=MESH
        )

    loads = []
    for n, (a, b) in enumerate(
        ((og_h, og), (k_h, k), (v_h, v), (g_h, g), (q_h, q), (res_h, res), (router_h, router), (hid_h, hid), (w_h, w))
    ):
        loads.append(pltpu.make_async_copy(a, b, in_sem.at[n]))
        loads[-1].start()

    info[0:TOP] = ids_ref[...].astype(F32)
    info[TOP:2 * TOP] = slot_ref[...].astype(F32)

    barrier = pltpu.get_barrier_semaphore()

    def tell(device):
        pl.semaphore_signal(barrier, inc=1, device_id=device, device_id_type=MESH)

    def tell_ctx(i, _):
        tell((lax.rem(ctx + i, CTX), ex))
        return 0

    def tell_exp(i, _):
        tell((ctx, lax.rem(ex + i, 8)))
        return 0

    lax.fori_loop(1, CTX, tell_ctx, 0)
    lax.fori_loop(1, 8, tell_exp, 0)
    for axis in (0, 1):
        for by in (1, 2, 3):
            tell(at(moved(axis, by, True)))
    pl.semaphore_wait(barrier, CTX - 1 + 7 + 6)

    loads[0].wait()
    sends = []

    def send(src, dst, ss, rs, device):
        cp = remote(src, dst, ss, rs, device)
        cp.start()
        sends.append(cp)

    def rows_of(n, size):
        return pl.ds(pl.multiple_of(n * size, size), size)

    for by in (1, 3, 2):
        for i in range(3):
            send(info, inf.at[i, here[i]], i1_s.at[i, by], i1_r.at[i, here[i]], at(moved(i, by)))
    for by in (1, 3, 2):
        for i in range(3):
            send(og.at[:, pl.ds(i * THIRD, THIRD)], ph1.at[i, rows_of(here[i], TOK)],
                 s1_s.at[i, by], s1_r.at[i, here[i]], at(moved(i, by)))
    for i in range(3):
        pltpu.make_async_copy(
            og.at[:, pl.ds(i * THIRD, THIRD)], ph1.at[i, rows_of(here[i], TOK)], s1_r.at[i, here[i]]).start()
        pltpu.make_async_copy(info, inf.at[i, here[i]], i1_r.at[i, here[i]]).start()

    for n in (1, 2, 3):
        loads[n].wait()
    seg_row, seg_col = segments(starts_ref)
    last_seg = seg_row[:, TOK - 1:TOK]
    tri = lower_ones()
    allowed[...] = jnp.where(
        (seg_row == seg_col) & (iota((TOK, TOK), 0) >= iota((TOK, TOK), 1)), 1.0, 0.0)
    carried[...] = jnp.broadcast_to(jnp.where(seg_col == 0.0, 1.0, 0.0), (TOK, TOK))
    tail = jnp.broadcast_to(jnp.where(seg_col == last_seg, 1.0, 0.0), (TOK, TOK))
    unbroken = jnp.where(last_seg == 0.0, 1.0, 0.0)
    prow[...] = jnp.zeros_like(prow)

    def own_state(h, _):
        cum = dot(tri, g[:, head(h)])
        cum_s[:, head(h)] = cum
        last = cum[TOK - 1:TOK]
        key_end = (k[:, head(h)].astype(F32) * jnp.exp(last - cum) * tail).astype(BF)
        fresh = dot(v[:, head(h)], key_end, TN)
        f32buf[:, rows_of(h, 8), :] = fresh.reshape(CTX, 8, HD)
        prow[pl.ds(h, 1), :] = jnp.exp(last) * unbroken
        return 0

    lax.fori_loop(0, HEADS, own_state, 0, unroll=UNROLL)
    passing = prow[...].astype(BF)

    def pack(j, _):
        fsend[j, 0:GROUP, :] = f32buf[j].astype(BF)
        fsend[j, GROUP:PACK, :] = passing
        return 0

    lax.fori_loop(0, CTX, pack, 0, unroll=4)

    def ctx_exchange(src, dst, ss, rs):
        def one(i, _):
            t = lax.rem(ctx + i, CTX)
            remote(src.at[t], dst.at[ctx], ss.at[i], rs.at[ctx], (t, ex)).start()
            return 0

        lax.fori_loop(1, CTX, one, 0)
        pltpu.make_async_copy(src.at[ctx], dst.at[ctx], rs.at[ctx]).start()

    def ctx_arrive(src, dst, ss, rs):
        def one(i, _):
            pltpu.make_async_copy(src.at[0], dst.at[i], rs.at[i]).wait()
            return 0

        lax.fori_loop(0, CTX, one, 0)

    def ctx_sent(src, dst, ss, rs):
        def one(i, _):
            pltpu.make_async_copy(src.at[0], dst.at[0], ss.at[i]).wait()
            return 0

        lax.fori_loop(1, CTX, one, 0)

    ctx_exchange(fsend, frecv, f_s, f_r)

    pat_a, pat_s = digits(iota((48, SIDE * TOK), 0).astype(F32), (SLOTS,))
    pattern = jnp.where(pat_a == floor_div(iota((48, SIDE * TOK), 1).astype(F32), TOK), pat_s, -5.0)
    bb, cc, kk = digits(iota((32, TOK), 0).astype(F32), (SIDE, 2))
    for i, (A, B, C) in enumerate(AXES):
        e = bb * STRIDE[B] + cc * STRIDE[C] + kk + (here[A] * STRIDE[A]).astype(F32)
        for a in range(SIDE):
            pltpu.make_async_copy(info, inf.at[i, a], i1_r.at[i, a]).wait()
            found = jnp.full((32, TOK), -1.0, F32)
            for j in range(TOP):
                found = jnp.where(inf[i, a, j:j + 1, :] == e, inf[i, a, TOP + j:TOP + j + 1, :], found)
            tab[i, :, a * TOK:(a + 1) * TOK] = found

    def select(i, b):
        blocks = []
        for m in range(8):
            line = tab[i, pl.ds(b * 8 + m, 1), :]
            blocks.append(jnp.where(line == pattern, 1.0, 0.0).astype(BF))
        return dot(jnp.concatenate(blocks, axis=0), ph1[i]).astype(BF)

    for by in (1, 3, 2):
        for i, (A, B, C) in enumerate(AXES):
            if by == 1:
                for a in range(SIDE):
                    pltpu.make_async_copy(
                        og.at[:, pl.ds(0, THIRD)], ph1.at[i, pl.ds(a * TOK, TOK)], s1_r.at[i, a]).wait()
            b = lax.rem(here[B] + by, SIDE)
            s2[i, rows_of(b, 384)] = select(i, b)
            remote(s2.at[i, rows_of(b, 384)], r2.at[i, rows_of(here[B], 384)],
                   s2_s.at[i, by], s2_r.at[i, here[B]], at(moved(B, by))).start()
    for i, (A, B, C) in enumerate(AXES):
        r2[i, rows_of(here[B], 384)] = select(i, here[B])

    def onward(b_by):
        for i, (A, B, C) in enumerate(AXES):
            b = lax.rem(here[B] + b_by, SIDE)
            if b_by:
                pltpu.make_async_copy(
                    s2.at[i, pl.ds(0, 384)], r2.at[i, rows_of(b, 384)], s2_r.at[i, b]).wait()
        for by in (1, 3, 2, 0):
            for flip in (0, 1):
                for i, (A, B, C) in enumerate(AXES):
                    b = lax.rem(here[B] + b_by, SIDE)
                    slot = here[3] * SIDE + here[C]
                    to = moved(C, by, bool(flip))
                    src = r2.at[i, rows_of(b * 8 + to[C] * 2 + to[3], 48)]
                    dst = arr.at[i, rows_of(slot * SIDE + b, 48)]
                    if by == 0 and flip == 0:
                        pltpu.make_async_copy(src, dst, s3_r.at[i, slot]).start()
                    else:
                        send(src, dst, s3_s.at[i, by * 2 + flip, b_by], s3_r.at[i, slot], at(to))

    onward(0)

    ctx_arrive(fsend, frecv, f_s, f_r)

    def factor(j):
        p = frecv[j, GROUP:PACK, :].astype(F32)
        return jnp.concatenate([jnp.broadcast_to(p[h:h + 1], (8, HD)) for h in range(HEADS)], axis=0)

    def forward(j, acc):
        ssend[j] = acc.astype(BF)
        return factor(j) * acc + frecv[j, 0:GROUP, :].astype(F32)

    lax.fori_loop(0, CTX, forward, jnp.zeros((GROUP, HD), F32), unroll=2)
    ctx_exchange(ssend, srecv, b_s, b_r)

    loads[7].wait()
    d = iota((384, 1), 0).astype(F32)
    lanes384 = iota((384, 384), 1)

    def pick_from(where):
        return jnp.where(lanes384 == where.astype(I32), 1.0, 0.0).astype(BF)

    core_, z_, x_, s_ = digits(d, (SIDE, SIDE, SLOTS))
    pick = pick_from(x_ * 96 + z_ * 24 + core_ * 12 + s_)
    for y in range(SIDE):
        block = jnp.concatenate([hid[x * 384 + y * 96:x * 384 + y * 96 + 96, :] for x in range(SIDE)], axis=0)
        got = dot(pick, block).astype(BF)
        for n in range(8):
            hp[0, n * 192 + y * 48:n * 192 + y * 48 + 48] = got[n * 48:n * 48 + 48]
    pick = pick_from(x_ * 96 + z_ * 24 + core_ * 12 + s_)
    for x in range(SIDE):
        got = dot(pick, hid[x * 384:x * 384 + 384, :]).astype(BF)
        for core in range(2):
            n = core * SIDE + x
            hp[1, n * 192:n * 192 + 192] = got[core * 192:core * 192 + 192]
    core_, y_, z_, s_ = digits(d, (SIDE, SIDE, SLOTS))
    pick = pick_from(y_ * 96 + z_ * 24 + core_ * 12 + s_)
    for x in range(SIDE):
        got = dot(pick, hid[x * 384:x * 384 + 384, :]).astype(BF)
        for n in range(8):
            hp[2, n * 192 + x * 48:n * 192 + x * 48 + 48] = got[n * 48:n * 48 + 48]

    onward(1)
    onward(3)

    for n in (4, 5, 6):
        loads[n].wait()
    ctx_arrive(ssend, srecv, b_s, b_r)

    def widen(j, _):
        f32buf[j] = srecv[j].astype(F32)
        return 0

    lax.fori_loop(0, CTX, widen, 0, unroll=4)

    def attend(h, _):
        cum = cum_s[:, head(h)]
        q_dec = q[:, head(h)].astype(F32) * jnp.exp(cum)
        k_dec = (k[:, head(h)].astype(F32) * jnp.exp(-cum)).astype(BF)
        scores = (dot(q_dec.astype(BF), k_dec, NT) * allowed[...]).astype(BF)
        q_c = (q_dec * carried[...]).astype(BF)
        qcar[:, head(h)] = q_c
        st = f32buf[:, rows_of(h, 8), :].reshape(HD, HD).astype(BF)
        state[h] = st
        out = SCALING * (dot(scores, v[:, head(h)]) + dot(q_c, st, NT))
        mixed[:, head(h)] = res[:, head(h)].astype(F32) + out.astype(BF).astype(F32)
        return 0

    lax.fori_loop(0, HEADS, attend, 0, unroll=UNROLL)
    state_out = pltpu.make_async_copy(state, state_o, out_sem.at[0])
    state_out.start()

    def third(i):
        return slice(i * THIRD, (i + 1) * THIRD)

    def lane_sum(x):
        acc = x[:, 0:HD]
        for n in range(1, x.shape[1] // HD):
            acc = acc + x[:, n * HD:(n + 1) * HD]
        return jnp.sum(acc, axis=1, keepdims=True)

    sq = sum(lane_sum(mixed[:, third(i)] * mixed[:, third(i)]) for i in range(3))
    inverse = lax.rsqrt(sq * (1.0 / WIDTH) + NORM_EPS)
    logits = sum(dot((mixed[:, third(i)] * inverse).astype(BF), router[third(i), :]) for i in range(3))
    rank_t = jnp.full((EXPERTS, TOK), -1.0, F32)
    for j in range(TOP):
        eq = info[j:j + 1, :] == iota((EXPERTS, TOK), 0).astype(F32)
        rank_t = jnp.where(eq, info[TOP + j:TOP + j + 1, :], rank_t)
    rank = jnp.transpose(rank_t)
    chosen = jnp.where(rank >= 0.0, 1.0, 0.0)
    gate = chosen * jax.nn.sigmoid(logits)
    total = jnp.sum(gate, axis=1, keepdims=True)
    weights = gate / total
    w_round = weights.astype(BF).astype(F32)
    rows_ = []
    for s in range(SLOTS):
        rows_.append(jnp.sum(jnp.where(rank == float(s), w_round, 0.0), axis=0, keepdims=True))
    w_t = jnp.concatenate(rows_ + [jnp.zeros((4, EXPERTS), F32)], axis=0).astype(BF)
    turn_e, turn_c = digits(iota((EXPERTS, EXPERTS), 0).astype(F32), (CTX,))
    turn = jnp.where(turn_c * 8 + turn_e == iota((EXPERTS, EXPERTS), 1).astype(F32), 1.0, 0.0).astype(BF)
    small[...] = jnp.zeros_like(small)
    small[:, 0:16] = dot(turn, w_t, NT)
    wsend[...] = small[...].reshape(8, CTX, EXPERTS)

    def exp_out(src, dst, ss, rs):
        def one(i, _):
            t = lax.rem(ex + i, 8)
            remote(src.at[t], dst.at[:, ex], ss.at[i], rs.at[ex], (ctx, t)).start()
            return 0

        lax.fori_loop(1, 8, one, 0)
        pltpu.make_async_copy(src.at[ex], dst.at[:, ex], rs.at[ex]).start()

    def exp_in(src, dst, ss, rs):
        def one(i, _):
            pltpu.make_async_copy(src.at[0], dst.at[:, i], rs.at[i]).wait()
            return 0

        lax.fori_loop(0, 8, one, 0)

    def exp_sent(src, dst, ss, rs):
        def one(i, _):
            pltpu.make_async_copy(src.at[0], dst.at[:, 0], ss.at[i]).wait()
            return 0

        lax.fori_loop(1, 8, one, 0)

    exp_out(wsend, wmid, w1_s, w1_r)
    onward(2)

    for i in range(3):
        for by in (1, 2, 3):
            pltpu.make_async_copy(s2.at[i, pl.ds(0, 384)], r2.at[i, pl.ds(0, 384)], s2_s.at[i, by]).wait()
    loads[8].wait()
    for i in range(3):
        def produce(n, _, i=i):
            s2[i, rows_of(n, 384)] = dot(hp[i, rows_of(n, 384)], w[:, third(i)]).astype(BF)
            return 0

        lax.fori_loop(0, SIDE, produce, 0)
    exp_in(wsend, wmid, w1_s, w1_r)
    ctx_exchange(wmid, wrecv, w2_s, w2_r)

    pb, pa, ps = digits(iota((192, 1), 0).astype(F32), (SIDE, SLOTS))
    lanes192 = iota((192, EXPERTS), 1)
    own_slot = lanes192 == ps.astype(I32)
    small[...] = jnp.zeros_like(small)
    for n in range(8):
        for i, (A, B, C) in enumerate(AXES):
            core = here[3] if n % 2 == 0 else 1 - here[3]
            c = lax.rem(here[C] + (0, 1, 3, 2)[n // 2], SIDE)
            piece = core * SIDE + c
            rows = rows_of(piece, 192)
            pltpu.make_async_copy(s2.at[i, pl.ds(0, 192)], arr.at[i, rows], s3_r.at[i, piece]).wait()
            score = lane_sum(s2[i, rows].astype(F32) * arr[i, rows].astype(F32))
            at_slot = jnp.where(own_slot, score, 0.0)
            coord = [None, None, None]
            coord[A], coord[B], coord[C] = pa, pb, c.astype(F32)
            to = (coord[2] * 2 + core.astype(F32)) * CTX + coord[0] * SIDE + coord[1]
            spread = jnp.where(lanes192 == to.astype(I32), 1.0, 0.0).astype(BF)
            hi, lo = split(at_slot)
            small[...] += dot(spread, hi, TN) + dot(spread, lo, TN)
    csend[...] = small[...].reshape(8, CTX, EXPERTS)
    exp_out(csend, cmid, c1_s, c1_r)

    ctx_arrive(wmid, wrecv, w2_s, w2_r)
    w_in = wrecv[...].reshape(EXPERTS, EXPERTS).astype(BF)

    def expert_grad(i):
        A, B, C = AXES[i]

        def part(n):
            rows = 2 * 192
            d2, b2, a2, s2_ = digits(iota((rows, 1), 0).astype(F32), (SIDE, SIDE, SLOTS))
            core = lax.div(n, 2)
            c2 = (lax.rem(n, 2) * 2).astype(F32) + d2
            src = a2 * STRIDE[A] + b2 * STRIDE[B] + c2 * STRIDE[C] + core.astype(F32)
            lanes_ = iota((rows, EXPERTS), 1)
            pick = jnp.where(lanes_ == src.astype(I32), 1.0, 0.0).astype(BF)
            col = jnp.sum(jnp.where(lanes_ == s2_.astype(I32), dot(pick, w_in), 0.0), axis=1, keepdims=True)
            scaled = (arr[i, rows_of(n, 384)].astype(F32) * col).astype(BF)
            return dot(hp[i, rows_of(n, 384)], scaled, TN)

        gbuf[i] = part(jnp.int32(0))

        def more(n, _):
            gbuf[i] += part(n)
            return 0

        lax.fori_loop(1, SIDE, more, 0)
        cp = pltpu.make_async_copy(gbuf.at[i], grad_o.at[:, pl.ds(i * THIRD, THIRD)], out_sem.at[3 + i])
        cp.start()
        return cp

    exp_in(csend, cmid, c1_s, c1_r)
    ctx_exchange(cmid, crecv, c2_s, c2_r)
    grads = [expert_grad(0)]
    ctx_arrive(cmid, crecv, c2_s, c2_r)

    back = jnp.transpose(crecv[...].reshape(EXPERTS, EXPERTS))
    prob = jnp.zeros((TOK, EXPERTS), F32)
    for s in range(SLOTS):
        prob = jnp.where(rank == float(s), back[s:s + 1], prob)
    mix = jnp.sum(weights * prob, axis=1, keepdims=True)
    logit_grad = (chosen * ((prob - mix) / total * gate * (1.0 - gate))).astype(BF)
    mean = 0.0
    for i in range(3):
        ng = dot(logit_grad, router[third(i), :], NT)
        cum_s[:, third(i)] = ng
        mean = mean + lane_sum(ng * mixed[:, third(i)])
    pull = inverse * inverse * inverse * (mean * (1.0 / WIDTH))

    def residual(h, _):
        grad = (
            og[:, head(h)].astype(F32) + inverse * cum_s[:, head(h)] - mixed[:, head(h)] * pull
        ).astype(BF)
        cot[:, head(h)] = grad
        adj = SCALING * dot(grad, qcar[:, head(h)], TN)
        f32buf[:, rows_of(h, 8), :] = adj.reshape(CTX, 8, HD)
        return 0

    lax.fori_loop(0, HEADS, residual, 0, unroll=UNROLL)

    def pack_back(j, _):
        asend[j] = f32buf[j].astype(BF)
        return 0

    lax.fori_loop(0, CTX, pack_back, 0, unroll=4)
    ctx_exchange(asend, arecv, a_s, a_r)
    gres_out = pltpu.make_async_copy(cot, gres_o, out_sem.at[1])
    gres_out.start()
    grads.append(expert_grad(1))
    ctx_arrive(asend, arecv, a_s, a_r)

    def backward(n, acc):
        j = CTX - 1 - n
        bsend[j] = acc.astype(BF)
        return factor(j) * acc + arecv[j].astype(F32)

    lax.fori_loop(0, CTX, backward, jnp.zeros((GROUP, HD), F32), unroll=2)
    ctx_exchange(bsend, brecv, e_s, e_r)
    grads.append(expert_grad(2))
    ctx_arrive(bsend, brecv, e_s, e_r)

    def widen_back(j, _):
        f32buf[j] = brecv[j].astype(F32)
        return 0

    lax.fori_loop(0, CTX, widen_back, 0, unroll=4)
    state_out.wait()

    def gather(h, _):
        state[h] = f32buf[:, rows_of(h, 8), :].reshape(HD, HD).astype(BF)
        return 0

    lax.fori_loop(0, HEADS, gather, 0, unroll=UNROLL)
    sgrad_out = pltpu.make_async_copy(state, sgrad_o, out_sem.at[2])
    sgrad_out.start()

    for cp in sends:
        cp.wait_send()
    ctx_sent(fsend, frecv, f_s, f_r)
    ctx_sent(ssend, srecv, b_s, b_r)
    ctx_sent(asend, arecv, a_s, a_r)
    ctx_sent(bsend, brecv, e_s, e_r)
    exp_sent(wsend, wmid, w1_s, w1_r)
    exp_sent(csend, cmid, c1_s, c1_r)
    ctx_sent(wmid, wrecv, w2_s, w2_r)
    ctx_sent(cmid, crecv, c2_s, c2_r)
    gres_out.wait()
    sgrad_out.wait()
    for cp in grads:
        cp.wait()


def finish(
    q_ref, k_ref, v_ref, g_ref, cot_ref, state_ref, sgrad_ref, starts_ref, w_ref, m_ref, grad_ref,
    dq_o, dk_o, dv_o, dg_o, gres_o, nw_o, nm_o,
):
    seg_row, seg_col = segments(starts_ref)
    last_seg = seg_row[:, TOK - 1:TOK]
    lower = iota((TOK, TOK), 0) >= iota((TOK, TOK), 1)
    tri = lower.astype(F32).astype(BF)
    allowed = jnp.where((seg_row == seg_col) & lower, 1.0, 0.0)
    carried = jnp.where(seg_col == 0.0, 1.0, 0.0)
    tail = jnp.where(seg_col == last_seg, 1.0, 0.0)
    unbroken = jnp.where(last_seg == 0.0, 1.0, 0.0)
    for n in range(state_ref.shape[0]):
        cols = slice(n * HD, (n + 1) * HD)
        v, cot = v_ref[:, cols], cot_ref[:, cols]
        st, sg = state_ref[n], sgrad_ref[n]
        cum = dot(tri, g_ref[:, cols])
        last = cum[TOK - 1:TOK]
        grow, shrink, to_end = jnp.exp(cum), jnp.exp(-cum), jnp.exp(last - cum) * tail
        k = k_ref[:, cols].astype(F32)
        q_dec = (q_ref[:, cols].astype(F32) * grow).astype(BF)
        k_dec = (k * shrink).astype(BF)
        key_end = (k * to_end).astype(BF)
        scores = (SCALING * allowed * dot(q_dec, k_dec, NT)).astype(BF)
        d_scores = (SCALING * allowed * dot(cot, v, NT)).astype(BF)
        dq_dec = dot(d_scores, k_dec) + (SCALING * carried) * dot(cot, st)
        dk_dec = dot(d_scores, q_dec, TN)
        dk_end = dot(v, sg)
        dv_o[:, cols] = (dot(scores, cot, TN) + dot(key_end, sg, NT)).astype(BF)
        dq_o[:, cols] = (dq_dec * grow).astype(BF)
        dk_o[:, cols] = (dk_dec * shrink + dk_end * to_end).astype(BF)
        end_term = dk_end * key_end.astype(F32)
        d_cum = dq_dec * q_dec.astype(F32) - dk_dec * k_dec.astype(F32) - end_term
        d_last = jnp.sum(end_term, axis=0, keepdims=True) + unbroken * jnp.exp(last) * jnp.sum(
            st.astype(F32) * sg.astype(F32), axis=0, keepdims=True)
        hi, lo = split(d_cum)
        dg_o[:, cols] = (dot(tri, hi, TN) + dot(tri, lo, TN) + d_last).astype(BF)
        gres_o[:, cols] = cot
    wf, mf, grad = w_ref[...].astype(F32), m_ref[...].astype(F32), grad_ref[...]
    turn = BETA_ONE * mf + (1.0 - BETA_ONE) * grad
    direction = jnp.where(turn > 0.0, 1.0, jnp.where(turn < 0.0, -1.0, 0.0))
    nw_o[...] = (wf - LION_RATE * (direction + WEIGHT_DECAY * wf)).astype(BF)
    nm_o[...] = (BETA_TWO * mf + (1.0 - BETA_TWO) * grad).astype(BF)


def local(
    queries, key_vectors, values, log_decay, starts, residual_in, out_grad,
    expert_ids, slot_index, router, hidden_saved, w_down, momentum,
):
    any_, vm = pl.BlockSpec(memory_space=pl.ANY), pl.BlockSpec(memory_space=pltpu.VMEM)
    dma = pltpu.SemaphoreType.DMA
    V = pltpu.VMEM
    scratch = [
        *[V((TOK, WIDTH), BF)] * 6, V((WIDTH, EXPERTS), BF), V((CAP, FF), BF), V((FF, WIDTH), BF),
        V((3, SIDE * TOK, THIRD), BF), V((16, TOK), F32), V((3, SIDE, 16, TOK), F32), V((3, 32, SIDE * TOK), F32),
        *[V((3, CAP, THIRD), BF)] * 3,
        V((3, CAP, FF), BF),
        V((CTX, GROUP, HD), F32), V((CTX, PACK, HD), BF), V((CTX, PACK, HD), BF),
        V((CTX, GROUP, HD), BF), V((CTX, GROUP, HD), BF), V((HEADS, HD, HD), BF),
        *[V((CTX, GROUP, HD), BF)] * 4,
        V((32, HD), F32), V((TOK, TOK), F32), V((TOK, TOK), F32), V((TOK, WIDTH), F32),
        V((TOK, WIDTH), BF), V((TOK, WIDTH), BF), V((EXPERTS, EXPERTS), F32),
        V((8, CTX, EXPERTS), F32), V((CTX, 8, EXPERTS), F32), V((CTX, 8, EXPERTS), F32),
        V((8, CTX, EXPERTS), F32), V((CTX, 8, EXPERTS), F32), V((CTX, 8, EXPERTS), F32),
        V((3, FF, THIRD), F32), V((TOK, WIDTH), F32),
        dma((9,)), dma((6,)),
        dma((3, 4)), dma((3, 4)), dma((3, 4)), dma((3, 4)), dma((3, 4)), dma((3, 4)), dma((3, 8, 4)), dma((3, 8)),
        dma((CTX,)), dma((CTX,)), dma((CTX,)), dma((CTX,)),
        dma((8,)), dma((8,)), dma((CTX,)), dma((CTX,)), dma((8,)), dma((8,)), dma((CTX,)), dma((CTX,)),
        dma((CTX,)), dma((CTX,)), dma((CTX,)), dma((CTX,)),
    ]
    gres, state, sgrad, grad = pl.pallas_call(
        mixer,
        name="dispatch_and_scan",
        out_shape=(
            jax.ShapeDtypeStruct((TOK, WIDTH), BF),
            jax.ShapeDtypeStruct((HEADS, HD, HD), BF),
            jax.ShapeDtypeStruct((HEADS, HD, HD), BF),
            jax.ShapeDtypeStruct((FF, WIDTH), F32),
        ),
        in_specs=[any_] * 9 + [vm] * 3,
        out_specs=(any_,) * 4,
        scratch_shapes=scratch,
        compiler_params=pltpu.CompilerParams(
            collective_id=0, has_side_effects=True, vmem_limit_bytes=62 * 2**20),
    )(
        out_grad[0], queries[0], key_vectors[0], values[0], log_decay[0], residual_in[0], router,
        hidden_saved[0], w_down[0], expert_ids[0].T, slot_index[0].T, starts,
    )
    per = PER
    tok = pl.BlockSpec((TOK, per * HD), lambda i: (0, i))
    st = pl.BlockSpec((per, HD, HD), lambda i: (i, 0, 0))
    ex = pl.BlockSpec((FF, per * HD), lambda i: (0, i))
    outs = pl.pallas_call(
        finish,
        name="backward_and_step",
        grid=(HEADS // per,),
        out_shape=(jax.ShapeDtypeStruct((TOK, WIDTH), BF),) * 5 + (jax.ShapeDtypeStruct((FF, WIDTH), BF),) * 2,
        in_specs=[tok] * 5 + [st] * 2 + [pl.BlockSpec((1, TOK), lambda i: (0, 0))] + [ex] * 3,
        out_specs=(tok,) * 5 + (ex,) * 2,
        compiler_params=pltpu.CompilerParams(vmem_limit_bytes=62 * 2**20),
    )(
        queries[0], key_vectors[0], values[0], log_decay[0], gres, state, sgrad, starts,
        w_down[0], momentum[0], grad,
    )
    return tuple(x[None] for x in outs)


def solution(mesh):
    tokens = P("exp", "ctx", None)
    owned = P(("ctx", "exp"), None, None)
    in_specs = (tokens,) * 4 + (P("exp", "ctx"),) + (tokens,) * 4 + (P(),) + (owned,) * 3
    out_specs = (tokens,) * 5 + (owned,) * 2
    return jax.shard_map(local, mesh=mesh, in_specs=in_specs, out_specs=out_specs, check_vma=False)
```

```python
import functools

import jax
import jax.numpy as jnp
from jax import lax
from jax.experimental import pallas as pl
from jax.experimental.pallas import tpu as pltpu
from jax.sharding import PartitionSpec as P

HEADS = 18
HD = 128
TOP = 8
TOK = 128
WIDTH = HEADS * HD
FF = 512
SLOTS = 12
EXPERTS = 128
CAP = EXPERTS * SLOTS
THIRD = WIDTH // 3
SIDE = 4
CTX = 16
GROUP = HEADS * 8
PACK = GROUP + 32
NORM_EPS = 1e-06
LION_RATE = 0.001
BETA_ONE = 0.9
BETA_TWO = 0.99
WEIGHT_DECAY = 0.1
SCALING = HD ** (-0.5)
BF = jnp.bfloat16
F32 = jnp.float32
I32 = jnp.int32
UNROLL = 3
PER = 3
LION_STEPS = 4
MESH = pl.DeviceIdType.MESH
STRIDE = (32, 8, 2)
AXES = ((0, 1, 2), (1, 2, 0), (2, 0, 1))


def dot(a, b, dims=((1,), (0,))):
    return lax.dot_general(a, b, (dims, ((), ())), preferred_element_type=F32)


NN = ((1,), (0,))
NT = ((1,), (1,))
TN = ((0,), (0,))


def split(x):
    hi = x.astype(BF)
    return hi, (x - hi.astype(F32)).astype(BF)


def iota(shape, dim):
    return lax.broadcasted_iota(I32, shape, dim)


def lower_ones():
    return (iota((TOK, TOK), 0) >= iota((TOK, TOK), 1)).astype(F32).astype(BF)


def segments(starts_ref):
    begin = jnp.broadcast_to(starts_ref[...].astype(F32), (8, TOK)).astype(BF)
    tri = lower_ones()
    row = dot(begin, tri, NT)[0:1]
    col = dot(tri, begin, NT)[:, 0:1]
    return row, col


def head(h):
    return pl.ds(pl.multiple_of(h * HD, HD), HD)


def floor_div(r, by):
    return jnp.floor((r + 0.5) * (1.0 / by))


def digits(r, sizes):
    out = []
    for size in reversed(sizes):
        rest = floor_div(r, size)
        out.append(r - size * rest)
        r = rest
    return [r] + out[::-1]


def mixer(
    og_h, q_h, k_h, v_h, g_h, res_h, router_h, hid_h, w_h, ids_h, slot_h, starts_h,
    gres_o, state_o, sgrad_o, grad_o,
    ids_ref, slot_ref, starts_ref, og, q, k, v, g, res, router, hid, w,
    ph1, info, inf, tab, s2, r2, arr, hp,
    f32buf, fsend, frecv, ssend, srecv, state, asend, arecv, bsend, brecv,
    prow, allowed, carried, mixed, qcar, cot, small, wsend, wmid, wrecv, csend, cmid, crecv, gbuf, cum_s,
    in_sem, out_sem, s1_s, s1_r, i1_s, i1_r, s2_s, s2_r, s3_s, s3_r, f_s, f_r, b_s, b_r,
    w1_s, w1_r, w2_s, w2_r, c1_s, c1_r, c2_s, c2_r, a_s, a_r, e_s, e_r,
):
    ctx, ex = lax.axis_index("ctx"), lax.axis_index("exp")
    here = (lax.div(ctx, SIDE), lax.rem(ctx, SIDE), lax.div(ex, 2), lax.rem(ex, 2))

    def at(coords):
        return (coords[0] * SIDE + coords[1], coords[2] * 2 + coords[3])

    def moved(axis, by, flip=False):
        c = list(here)
        c[axis] = lax.rem(c[axis] + by, SIDE)
        if flip:
            c[3] = 1 - c[3]
        return tuple(c)

    def remote(src, dst, ss, rs, device):
        return pltpu.make_async_remote_copy(
            src_ref=src, dst_ref=dst, send_sem=ss, recv_sem=rs, device_id=device, device_id_type=MESH
        )

    barrier = pltpu.get_barrier_semaphore()

    def tell(device):
        pl.semaphore_signal(barrier, inc=1, device_id=device, device_id_type=MESH)

    def tell_ctx(i, _):
        tell((lax.rem(ctx + i, CTX), ex))
        return 0

    def tell_exp(i, _):
        tell((ctx, lax.rem(ex + i, 8)))
        return 0

    lax.fori_loop(1, CTX, tell_ctx, 0)
    lax.fori_loop(1, 8, tell_exp, 0)
    for axis in (0, 1):
        for by in (1, 2, 3):
            tell(at(moved(axis, by, True)))
    loads = []
    for n, (a, b) in enumerate(
        ((ids_h, ids_ref), (slot_h, slot_ref), (starts_h, starts_ref), (og_h, og), (k_h, k), (v_h, v), (g_h, g), (q_h, q), (res_h, res), (router_h, router), (hid_h, hid), (w_h, w))
    ):
        loads.append(pltpu.make_async_copy(a, b, in_sem.at[n]))
        loads[-1].start()

    small_loads, loads = loads[:3], loads[3:]
    for cp in small_loads:
        cp.wait()
    info[0:TOP] = ids_ref[...].astype(F32)
    info[TOP:2 * TOP] = slot_ref[...].astype(F32)

    pl.semaphore_wait(barrier, CTX - 1 + 7 + 6)

    loads[0].wait()
    sends = []

    def send(src, dst, ss, rs, device):
        cp = remote(src, dst, ss, rs, device)
        cp.start()
        sends.append(cp)

    def rows_of(n, size):
        return pl.ds(pl.multiple_of(n * size, size), size)

    for by in (1, 3, 2):
        for i in range(3):
            send(info, inf.at[i, here[i]], i1_s.at[i, by], i1_r.at[i, here[i]], at(moved(i, by)))
    for by in (1, 3, 2):
        for i in range(3):
            send(og.at[:, pl.ds(i * THIRD, THIRD)], ph1.at[i, rows_of(here[i], TOK)],
                 s1_s.at[i, by], s1_r.at[i, here[i]], at(moved(i, by)))
    for i in range(3):
        pltpu.make_async_copy(
            og.at[:, pl.ds(i * THIRD, THIRD)], ph1.at[i, rows_of(here[i], TOK)], s1_r.at[i, here[i]]).start()
        pltpu.make_async_copy(info, inf.at[i, here[i]], i1_r.at[i, here[i]]).start()

    for n in (1, 2, 3):
        loads[n].wait()
    seg_row, seg_col = segments(starts_ref)
    last_seg = seg_row[:, TOK - 1:TOK]
    tri = lower_ones()
    allowed[...] = jnp.where(
        (seg_row == seg_col) & (iota((TOK, TOK), 0) >= iota((TOK, TOK), 1)), 1.0, 0.0)
    carried[...] = jnp.broadcast_to(jnp.where(seg_col == 0.0, 1.0, 0.0), (TOK, TOK))
    tail = jnp.broadcast_to(jnp.where(seg_col == last_seg, 1.0, 0.0), (TOK, TOK))
    unbroken = jnp.where(last_seg == 0.0, 1.0, 0.0)
    prow[...] = jnp.zeros_like(prow)

    def own_state(h, _):
        cum = dot(tri, g[:, head(h)])
        cum_s[:, head(h)] = cum
        last = cum[TOK - 1:TOK]
        key_end = (k[:, head(h)].astype(F32) * jnp.exp(last - cum) * tail).astype(BF)
        fresh = dot(v[:, head(h)], key_end, TN)
        f32buf[:, rows_of(h, 8), :] = fresh.reshape(CTX, 8, HD)
        prow[pl.ds(h, 1), :] = jnp.exp(last) * unbroken
        return 0

    lax.fori_loop(0, HEADS, own_state, 0, unroll=UNROLL)
    passing = prow[...].astype(BF)

    def pack(j, _):
        fsend[j, 0:GROUP, :] = f32buf[j].astype(BF)
        fsend[j, GROUP:PACK, :] = passing
        return 0

    lax.fori_loop(0, CTX, pack, 0, unroll=4)

    def ctx_exchange(src, dst, ss, rs):
        def one(i, _):
            i7 = lax.rem(i * 7, CTX)
            t = lax.rem(here[0] + lax.div(i7, SIDE), SIDE) * SIDE + lax.rem(here[1] + lax.rem(i7, SIDE), SIDE)
            remote(src.at[t], dst.at[ctx], ss.at[i], rs.at[ctx], (t, ex)).start()
            return 0

        lax.fori_loop(1, CTX, one, 0)
        pltpu.make_async_copy(src.at[ctx], dst.at[ctx], rs.at[ctx]).start()

    def ctx_arrive(src, dst, ss, rs):
        def one(i, _):
            pltpu.make_async_copy(src.at[0], dst.at[i], rs.at[i]).wait()
            return 0

        lax.fori_loop(0, CTX, one, 0)

    def ctx_sent(src, dst, ss, rs):
        def one(i, _):
            pltpu.make_async_copy(src.at[0], dst.at[0], ss.at[i]).wait()
            return 0

        lax.fori_loop(1, CTX, one, 0)

    ctx_exchange(fsend, frecv, f_s, f_r)

    pat_a, pat_s = digits(iota((48, SIDE * TOK), 0).astype(F32), (SLOTS,))
    pattern = jnp.where(pat_a == floor_div(iota((48, SIDE * TOK), 1).astype(F32), TOK), pat_s, -5.0)
    bb, cc, kk = digits(iota((32, TOK), 0).astype(F32), (SIDE, 2))
    for i, (A, B, C) in enumerate(AXES):
        e = bb * STRIDE[B] + cc * STRIDE[C] + kk + (here[A] * STRIDE[A]).astype(F32)
        for a in range(SIDE):
            pltpu.make_async_copy(info, inf.at[i, a], i1_r.at[i, a]).wait()
            found = jnp.full((32, TOK), -1.0, F32)
            for j in range(TOP):
                found = jnp.where(inf[i, a, j:j + 1, :] == e, inf[i, a, TOP + j:TOP + j + 1, :], found)
            tab[i, :, a * TOK:(a + 1) * TOK] = found

    def select(i, b):
        blocks = []
        for m in range(8):
            line = tab[i, pl.ds(b * 8 + m, 1), :]
            blocks.append(jnp.where(line == pattern, 1.0, 0.0).astype(BF))
        return dot(jnp.concatenate(blocks, axis=0), ph1[i]).astype(BF)

    for by in (1, 3, 2):
        for i, (A, B, C) in enumerate(AXES):
            if by == 1:
                for a in range(SIDE):
                    pltpu.make_async_copy(
                        og.at[:, pl.ds(0, THIRD)], ph1.at[i, pl.ds(a * TOK, TOK)], s1_r.at[i, a]).wait()
            b = lax.rem(here[B] + by, SIDE)
            s2[i, rows_of(b, 384)] = select(i, b)
            remote(s2.at[i, rows_of(b, 384)], r2.at[i, rows_of(here[B], 384)],
                   s2_s.at[i, by], s2_r.at[i, here[B]], at(moved(B, by))).start()
    for i, (A, B, C) in enumerate(AXES):
        r2[i, rows_of(here[B], 384)] = select(i, here[B])

    def onward(b_by):
        for i, (A, B, C) in enumerate(AXES):
            b = lax.rem(here[B] + b_by, SIDE)
            if b_by:
                pltpu.make_async_copy(
                    s2.at[i, pl.ds(0, 384)], r2.at[i, rows_of(b, 384)], s2_r.at[i, b]).wait()
        for by in (1, 3, 2, 0):
            for flip in (0, 1):
                for i, (A, B, C) in enumerate(AXES):
                    b = lax.rem(here[B] + b_by, SIDE)
                    slot = here[3] * SIDE + here[C]
                    to = moved(C, by, bool(flip))
                    src = r2.at[i, rows_of(b * 8 + to[C] * 2 + to[3], 48)]
                    dst = arr.at[i, rows_of(b * 8 + slot, 48)]
                    if by == 0 and flip == 0:
                        pltpu.make_async_copy(src, dst, s3_r.at[i, b]).start()
                    else:
                        send(src, dst, s3_s.at[i, by * 2 + flip, b_by], s3_r.at[i, b], at(to))

    onward(0)

    ctx_arrive(fsend, frecv, f_s, f_r)

    def factor(j):
        p = frecv[j, GROUP:PACK, :].astype(F32)
        return jnp.concatenate([jnp.broadcast_to(p[h:h + 1], (8, HD)) for h in range(HEADS)], axis=0)

    def forward(j, acc):
        ssend[j] = acc.astype(BF)
        return factor(j) * acc + frecv[j, 0:GROUP, :].astype(F32)

    lax.fori_loop(0, CTX, forward, jnp.zeros((GROUP, HD), F32), unroll=2)
    ctx_exchange(ssend, srecv, b_s, b_r)

    loads[7].wait()
    d = iota((384, 1), 0).astype(F32)
    lanes384 = iota((384, 384), 1)

    def pick_from(where):
        return jnp.where(lanes384 == where.astype(I32), 1.0, 0.0).astype(BF)

    core_, z_, x_, s_ = digits(d, (SIDE, SIDE, SLOTS))
    pick = pick_from(x_ * 96 + z_ * 24 + core_ * 12 + s_)
    for y in range(SIDE):
        block = jnp.concatenate([hid[x * 384 + y * 96:x * 384 + y * 96 + 96, :] for x in range(SIDE)], axis=0)
        hp[0, y * 384:y * 384 + 384] = dot(pick, block).astype(BF)
    z_, core_, y_, s_ = digits(d, (2, SIDE, SLOTS))
    pick = pick_from(y_ * 96 + z_ * 24 + core_ * 12 + s_)
    for x in range(SIDE):
        got = dot(pick, hid[x * 384:x * 384 + 384, :]).astype(BF)
        for n in range(8):
            to = n // 2 * 384 + (n % 2 * SIDE + x) * 48
            hp[1, to:to + 48] = got[n * 48:n * 48 + 48]
    core_, y_, z_, s_ = digits(d, (SIDE, SIDE, SLOTS))
    pick = pick_from(y_ * 96 + z_ * 24 + core_ * 12 + s_)
    for x in range(SIDE):
        hp[2, x * 384:x * 384 + 384] = dot(pick, hid[x * 384:x * 384 + 384, :]).astype(BF)

    onward(1)
    onward(3)

    for n in (4, 5, 6):
        loads[n].wait()
    ctx_arrive(ssend, srecv, b_s, b_r)

    def widen(j, _):
        f32buf[j] = srecv[j].astype(F32)
        return 0

    lax.fori_loop(0, CTX, widen, 0, unroll=4)

    def attend(h, _):
        cum = cum_s[:, head(h)]
        q_dec = q[:, head(h)].astype(F32) * jnp.exp(cum)
        k_dec = (k[:, head(h)].astype(F32) * jnp.exp(-cum)).astype(BF)
        scores = (dot(q_dec.astype(BF), k_dec, NT) * allowed[...]).astype(BF)
        q_c = (q_dec * carried[...]).astype(BF)
        qcar[:, head(h)] = q_c
        st = f32buf[:, rows_of(h, 8), :].reshape(HD, HD).astype(BF)
        state[h] = st
        out = SCALING * (dot(scores, v[:, head(h)]) + dot(q_c, st, NT))
        mixed[:, head(h)] = res[:, head(h)].astype(F32) + out.astype(BF).astype(F32)
        return 0

    lax.fori_loop(0, HEADS, attend, 0, unroll=UNROLL)
    state_out = pltpu.make_async_copy(state, state_o, out_sem.at[0])
    state_out.start()

    def third(i):
        return slice(i * THIRD, (i + 1) * THIRD)

    def lane_sum(x):
        acc = x[:, 0:HD]
        for n in range(1, x.shape[1] // HD):
            acc = acc + x[:, n * HD:(n + 1) * HD]
        return jnp.sum(acc, axis=1, keepdims=True)

    sq = sum(lane_sum(mixed[:, third(i)] * mixed[:, third(i)]) for i in range(3))
    inverse = lax.rsqrt(sq * (1.0 / WIDTH) + NORM_EPS)
    logits = sum(dot((mixed[:, third(i)] * inverse).astype(BF), router[third(i), :]) for i in range(3))
    rank_t = jnp.full((EXPERTS, TOK), -1.0, F32)
    for j in range(TOP):
        eq = info[j:j + 1, :] == iota((EXPERTS, TOK), 0).astype(F32)
        rank_t = jnp.where(eq, info[TOP + j:TOP + j + 1, :], rank_t)
    rank = jnp.transpose(rank_t)
    chosen = jnp.where(rank >= 0.0, 1.0, 0.0)
    gate = chosen * jax.nn.sigmoid(logits)
    total = jnp.sum(gate, axis=1, keepdims=True)
    weights = gate / total
    w_round = weights.astype(BF).astype(F32)
    rows_ = []
    for s in range(SLOTS):
        rows_.append(jnp.sum(jnp.where(rank == float(s), w_round, 0.0), axis=0, keepdims=True))
    w_t = jnp.concatenate(rows_ + [jnp.zeros((4, EXPERTS), F32)], axis=0).astype(BF)
    turn_e, turn_c = digits(iota((EXPERTS, EXPERTS), 0).astype(F32), (CTX,))
    turn = jnp.where(turn_c * 8 + turn_e == iota((EXPERTS, EXPERTS), 1).astype(F32), 1.0, 0.0).astype(BF)
    small[...] = jnp.zeros_like(small)
    small[:, 0:16] = dot(turn, w_t, NT)
    wsend[...] = small[...].reshape(8, CTX, EXPERTS)

    def exp_out(src, dst, ss, rs):
        def one(i, _):
            t = lax.rem(ex + i, 8)
            remote(src.at[t], dst.at[:, ex], ss.at[i], rs.at[ex], (ctx, t)).start()
            return 0

        lax.fori_loop(1, 8, one, 0)
        pltpu.make_async_copy(src.at[ex], dst.at[:, ex], rs.at[ex]).start()

    def exp_in(src, dst, ss, rs):
        def one(i, _):
            pltpu.make_async_copy(src.at[0], dst.at[:, i], rs.at[i]).wait()
            return 0

        lax.fori_loop(0, 8, one, 0)

    def exp_sent(src, dst, ss, rs):
        def one(i, _):
            pltpu.make_async_copy(src.at[0], dst.at[:, 0], ss.at[i]).wait()
            return 0

        lax.fori_loop(1, 8, one, 0)

    exp_out(wsend, wmid, w1_s, w1_r)
    onward(2)

    for i in range(3):
        for by in (1, 2, 3):
            pltpu.make_async_copy(s2.at[i, pl.ds(0, 384)], r2.at[i, pl.ds(0, 384)], s2_s.at[i, by]).wait()
    loads[8].wait()
    for i in range(3):
        def produce(n, _, i=i):
            s2[i, rows_of(n, 384)] = dot(hp[i, rows_of(n, 384)], w[:, third(i)]).astype(BF)
            return 0

        lax.fori_loop(0, SIDE, produce, 0)
    exp_in(wsend, wmid, w1_s, w1_r)
    ctx_exchange(wmid, wrecv, w2_s, w2_r)

    p_core, p_c, p_a, p_s = digits(d, (SIDE, SIDE, SLOTS))
    lanes_r = iota((384, EXPERTS), 1)
    own_slot = lanes_r == p_s.astype(I32)
    small[...] = jnp.zeros_like(small)

    def score_group(b_by):
        for i, (A, B, C) in enumerate(AXES):
            b = lax.rem(here[B] + b_by, SIDE)
            rows = rows_of(b, 384)
            pltpu.make_async_copy(s2.at[i, pl.ds(0, 384)], arr.at[i, rows], s3_r.at[i, b]).wait()
            score = lane_sum(s2[i, rows].astype(F32) * arr[i, rows].astype(F32))
            at_slot = jnp.where(own_slot, score, 0.0)
            coord = [None, None, None]
            coord[A], coord[B], coord[C] = p_a, b.astype(F32), p_c
            to = (coord[2] * 2 + p_core) * CTX + coord[0] * SIDE + coord[1]
            spread = jnp.where(lanes_r == to.astype(I32), 1.0, 0.0).astype(BF)
            hi, lo = split(at_slot)
            small[...] += dot(spread, hi, TN) + dot(spread, lo, TN)

    def grad_group(i, b_by):
        A, B, C = AXES[i]
        b = lax.rem(here[B] + b_by, SIDE)
        src = p_a * STRIDE[A] + b.astype(F32) * STRIDE[B] + p_c * STRIDE[C] + p_core
        pick = jnp.where(lanes_r == src.astype(I32), 1.0, 0.0).astype(BF)
        w_in = wrecv[...].reshape(EXPERTS, EXPERTS).astype(BF)
        col = jnp.sum(jnp.where(own_slot, dot(pick, w_in), 0.0), axis=1, keepdims=True)
        scaled = (arr[i, rows_of(b, 384)].astype(F32) * col).astype(BF)
        part = dot(hp[i, rows_of(b, 384)], scaled, TN)
        if b_by == 0:
            gbuf[i] = part
        else:
            gbuf[i] += part

    grads = []

    def last_grad(i):
        for by in range(SIDE):
            grad_group(i, by)
        cp = pltpu.make_async_copy(gbuf.at[i], grad_o.at[:, pl.ds(i * THIRD, THIRD)], out_sem.at[3 + i])
        cp.start()
        grads.append(cp)

    score_group(0)
    score_group(1)
    score_group(3)
    score_group(2)
    csend[...] = small[...].reshape(8, CTX, EXPERTS)
    exp_out(csend, cmid, c1_s, c1_r)
    exp_in(csend, cmid, c1_s, c1_r)
    ctx_exchange(cmid, crecv, c2_s, c2_r)
    ctx_arrive(wmid, wrecv, w2_s, w2_r)
    last_grad(0)
    ctx_arrive(cmid, crecv, c2_s, c2_r)

    back = jnp.transpose(crecv[...].reshape(EXPERTS, EXPERTS))
    prob = jnp.zeros((TOK, EXPERTS), F32)
    for s in range(SLOTS):
        prob = jnp.where(rank == float(s), back[s:s + 1], prob)
    mix = jnp.sum(weights * prob, axis=1, keepdims=True)
    logit_grad = (chosen * ((prob - mix) / total * gate * (1.0 - gate))).astype(BF)
    mean = 0.0
    for i in range(3):
        ng = dot(logit_grad, router[third(i), :], NT)
        cum_s[:, third(i)] = ng
        mean = mean + lane_sum(ng * mixed[:, third(i)])
    pull = inverse * inverse * inverse * (mean * (1.0 / WIDTH))

    def residual(h, _):
        grad = (
            og[:, head(h)].astype(F32) + inverse * cum_s[:, head(h)] - mixed[:, head(h)] * pull
        ).astype(BF)
        cot[:, head(h)] = grad
        adj = SCALING * dot(grad, qcar[:, head(h)], TN)
        f32buf[:, rows_of(h, 8), :] = adj.reshape(CTX, 8, HD)
        return 0

    lax.fori_loop(0, HEADS, residual, 0, unroll=UNROLL)

    def pack_back(j, _):
        asend[j] = f32buf[j].astype(BF)
        return 0

    lax.fori_loop(0, CTX, pack_back, 0, unroll=4)
    ctx_exchange(asend, arecv, a_s, a_r)
    gres_out = pltpu.make_async_copy(cot, gres_o, out_sem.at[1])
    gres_out.start()
    last_grad(1)
    ctx_arrive(asend, arecv, a_s, a_r)

    def backward(n, acc):
        j = CTX - 1 - n
        bsend[j] = acc.astype(BF)
        return factor(j) * acc + arecv[j].astype(F32)

    lax.fori_loop(0, CTX, backward, jnp.zeros((GROUP, HD), F32), unroll=2)
    ctx_exchange(bsend, brecv, e_s, e_r)
    last_grad(2)
    ctx_arrive(bsend, brecv, e_s, e_r)

    def widen_back(j, _):
        f32buf[j] = brecv[j].astype(F32)
        return 0

    lax.fori_loop(0, CTX, widen_back, 0, unroll=4)
    state_out.wait()

    def gather(h, _):
        state[h] = f32buf[:, rows_of(h, 8), :].reshape(HD, HD).astype(BF)
        return 0

    lax.fori_loop(0, HEADS, gather, 0, unroll=UNROLL)
    sgrad_out = pltpu.make_async_copy(state, sgrad_o, out_sem.at[2])
    sgrad_out.start()

    for cp in sends:
        cp.wait_send()
    ctx_sent(fsend, frecv, f_s, f_r)
    ctx_sent(ssend, srecv, b_s, b_r)
    ctx_sent(asend, arecv, a_s, a_r)
    ctx_sent(bsend, brecv, e_s, e_r)
    exp_sent(wsend, wmid, w1_s, w1_r)
    exp_sent(csend, cmid, c1_s, c1_r)
    ctx_sent(wmid, wrecv, w2_s, w2_r)
    ctx_sent(cmid, crecv, c2_s, c2_r)
    gres_out.wait()
    sgrad_out.wait()
    for cp in grads:
        cp.wait()


def finish(
    q_h, k_h, v_h, g_h, cot_h, state_h, sgrad_h, starts_ref, w_h, m_h, grad_h,
    dq_h, dk_h, dv_h, dg_h, gres_h, nw_h, nm_h,
    q, k, v, g, cot, state, sgrad, w, m, grad, dq, dk, dv, dg, in_sem, out_sem, l_sem, s_sem,
):
    wide, tall = PER * HD, FF // LION_STEPS
    head_steps = HEADS // PER

    def cols(n):
        return pl.ds(n * wide, wide)

    def rows(n):
        return pl.ds(n * tall, tall)

    def loads(n):
        out = [
            pltpu.make_async_copy(a.at[:, cols(n)], b.at[:, cols(n)], in_sem.at[n, j])
            for j, (a, b) in enumerate(((g_h, g), (k_h, k), (q_h, q), (v_h, v), (cot_h, cot)))
        ]
        for j, (a, b) in enumerate(((state_h, state), (sgrad_h, sgrad))):
            out.append(pltpu.make_async_copy(a.at[pl.ds(n * PER, PER)], b.at[pl.ds(n * PER, PER)], in_sem.at[n, 5 + j]))
        return out

    def lion_loads(n):
        return [
            pltpu.make_async_copy(a.at[rows(n)], b.at[rows(n)], l_sem.at[n, j])
            for j, (a, b) in enumerate(((w_h, w), (m_h, m), (grad_h, grad)))
        ]

    stores = []

    def store(a, b, sem):
        cp = pltpu.make_async_copy(a, b, sem)
        cp.start()
        stores.append(cp)

    order = []
    for n in range(max(head_steps, LION_STEPS)):
        if n < head_steps:
            order.append(("heads", n, loads(n)))
        if n < LION_STEPS:
            order.append(("lion", n, lion_loads(n)))
    for _, _, copies in order:
        for cp in copies:
            cp.start()

    seg_row, seg_col = segments(starts_ref)
    last_seg = seg_row[:, TOK - 1:TOK]
    lower = iota((TOK, TOK), 0) >= iota((TOK, TOK), 1)
    upper = iota((TOK, TOK), 0) <= iota((TOK, TOK), 1)
    tri, tri_up = lower.astype(F32).astype(BF), upper.astype(F32).astype(BF)
    same = seg_row == seg_col
    below = jnp.where(same & lower, SCALING, 0.0)
    above = jnp.where(same & upper, SCALING, 0.0)
    carried = jnp.where(seg_col == 0.0, SCALING, 0.0)
    tail = jnp.where(seg_col == last_seg, 1.0, 0.0)
    unbroken = jnp.where(last_seg == 0.0, 1.0, 0.0)

    def heads_step(n):
        at_ = slice(n * wide, (n + 1) * wide)
        store(cot.at[:, cols(n)], gres_h.at[:, cols(n)], out_sem.at[n, 4])
        cum = dot(tri, g[:, at_])
        last = cum[TOK - 1:TOK]
        grow, shrink, to_end = jnp.exp(cum), jnp.exp(-cum), jnp.exp(last - cum) * tail
        kf = k[:, at_].astype(F32)
        q_dec = (q[:, at_].astype(F32) * grow).astype(BF)
        k_dec = (kf * shrink).astype(BF)
        key_end = (kf * to_end).astype(BF)
        d_cums, d_lasts = [], []
        R = range(PER)
        part = [slice(j * HD, (j + 1) * HD) for j in R]
        full = [slice(n * wide + j * HD, n * wide + (j + 1) * HD) for j in R]
        vs, cs = [v[:, c] for c in full], [cot[:, c] for c in full]
        scores_t = [(above * dot(k_dec[:, c], q_dec[:, c], NT)).astype(BF) for c in part]
        d_scores = [(below * dot(cs[j], vs[j], NT)).astype(BF) for j in R]
        d_scores_t = [(above * dot(vs[j], cs[j], NT)).astype(BF) for j in R]
        dq_dec = [dot(d_scores[j], k_dec[:, part[j]]) + carried * dot(cs[j], state[n * PER + j]) for j in R]
        dk_dec = [dot(d_scores_t[j], q_dec[:, part[j]]) for j in R]
        dk_end = [dot(vs[j], sgrad[n * PER + j]) for j in R]
        for j in R:
            c, f, st, sg = part[j], full[j], state[n * PER + j], sgrad[n * PER + j]
            dv[:, f] = (dot(scores_t[j], cs[j]) + dot(key_end[:, c], sg, NT)).astype(BF)
            dq[:, f] = (dq_dec[j] * grow[:, c]).astype(BF)
            dk[:, f] = (dk_dec[j] * shrink[:, c] + dk_end[j] * to_end[:, c]).astype(BF)
            end_term = dk_end[j] * key_end[:, c].astype(F32)
            d_cums.append(dq_dec[j] * q_dec[:, c].astype(F32) - dk_dec[j] * k_dec[:, c].astype(F32) - end_term)
            d_lasts.append(
                jnp.sum(end_term, axis=0, keepdims=True)
                + unbroken * jnp.exp(last[:, c]) * jnp.sum(st.astype(F32) * sg.astype(F32), axis=0, keepdims=True))
        hi, lo = split(jnp.concatenate(d_cums, axis=1))
        dg[:, at_] = (dot(tri_up, hi) + dot(tri_up, lo) + jnp.concatenate(d_lasts, axis=1)).astype(BF)
        for j, (a, b) in enumerate(((dq, dq_h), (dk, dk_h), (dv, dv_h), (dg, dg_h))):
            store(a.at[:, cols(n)], b.at[:, cols(n)], out_sem.at[n, j])

    def lion_step(n):
        r = slice(n * tall, (n + 1) * tall)
        for third in range(3):
            c = slice(third * THIRD, (third + 1) * THIRD)
            wf, mf, gf = w[r, c].astype(F32), m[r, c].astype(F32), grad[r, c]
            turn = BETA_ONE * mf + (1.0 - BETA_ONE) * gf
            move = jnp.where(turn > 0.0, -LION_RATE, jnp.where(turn < 0.0, LION_RATE, 0.0))
            w[r, c] = (wf * (1.0 - LION_RATE * WEIGHT_DECAY) + move).astype(BF)
            m[r, c] = (BETA_TWO * mf + (1.0 - BETA_TWO) * gf).astype(BF)
        store(w.at[rows(n)], nw_h.at[rows(n)], s_sem.at[n, 0])
        store(m.at[rows(n)], nm_h.at[rows(n)], s_sem.at[n, 1])

    for kind, n, copies in order:
        for cp in copies:
            cp.wait()
        if kind == "heads":
            heads_step(n)
        else:
            lion_step(n)
    for cp in stores:
        cp.wait()


def local(
    queries, key_vectors, values, log_decay, starts, residual_in, out_grad,
    expert_ids, slot_index, router, hidden_saved, w_down, momentum,
):
    any_, vm = pl.BlockSpec(memory_space=pl.ANY), pl.BlockSpec(memory_space=pltpu.VMEM)
    dma = pltpu.SemaphoreType.DMA
    V = pltpu.VMEM
    scratch = [
        V((TOP, TOK), I32), V((TOP, TOK), I32), V((1, TOK), I32),
        *[V((TOK, WIDTH), BF)] * 6, V((WIDTH, EXPERTS), BF), V((CAP, FF), BF), V((FF, WIDTH), BF),
        V((3, SIDE * TOK, THIRD), BF), V((16, TOK), F32), V((3, SIDE, 16, TOK), F32), V((3, 32, SIDE * TOK), F32),
        *[V((3, CAP, THIRD), BF)] * 3,
        V((3, CAP, FF), BF),
        V((CTX, GROUP, HD), F32), V((CTX, PACK, HD), BF), V((CTX, PACK, HD), BF),
        V((CTX, GROUP, HD), BF), V((CTX, GROUP, HD), BF), V((HEADS, HD, HD), BF),
        *[V((CTX, GROUP, HD), BF)] * 4,
        V((32, HD), F32), V((TOK, TOK), F32), V((TOK, TOK), F32), V((TOK, WIDTH), F32),
        V((TOK, WIDTH), BF), V((TOK, WIDTH), BF), V((EXPERTS, EXPERTS), F32),
        V((8, CTX, EXPERTS), F32), V((CTX, 8, EXPERTS), F32), V((CTX, 8, EXPERTS), F32),
        V((8, CTX, EXPERTS), F32), V((CTX, 8, EXPERTS), F32), V((CTX, 8, EXPERTS), F32),
        V((3, FF, THIRD), F32), V((TOK, WIDTH), F32),
        dma((12,)), dma((6,)),
        dma((3, 4)), dma((3, 4)), dma((3, 4)), dma((3, 4)), dma((3, 4)), dma((3, 4)), dma((3, 8, 4)), dma((3, 4)),
        dma((CTX,)), dma((CTX,)), dma((CTX,)), dma((CTX,)),
        dma((8,)), dma((8,)), dma((CTX,)), dma((CTX,)), dma((8,)), dma((8,)), dma((CTX,)), dma((CTX,)),
        dma((CTX,)), dma((CTX,)), dma((CTX,)), dma((CTX,)),
    ]
    gres, state, sgrad, grad = pl.pallas_call(
        mixer,
        name="dispatch_and_scan",
        out_shape=(
            jax.ShapeDtypeStruct((TOK, WIDTH), BF),
            jax.ShapeDtypeStruct((HEADS, HD, HD), BF),
            jax.ShapeDtypeStruct((HEADS, HD, HD), BF),
            jax.ShapeDtypeStruct((FF, WIDTH), F32),
        ),
        in_specs=[any_] * 12,
        out_specs=(any_,) * 4,
        scratch_shapes=scratch,
        compiler_params=pltpu.CompilerParams(
            collective_id=0, has_side_effects=True, vmem_limit_bytes=62 * 2**20),
    )(
        out_grad[0], queries[0], key_vectors[0], values[0], log_decay[0], residual_in[0], router,
        hidden_saved[0], w_down[0], expert_ids[0].T, slot_index[0].T, starts,
    )
    tok = V((TOK, WIDTH), BF)
    outs = pl.pallas_call(
        finish,
        name="backward_and_step",
        out_shape=(jax.ShapeDtypeStruct((TOK, WIDTH), BF),) * 5 + (jax.ShapeDtypeStruct((FF, WIDTH), BF),) * 2,
        in_specs=[any_] * 7 + [vm] + [any_] * 3,
        out_specs=(any_,) * 7,
        scratch_shapes=[
            *[tok] * 5, *[V((HEADS, HD, HD), BF)] * 2, *[V((FF, WIDTH), BF)] * 2, V((FF, WIDTH), F32), *[tok] * 4,
            dma((HEADS // PER, 7)), dma((HEADS // PER, 5)), dma((LION_STEPS, 3)), dma((LION_STEPS, 2)),
        ],
        compiler_params=pltpu.CompilerParams(vmem_limit_bytes=62 * 2**20),
    )(
        queries[0], key_vectors[0], values[0], log_decay[0], gres, state, sgrad, starts,
        w_down[0], momentum[0], grad,
    )
    return tuple(x[None] for x in outs)


def solution(mesh):
    tokens = P("exp", "ctx", None)
    owned = P(("ctx", "exp"), None, None)
    in_specs = (tokens,) * 4 + (P("exp", "ctx"),) + (tokens,) * 4 + (P(),) + (owned,) * 3
    out_specs = (tokens,) * 5 + (owned,) * 2
    return jax.shard_map(local, mesh=mesh, in_specs=in_specs, out_specs=out_specs, check_vma=False)
```

```python
import functools

import jax
import jax.numpy as jnp
from jax import lax
from jax.experimental import pallas as pl
from jax.experimental.pallas import tpu as pltpu
from jax.sharding import PartitionSpec as P

HEADS = 18
HD = 128
TOP = 8
TOK = 128
WIDTH = HEADS * HD
FF = 512
SLOTS = 12
EXPERTS = 128
CAP = EXPERTS * SLOTS
PARTS = (768, 768, 768)
STARTS = (0, 768, 1536)
SIDE = 4
CTX = 16
GROUP = HEADS * 8
PACK = GROUP + 32
NORM_EPS = 1e-06
LION_RATE = 0.001
BETA_ONE = 0.9
BETA_TWO = 0.99
WEIGHT_DECAY = 0.1
SCALING = HD ** (-0.5)
BF = jnp.bfloat16
F32 = jnp.float32
I32 = jnp.int32
UNROLL = 3
PER = 6
MESH = pl.DeviceIdType.MESH
STRIDE = (32, 8, 2)
AXES = ((0, 1, 2), (1, 2, 0), (2, 0, 1))


def dot(a, b, dims=((1,), (0,))):
    return lax.dot_general(a, b, (dims, ((), ())), preferred_element_type=F32)


NN = ((1,), (0,))
NT = ((1,), (1,))
TN = ((0,), (0,))


def split(x):
    hi = x.astype(BF)
    return hi, (x - hi.astype(F32)).astype(BF)


def part(i):
    return slice(STARTS[i], STARTS[i] + PARTS[i])


def lanes(i):
    return pl.ds(STARTS[i], PARTS[i])


def half_lanes(i, h):
    return pl.ds(STARTS[i] + h * (PARTS[i] // 2), PARTS[i] // 2)


def iota(shape, dim):
    return lax.broadcasted_iota(I32, shape, dim)


def lower_ones():
    return (iota((TOK, TOK), 0) >= iota((TOK, TOK), 1)).astype(F32).astype(BF)


def segments(starts_ref):
    begin = jnp.broadcast_to(starts_ref[...].astype(F32), (8, TOK)).astype(BF)
    tri = lower_ones()
    row = dot(begin, tri, NT)[0:1]
    col = dot(tri, begin, NT)[:, 0:1]
    return row, col


def head(h):
    return pl.ds(pl.multiple_of(h * HD, HD), HD)


def floor_div(r, by):
    return jnp.floor((r + 0.5) * (1.0 / by))


def digits(r, sizes):
    out = []
    for size in reversed(sizes):
        rest = floor_div(r, size)
        out.append(r - size * rest)
        r = rest
    return [r] + out[::-1]


def mixer(
    og_h, q_h, k_h, v_h, g_h, res_h, router_h, hid_h, w_h, m_h, ids_h, slot_h, starts_h,
    gres_o, state_o, sgrad_o, nw_o, nm_o,
    ids_ref, slot_ref, starts_ref, og, q, k, v, g, res, router, hid, w, m,
    ph1, info, inf, tab, s2, r2, arr, hp,
    f32buf, fsend, frecv, ssend, srecv, state, asend, arecv, bsend, brecv,
    prow, allowed, carried, mixed, qcar, cot, small, wsend, wmid, wrecv, csend, cmid, crecv, gbuf, cum_s,
    in_sem, out_sem, s1_s, s1_r, i1_s, i1_r, s2_s, s2_r, s3_s, s3_r, f_s, f_r, b_s, b_r,
    w1_s, w1_r, w2_s, w2_r, c1_s, c1_r, c2_s, c2_r, a_s, a_r, e_s, e_r,
):
    ctx, ex = lax.axis_index("ctx"), lax.axis_index("exp")
    here = (lax.div(ctx, SIDE), lax.rem(ctx, SIDE), lax.div(ex, 2), lax.rem(ex, 2))

    def at(coords):
        return (coords[0] * SIDE + coords[1], coords[2] * 2 + coords[3])

    def moved(axis, by, flip=False):
        c = list(here)
        c[axis] = lax.rem(c[axis] + by, SIDE)
        if flip:
            c[3] = 1 - c[3]
        return tuple(c)

    def remote(src, dst, ss, rs, device):
        return pltpu.make_async_remote_copy(
            src_ref=src, dst_ref=dst, send_sem=ss, recv_sem=rs, device_id=device, device_id_type=MESH
        )

    barrier = pltpu.get_barrier_semaphore()

    def tell(device):
        pl.semaphore_signal(barrier, inc=1, device_id=device, device_id_type=MESH)

    def tell_ctx(i, _):
        tell((lax.rem(ctx + i, CTX), ex))
        return 0

    def tell_exp(i, _):
        tell((ctx, lax.rem(ex + i, 8)))
        return 0

    lax.fori_loop(1, CTX, tell_ctx, 0)
    lax.fori_loop(1, 8, tell_exp, 0)
    for axis in (0, 1):
        for by in (1, 2, 3):
            tell(at(moved(axis, by, True)))
    loads = []
    for n, (a, b) in enumerate(
        ((ids_h, ids_ref), (slot_h, slot_ref), (starts_h, starts_ref), (og_h, og), (k_h, k), (v_h, v), (g_h, g), (q_h, q), (res_h, res), (router_h, router), (hid_h, hid), (w_h, w), (m_h, m))
    ):
        loads.append(pltpu.make_async_copy(a, b, in_sem.at[n]))
        loads[-1].start()

    small_loads, loads = loads[:3], loads[3:]
    for cp in small_loads:
        cp.wait()
    info[0:TOP] = ids_ref[...].astype(F32)
    info[TOP:2 * TOP] = slot_ref[...].astype(F32)

    pl.semaphore_wait(barrier, CTX - 1 + 7 + 6)

    loads[0].wait()
    sends = []

    def send(src, dst, ss, rs, device):
        cp = remote(src, dst, ss, rs, device)
        cp.start()
        sends.append(cp)

    def rows_of(n, size):
        return pl.ds(pl.multiple_of(n * size, size), size)

    for by in (1, 3, 2):
        for i in range(3):
            send(info, inf.at[i, here[i]], i1_s.at[i, by], i1_r.at[i, here[i]], at(moved(i, by)))
    for h in range(2):
        for by in (1, 3, 2):
            for i in range(3):
                send(og.at[:, half_lanes(i, h)], ph1.at[rows_of(here[i], TOK), half_lanes(i, h)],
                     s1_s.at[i, h, by], s1_r.at[i, h, here[i]], at(moved(i, by)))
    for i in range(3):
        for h in range(2):
            pltpu.make_async_copy(
                og.at[:, half_lanes(i, h)], ph1.at[rows_of(here[i], TOK), half_lanes(i, h)],
                s1_r.at[i, h, here[i]]).start()
        pltpu.make_async_copy(info, inf.at[i, here[i]], i1_r.at[i, here[i]]).start()

    for n in (1, 2, 3):
        loads[n].wait()
    seg_row, seg_col = segments(starts_ref)
    last_seg = seg_row[:, TOK - 1:TOK]
    tri = lower_ones()
    allowed[...] = jnp.where(
        (seg_row == seg_col) & (iota((TOK, TOK), 0) >= iota((TOK, TOK), 1)), 1.0, 0.0)
    carried[...] = jnp.broadcast_to(jnp.where(seg_col == 0.0, 1.0, 0.0), (TOK, TOK))
    tail = jnp.broadcast_to(jnp.where(seg_col == last_seg, 1.0, 0.0), (TOK, TOK))
    unbroken = jnp.where(last_seg == 0.0, 1.0, 0.0)
    prow[...] = jnp.zeros_like(prow)

    def own_state(h, _):
        cum = dot(tri, g[:, head(h)])
        cum_s[:, head(h)] = cum
        last = cum[TOK - 1:TOK]
        key_end = (k[:, head(h)].astype(F32) * jnp.exp(last - cum) * tail).astype(BF)
        fresh = dot(v[:, head(h)], key_end, TN)
        f32buf[:, rows_of(h, 8), :] = fresh.reshape(CTX, 8, HD)
        prow[pl.ds(h, 1), :] = jnp.exp(last) * unbroken
        return 0

    lax.fori_loop(0, HEADS, own_state, 0, unroll=UNROLL)
    passing = prow[...].astype(BF)

    def pack(j, _):
        fsend[j, 0:GROUP, :] = f32buf[j].astype(BF)
        fsend[j, GROUP:PACK, :] = passing
        return 0

    lax.fori_loop(0, CTX, pack, 0, unroll=4)

    def ctx_exchange(src, dst, ss, rs, rows=None):
        def of(ref, n):
            return ref.at[n] if rows is None else ref.at[n, rows]

        def one(i, _):
            i7 = lax.rem(i * 7, CTX)
            t = lax.rem(here[0] + lax.div(i7, SIDE), SIDE) * SIDE + lax.rem(here[1] + lax.rem(i7, SIDE), SIDE)
            remote(of(src, t), of(dst, ctx), ss.at[i], rs.at[ctx], (t, ex)).start()
            return 0

        lax.fori_loop(1, CTX, one, 0)
        pltpu.make_async_copy(of(src, ctx), of(dst, ctx), rs.at[ctx]).start()

    def ctx_arrive(src, dst, ss, rs, rows=None):
        def one(i, _):
            a, b = (src.at[0], dst.at[i]) if rows is None else (src.at[0, rows], dst.at[i, rows])
            pltpu.make_async_copy(a, b, rs.at[i]).wait()
            return 0

        lax.fori_loop(0, CTX, one, 0)

    def ctx_sent(src, dst, ss, rs, rows=None):
        def one(i, _):
            a, b = (src.at[0], dst.at[0]) if rows is None else (src.at[0, rows], dst.at[0, rows])
            pltpu.make_async_copy(a, b, ss.at[i]).wait()
            return 0

        lax.fori_loop(1, CTX, one, 0)

    ctx_exchange(fsend, frecv, f_s, f_r)

    pat_a, pat_s = digits(iota((48, SIDE * TOK), 0).astype(F32), (SLOTS,))
    pattern = jnp.where(pat_a == floor_div(iota((48, SIDE * TOK), 1).astype(F32), TOK), pat_s, -5.0)
    bb, cc, kk = digits(iota((32, TOK), 0).astype(F32), (SIDE, 2))
    for i, (A, B, C) in enumerate(AXES):
        e = bb * STRIDE[B] + cc * STRIDE[C] + kk + (here[A] * STRIDE[A]).astype(F32)
        for a in range(SIDE):
            pltpu.make_async_copy(info, inf.at[i, a], i1_r.at[i, a]).wait()
            found = jnp.full((32, TOK), -1.0, F32)
            for j in range(TOP):
                found = jnp.where(inf[i, a, j:j + 1, :] == e, inf[i, a, TOP + j:TOP + j + 1, :], found)
            tab[i, :, a * TOK:(a + 1) * TOK] = found

    def choose(i, b):
        blocks = []
        for m_ in range(8):
            line = tab[i, pl.ds(b * 8 + m_, 1), :]
            blocks.append(jnp.where(line == pattern, 1.0, 0.0).astype(BF))
        hp[i, rows_of(b, 384)] = jnp.concatenate(blocks, axis=0)

    def half(i, h):
        return slice(STARTS[i] + h * (PARTS[i] // 2), STARTS[i] + (h + 1) * (PARTS[i] // 2))

    def select(i, h, b):
        return dot(hp[i, rows_of(b, 384)], ph1[:, half(i, h)]).astype(BF)

    for h in range(2):
        for by in (1, 3, 2):
            for i, (A, B, C) in enumerate(AXES):
                b = lax.rem(here[B] + by, SIDE)
                if h == 0:
                    choose(i, b)
                if by == 1:
                    for a in range(SIDE):
                        pltpu.make_async_copy(
                            og.at[:, half_lanes(i, h)], ph1.at[pl.ds(a * TOK, TOK), half_lanes(i, h)],
                            s1_r.at[i, h, a]).wait()
                s2[rows_of(b, 384), half(i, h)] = select(i, h, b)
                remote(s2.at[rows_of(b, 384), half_lanes(i, h)], r2.at[rows_of(here[B], 384), half_lanes(i, h)],
                       s2_s.at[i, h, by], s2_r.at[i, h, here[B]], at(moved(B, by))).start()
    for i, (A, B, C) in enumerate(AXES):
        choose(i, here[B])
        for h in range(2):
            r2[rows_of(here[B], 384), half(i, h)] = select(i, h, here[B])

    def onward(b_by):
        for i, (A, B, C) in enumerate(AXES):
            b = lax.rem(here[B] + b_by, SIDE)
            if b_by:
                for h in range(2):
                    pltpu.make_async_copy(
                        s2.at[pl.ds(0, 384), half_lanes(i, h)], r2.at[rows_of(b, 384), half_lanes(i, h)],
                        s2_r.at[i, h, b]).wait()
            slot = here[3] * SIDE + here[C]
            for by in (2, 1, 3, 0):
                for flip in (0, 1):
                    to = moved(C, by, bool(flip))
                    src = r2.at[rows_of(b * 8 + to[C] * 2 + to[3], 48), lanes(i)]
                    dst = arr.at[rows_of(b * 8 + slot, 48), lanes(i)]
                    if by == 0 and flip == 0:
                        pltpu.make_async_copy(src, dst, s3_r.at[i, b]).start()
                    else:
                        send(src, dst, s3_s.at[i, by * 2 + flip, b_by], s3_r.at[i, b], at(to))

    onward(0)

    ctx_arrive(fsend, frecv, f_s, f_r)

    def factor(j, first=0, last=HEADS):
        p = frecv[j, GROUP:PACK, :].astype(F32)
        return jnp.concatenate([jnp.broadcast_to(p[h:h + 1], (8, HD)) for h in range(first, last)], axis=0)

    def forward(j, acc):
        ssend[j] = acc.astype(BF)
        return factor(j) * acc + frecv[j, 0:GROUP, :].astype(F32)

    lax.fori_loop(0, CTX, forward, jnp.zeros((GROUP, HD), F32), unroll=2)
    ctx_exchange(ssend, srecv, b_s, b_r)

    loads[7].wait()
    d = iota((384, 1), 0).astype(F32)
    lanes384 = iota((384, 384), 1)

    def pick_from(where):
        return jnp.where(lanes384 == where.astype(I32), 1.0, 0.0).astype(BF)

    core_, z_, x_, s_ = digits(d, (SIDE, SIDE, SLOTS))
    pick = pick_from(x_ * 96 + z_ * 24 + core_ * 12 + s_)
    for y in range(SIDE):
        block = jnp.concatenate([hid[x * 384 + y * 96:x * 384 + y * 96 + 96, :] for x in range(SIDE)], axis=0)
        hp[0, y * 384:y * 384 + 384] = dot(pick, block).astype(BF)
    z_, core_, y_, s_ = digits(d, (2, SIDE, SLOTS))
    pick = pick_from(y_ * 96 + z_ * 24 + core_ * 12 + s_)
    for x in range(SIDE):
        got = dot(pick, hid[x * 384:x * 384 + 384, :]).astype(BF)
        for n in range(8):
            to = n // 2 * 384 + (n % 2 * SIDE + x) * 48
            hp[1, to:to + 48] = got[n * 48:n * 48 + 48]
    core_, y_, z_, s_ = digits(d, (SIDE, SIDE, SLOTS))
    pick = pick_from(y_ * 96 + z_ * 24 + core_ * 12 + s_)
    for x in range(SIDE):
        hp[2, x * 384:x * 384 + 384] = dot(pick, hid[x * 384:x * 384 + 384, :]).astype(BF)

    onward(1)
    onward(3)
    onward(2)

    for n in (4, 5, 6):
        loads[n].wait()
    ctx_arrive(ssend, srecv, b_s, b_r)

    def widen(j, _):
        f32buf[j] = srecv[j].astype(F32)
        return 0

    lax.fori_loop(0, CTX, widen, 0, unroll=4)

    def attend(h, _):
        cum = cum_s[:, head(h)]
        q_dec = q[:, head(h)].astype(F32) * jnp.exp(cum)
        k_dec = (k[:, head(h)].astype(F32) * jnp.exp(-cum)).astype(BF)
        scores = (dot(q_dec.astype(BF), k_dec, NT) * allowed[...]).astype(BF)
        q_c = (q_dec * carried[...]).astype(BF)
        qcar[:, head(h)] = q_c
        st = f32buf[:, rows_of(h, 8), :].reshape(HD, HD).astype(BF)
        state[h] = st
        out = SCALING * (dot(scores, v[:, head(h)]) + dot(q_c, st, NT))
        mixed[:, head(h)] = res[:, head(h)].astype(F32) + out.astype(BF).astype(F32)
        return 0

    lax.fori_loop(0, HEADS, attend, 0, unroll=UNROLL)
    state_out = pltpu.make_async_copy(state, state_o, out_sem.at[0])
    state_out.start()

    def lane_sum(x):
        acc = x[:, 0:HD]
        for n in range(1, x.shape[1] // HD):
            acc = acc + x[:, n * HD:(n + 1) * HD]
        return jnp.sum(acc, axis=1, keepdims=True)

    sq = sum(lane_sum(mixed[:, part(i)] * mixed[:, part(i)]) for i in range(3))
    inverse = lax.rsqrt(sq * (1.0 / WIDTH) + NORM_EPS)
    logits = sum(dot((mixed[:, part(i)] * inverse).astype(BF), router[part(i), :]) for i in range(3))
    rank_t = jnp.full((EXPERTS, TOK), -1.0, F32)
    for j in range(TOP):
        eq = info[j:j + 1, :] == iota((EXPERTS, TOK), 0).astype(F32)
        rank_t = jnp.where(eq, info[TOP + j:TOP + j + 1, :], rank_t)
    rank = jnp.transpose(rank_t)
    chosen = jnp.where(rank >= 0.0, 1.0, 0.0)
    gate = chosen * jax.nn.sigmoid(logits)
    total = jnp.sum(gate, axis=1, keepdims=True)
    weights = gate / total
    w_round = weights.astype(BF).astype(F32)
    rows_ = []
    for s in range(SLOTS):
        rows_.append(jnp.sum(jnp.where(rank == float(s), w_round, 0.0), axis=0, keepdims=True))
    w_t = jnp.concatenate(rows_ + [jnp.zeros((4, EXPERTS), F32)], axis=0).astype(BF)
    turn_e, turn_c = digits(iota((EXPERTS, EXPERTS), 0).astype(F32), (CTX,))
    turn = jnp.where(turn_c * 8 + turn_e == iota((EXPERTS, EXPERTS), 1).astype(F32), 1.0, 0.0).astype(BF)
    small[...] = jnp.zeros_like(small)
    small[:, 0:16] = dot(turn, w_t, NT)
    wsend[...] = small[...].reshape(8, CTX, EXPERTS)

    def exp_out(src, dst, ss, rs):
        def one(i, _):
            t = lax.rem(ex + i, 8)
            remote(src.at[t], dst.at[:, ex], ss.at[i], rs.at[ex], (ctx, t)).start()
            return 0

        lax.fori_loop(1, 8, one, 0)
        pltpu.make_async_copy(src.at[ex], dst.at[:, ex], rs.at[ex]).start()

    def exp_in(src, dst, ss, rs):
        def one(i, _):
            pltpu.make_async_copy(src.at[0], dst.at[:, i], rs.at[i]).wait()
            return 0

        lax.fori_loop(0, 8, one, 0)

    def exp_sent(src, dst, ss, rs):
        def one(i, _):
            pltpu.make_async_copy(src.at[0], dst.at[:, 0], ss.at[i]).wait()
            return 0

        lax.fori_loop(1, 8, one, 0)

    exp_out(wsend, wmid, w1_s, w1_r)

    for i in range(3):
        for by in (1, 2, 3):
            for h in range(2):
                pltpu.make_async_copy(
                    s2.at[pl.ds(0, 384), half_lanes(i, h)], r2.at[pl.ds(0, 384), half_lanes(i, h)],
                    s2_s.at[i, h, by]).wait()
    loads[8].wait()
    for i in range(3):
        def produce(n, _, i=i):
            s2[rows_of(n, 384), part(i)] = dot(hp[i, rows_of(n, 384)], w[:, part(i)]).astype(BF)
            return 0

        lax.fori_loop(0, SIDE, produce, 0)
    exp_in(wsend, wmid, w1_s, w1_r)
    ctx_exchange(wmid, wrecv, w2_s, w2_r)

    p_core, p_c, p_a, p_s = digits(d, (SIDE, SIDE, SLOTS))
    lanes_r = iota((384, EXPERTS), 1)
    own_slot = lanes_r == p_s.astype(I32)
    small[...] = jnp.zeros_like(small)

    def score_group(b_by):
        for i, (A, B, C) in enumerate(AXES):
            b = lax.rem(here[B] + b_by, SIDE)
            rows = rows_of(b, 384)
            pltpu.make_async_copy(s2.at[pl.ds(0, 384), lanes(i)], arr.at[rows, lanes(i)], s3_r.at[i, b]).wait()
            score = lane_sum(s2[rows, part(i)].astype(F32) * arr[rows, part(i)].astype(F32))
            at_slot = jnp.where(own_slot, score, 0.0)
            coord = [None, None, None]
            coord[A], coord[B], coord[C] = p_a, b.astype(F32), p_c
            to = (coord[2] * 2 + p_core) * CTX + coord[0] * SIDE + coord[1]
            spread = jnp.where(lanes_r == to.astype(I32), 1.0, 0.0).astype(BF)
            hi, lo = split(at_slot)
            small[...] += dot(spread, hi, TN) + dot(spread, lo, TN)

    def grad_group(i, b_by):
        A, B, C = AXES[i]
        b = lax.rem(here[B] + b_by, SIDE)
        src = p_a * STRIDE[A] + b.astype(F32) * STRIDE[B] + p_c * STRIDE[C] + p_core
        pick = jnp.where(lanes_r == src.astype(I32), 1.0, 0.0).astype(BF)
        w_in = wrecv[...].reshape(EXPERTS, EXPERTS).astype(BF)
        col = jnp.sum(jnp.where(own_slot, dot(pick, w_in), 0.0), axis=1, keepdims=True)
        scaled = (arr[rows_of(b, 384), part(i)].astype(F32) * col).astype(BF)
        piece = dot(hp[i, rows_of(b, 384)], scaled, TN)
        if b_by == 0:
            gbuf[:, 0:PARTS[i]] = piece
        else:
            gbuf[:, 0:PARTS[i]] += piece

    grads = []

    def last_grad(i):
        for by in range(SIDE):
            grad_group(i, by)

        def step(n, _):
            r = rows_of(n, 64)
            wf, mf, gf = w[r, part(i)].astype(F32), m[r, part(i)].astype(F32), gbuf[r, 0:PARTS[i]]
            turn = BETA_ONE * mf + (1.0 - BETA_ONE) * gf
            move = jnp.where(turn > 0.0, -LION_RATE, jnp.where(turn < 0.0, LION_RATE, 0.0))
            w[r, part(i)] = (wf * (1.0 - LION_RATE * WEIGHT_DECAY) + move).astype(BF)
            m[r, part(i)] = (BETA_TWO * mf + (1.0 - BETA_TWO) * gf).astype(BF)
            return 0

        lax.fori_loop(0, FF // 64, step, 0)
        for n, (a, b) in enumerate(((w, nw_o), (m, nm_o))):
            cp = pltpu.make_async_copy(a.at[:, lanes(i)], b.at[:, lanes(i)], out_sem.at[3 + 2 * i + n])
            cp.start()
            grads.append(cp)

    score_group(0)
    score_group(1)
    score_group(3)
    score_group(2)
    csend[...] = small[...].reshape(8, CTX, EXPERTS)
    exp_out(csend, cmid, c1_s, c1_r)
    exp_in(csend, cmid, c1_s, c1_r)
    ctx_exchange(cmid, crecv, c2_s, c2_r)
    ctx_arrive(wmid, wrecv, w2_s, w2_r)
    loads[9].wait()
    last_grad(2)
    ctx_arrive(cmid, crecv, c2_s, c2_r)

    back = jnp.transpose(crecv[...].reshape(EXPERTS, EXPERTS))
    prob = jnp.zeros((TOK, EXPERTS), F32)
    for s in range(SLOTS):
        prob = jnp.where(rank == float(s), back[s:s + 1], prob)
    mix = jnp.sum(weights * prob, axis=1, keepdims=True)
    logit_grad = (chosen * ((prob - mix) / total * gate * (1.0 - gate))).astype(BF)
    mean = 0.0
    for i in range(3):
        ng = dot(logit_grad, router[part(i), :], NT)
        cum_s[:, part(i)] = ng
        mean = mean + lane_sum(ng * mixed[:, part(i)])
    pull = inverse * inverse * inverse * (mean * (1.0 / WIDTH))

    def residual(h, _):
        grad = (
            og[:, head(h)].astype(F32) + inverse * cum_s[:, head(h)] - mixed[:, head(h)] * pull
        ).astype(BF)
        cot[:, head(h)] = grad
        adj = SCALING * dot(grad, qcar[:, head(h)], TN)
        f32buf[:, rows_of(h, 8), :] = adj.reshape(CTX, 8, HD)
        return 0

    halves = ((0, 10), (10, HEADS))

    def half_rows(n):
        first, last = halves[n]
        return pl.ds(first * 8, (last - first) * 8)

    for n, (first, last) in enumerate(halves):
        lax.fori_loop(first, last, residual, 0, unroll=2)

        def pack_back(j, _, n=n):
            asend[j, half_rows(n), :] = f32buf[j, half_rows(n), :].astype(BF)
            return 0

        lax.fori_loop(0, CTX, pack_back, 0, unroll=4)
        ctx_exchange(asend, arecv, a_s.at[n], a_r.at[n], half_rows(n))
    gres_out = pltpu.make_async_copy(cot, gres_o, out_sem.at[1])
    gres_out.start()
    last_grad(0)
    for n, (first, last) in enumerate(halves):
        ctx_arrive(asend, arecv, a_s.at[n], a_r.at[n], half_rows(n))

        def backward(t, acc, n=n, first=first, last=last):
            j = CTX - 1 - t
            bsend[j, half_rows(n), :] = acc.astype(BF)
            return factor(j, first, last) * acc + arecv[j, half_rows(n), :].astype(F32)

        lax.fori_loop(0, CTX, backward, jnp.zeros(((last - first) * 8, HD), F32), unroll=2)
        ctx_exchange(bsend, brecv, e_s.at[n], e_r.at[n], half_rows(n))
    last_grad(1)
    for n in range(2):
        ctx_arrive(bsend, brecv, e_s.at[n], e_r.at[n], half_rows(n))

    def widen_back(j, _):
        f32buf[j] = brecv[j].astype(F32)
        return 0

    lax.fori_loop(0, CTX, widen_back, 0, unroll=4)
    state_out.wait()

    def gather(h, _):
        state[h] = f32buf[:, rows_of(h, 8), :].reshape(HD, HD).astype(BF)
        return 0

    lax.fori_loop(0, HEADS, gather, 0, unroll=UNROLL)
    sgrad_out = pltpu.make_async_copy(state, sgrad_o, out_sem.at[2])
    sgrad_out.start()

    for cp in sends:
        cp.wait_send()
    ctx_sent(fsend, frecv, f_s, f_r)
    ctx_sent(ssend, srecv, b_s, b_r)
    for n in range(2):
        ctx_sent(asend, arecv, a_s.at[n], a_r.at[n], half_rows(n))
        ctx_sent(bsend, brecv, e_s.at[n], e_r.at[n], half_rows(n))
    exp_sent(wsend, wmid, w1_s, w1_r)
    exp_sent(csend, cmid, c1_s, c1_r)
    ctx_sent(wmid, wrecv, w2_s, w2_r)
    ctx_sent(cmid, crecv, c2_s, c2_r)
    gres_out.wait()
    sgrad_out.wait()
    for cp in grads:
        cp.wait()


def finish(
    q_h, k_h, v_h, g_h, cot_h, state_h, sgrad_h, starts_ref, stepped_h, moment_h,
    dq_h, dk_h, dv_h, dg_h, gres_h, nw_h, nm_h,
    q, k, v, g, cot, state, sgrad, stepped, moment, dq, dk, dv, dg, in_sem, out_sem, pass_sem,
):
    wide = PER * HD
    head_steps = HEADS // PER

    def cols(n):
        return pl.ds(n * wide, wide)

    def loads(n):
        out = [
            pltpu.make_async_copy(a.at[:, cols(n)], b.at[:, cols(n)], in_sem.at[n, j])
            for j, (a, b) in enumerate(((g_h, g), (k_h, k), (q_h, q), (v_h, v), (cot_h, cot)))
        ]
        for j, (a, b) in enumerate(((state_h, state), (sgrad_h, sgrad))):
            out.append(pltpu.make_async_copy(a.at[pl.ds(n * PER, PER)], b.at[pl.ds(n * PER, PER)], in_sem.at[n, 5 + j]))
        return out

    stores = []

    def store(a, b, sem):
        cp = pltpu.make_async_copy(a, b, sem)
        cp.start()
        stores.append(cp)

    order = [loads(n) for n in range(head_steps)]
    for copies in order:
        for cp in copies:
            cp.start()
    through = []
    for j, (a, b) in enumerate(((stepped_h, stepped), (moment_h, moment))):
        through.append(pltpu.make_async_copy(a, b, pass_sem.at[j]))
        through[-1].start()

    seg_row, seg_col = segments(starts_ref)
    last_seg = seg_row[:, TOK - 1:TOK]
    lower = iota((TOK, TOK), 0) >= iota((TOK, TOK), 1)
    upper = iota((TOK, TOK), 0) <= iota((TOK, TOK), 1)
    tri, tri_up = lower.astype(F32).astype(BF), upper.astype(F32).astype(BF)
    same = seg_row == seg_col
    below = jnp.where(same & lower, SCALING, 0.0)
    above = jnp.where(same & upper, SCALING, 0.0)
    carried = jnp.where(seg_col == 0.0, SCALING, 0.0)
    tail = jnp.where(seg_col == last_seg, 1.0, 0.0)
    unbroken = jnp.where(last_seg == 0.0, 1.0, 0.0)

    def heads_step(n):
        at_ = slice(n * wide, (n + 1) * wide)
        store(cot.at[:, cols(n)], gres_h.at[:, cols(n)], out_sem.at[n, 4])
        cum = dot(tri, g[:, at_])
        last = cum[TOK - 1:TOK]
        grow, shrink, to_end = jnp.exp(cum), jnp.exp(-cum), jnp.exp(last - cum) * tail
        kf = k[:, at_].astype(F32)
        q_dec = (q[:, at_].astype(F32) * grow).astype(BF)
        k_dec = (kf * shrink).astype(BF)
        key_end = (kf * to_end).astype(BF)
        d_cums, d_lasts = [], []
        R = range(PER)
        part = [slice(j * HD, (j + 1) * HD) for j in R]
        full = [slice(n * wide + j * HD, n * wide + (j + 1) * HD) for j in R]
        vs, cs = [v[:, c] for c in full], [cot[:, c] for c in full]
        scores_t = [(above * dot(k_dec[:, c], q_dec[:, c], NT)).astype(BF) for c in part]
        d_scores = [(below * dot(cs[j], vs[j], NT)).astype(BF) for j in R]
        d_scores_t = [(above * dot(vs[j], cs[j], NT)).astype(BF) for j in R]
        dq_dec = [dot(d_scores[j], k_dec[:, part[j]]) + carried * dot(cs[j], state[n * PER + j]) for j in R]
        dk_dec = [dot(d_scores_t[j], q_dec[:, part[j]]) for j in R]
        dk_end = [dot(vs[j], sgrad[n * PER + j]) for j in R]
        for j in R:
            c, f, st, sg = part[j], full[j], state[n * PER + j], sgrad[n * PER + j]
            dv[:, f] = (dot(scores_t[j], cs[j]) + dot(key_end[:, c], sg, NT)).astype(BF)
            dq[:, f] = (dq_dec[j] * grow[:, c]).astype(BF)
            dk[:, f] = (dk_dec[j] * shrink[:, c] + dk_end[j] * to_end[:, c]).astype(BF)
            end_term = dk_end[j] * key_end[:, c].astype(F32)
            d_cums.append(dq_dec[j] * q_dec[:, c].astype(F32) - dk_dec[j] * k_dec[:, c].astype(F32) - end_term)
            d_lasts.append(
                jnp.sum(end_term, axis=0, keepdims=True)
                + unbroken * jnp.exp(last[:, c]) * jnp.sum(st.astype(F32) * sg.astype(F32), axis=0, keepdims=True))
        hi, lo = split(jnp.concatenate(d_cums, axis=1))
        dg[:, at_] = (dot(tri_up, hi) + dot(tri_up, lo) + jnp.concatenate(d_lasts, axis=1)).astype(BF)
        for j, (a, b) in enumerate(((dq, dq_h), (dk, dk_h), (dv, dv_h), (dg, dg_h))):
            store(a.at[:, cols(n)], b.at[:, cols(n)], out_sem.at[n, j])

    for n, copies in enumerate(order):
        for cp in copies:
            cp.wait()
        heads_step(n)
        if n in (1, 2):
            through[n - 1].wait()
            store((stepped, moment)[n - 1], (nw_h, nm_h)[n - 1], pass_sem.at[n + 1])
    for cp in stores:
        cp.wait()


def local(
    queries, key_vectors, values, log_decay, starts, residual_in, out_grad,
    expert_ids, slot_index, router, hidden_saved, w_down, momentum,
):
    any_, vm = pl.BlockSpec(memory_space=pl.ANY), pl.BlockSpec(memory_space=pltpu.VMEM)
    dma = pltpu.SemaphoreType.DMA
    V = pltpu.VMEM
    scratch = [
        V((TOP, TOK), I32), V((TOP, TOK), I32), V((1, TOK), I32),
        *[V((TOK, WIDTH), BF)] * 6, V((WIDTH, EXPERTS), BF), V((CAP, FF), BF), V((FF, WIDTH), BF), V((FF, WIDTH), BF),
        V((SIDE * TOK, WIDTH), BF), V((16, TOK), F32), V((3, SIDE, 16, TOK), F32), V((3, 32, SIDE * TOK), F32),
        *[V((CAP, WIDTH), BF)] * 3,
        V((3, CAP, FF), BF),
        V((CTX, GROUP, HD), F32), V((CTX, PACK, HD), BF), V((CTX, PACK, HD), BF),
        V((CTX, GROUP, HD), BF), V((CTX, GROUP, HD), BF), V((HEADS, HD, HD), BF),
        *[V((CTX, GROUP, HD), BF)] * 4,
        V((32, HD), F32), V((TOK, TOK), F32), V((TOK, TOK), F32), V((TOK, WIDTH), F32),
        V((TOK, WIDTH), BF), V((TOK, WIDTH), BF), V((EXPERTS, EXPERTS), F32),
        V((8, CTX, EXPERTS), F32), V((CTX, 8, EXPERTS), F32), V((CTX, 8, EXPERTS), F32),
        V((8, CTX, EXPERTS), F32), V((CTX, 8, EXPERTS), F32), V((CTX, 8, EXPERTS), F32),
        V((FF, max(PARTS)), F32), V((TOK, WIDTH), F32),
        dma((13,)), dma((9,)),
        dma((3, 2, 4)), dma((3, 2, 4)), dma((3, 4)), dma((3, 4)), dma((3, 2, 4)), dma((3, 2, 4)), dma((3, 8, 4)), dma((3, 4)),
        dma((CTX,)), dma((CTX,)), dma((CTX,)), dma((CTX,)),
        dma((8,)), dma((8,)), dma((CTX,)), dma((CTX,)), dma((8,)), dma((8,)), dma((CTX,)), dma((CTX,)),
        dma((2, CTX)), dma((2, CTX)), dma((2, CTX)), dma((2, CTX)),
    ]
    gres, state, sgrad, stepped, moment = pl.pallas_call(
        mixer,
        name="dispatch_and_scan",
        out_shape=(
            jax.ShapeDtypeStruct((TOK, WIDTH), BF),
            jax.ShapeDtypeStruct((HEADS, HD, HD), BF),
            jax.ShapeDtypeStruct((HEADS, HD, HD), BF),
            jax.ShapeDtypeStruct((FF, WIDTH), BF),
            jax.ShapeDtypeStruct((FF, WIDTH), BF),
        ),
        in_specs=[any_] * 13,
        out_specs=(any_,) * 5,
        scratch_shapes=scratch,
        compiler_params=pltpu.CompilerParams(
            collective_id=0, has_side_effects=True, vmem_limit_bytes=62 * 2**20),
    )(
        out_grad[0], queries[0], key_vectors[0], values[0], log_decay[0], residual_in[0], router,
        hidden_saved[0], w_down[0], momentum[0], expert_ids[0].T, slot_index[0].T, starts,
    )
    tok = V((TOK, WIDTH), BF)
    outs = pl.pallas_call(
        finish,
        name="backward_and_step",
        out_shape=(jax.ShapeDtypeStruct((TOK, WIDTH), BF),) * 5 + (jax.ShapeDtypeStruct((FF, WIDTH), BF),) * 2,
        in_specs=[any_] * 7 + [vm] + [any_] * 2,
        out_specs=(any_,) * 7,
        scratch_shapes=[
            *[tok] * 5, *[V((HEADS, HD, HD), BF)] * 2, *[V((FF, WIDTH), BF)] * 2, *[tok] * 4,
            dma((HEADS // PER, 7)), dma((HEADS // PER, 5)), dma((4,)),
        ],
        compiler_params=pltpu.CompilerParams(vmem_limit_bytes=62 * 2**20),
    )(
        queries[0], key_vectors[0], values[0], log_decay[0], gres, state, sgrad, starts,
        stepped, moment,
    )
    return tuple(x[None] for x in outs)


def solution(mesh):
    tokens = P("exp", "ctx", None)
    owned = P(("ctx", "exp"), None, None)
    in_specs = (tokens,) * 4 + (P("exp", "ctx"),) + (tokens,) * 4 + (P(),) + (owned,) * 3
    out_specs = (tokens,) * 5 + (owned,) * 2
    return jax.shard_map(local, mesh=mesh, in_specs=in_specs, out_specs=out_specs, check_vma=False)
```

```python
import functools

import jax
import jax.numpy as jnp
from jax import lax
from jax.experimental import pallas as pl
from jax.experimental.pallas import tpu as pltpu
from jax.sharding import PartitionSpec as P

HEADS = 18
HD = 128
TOP = 8
TOK = 128
WIDTH = HEADS * HD
FF = 512
SLOTS = 12
EXPERTS = 128
CAP = EXPERTS * SLOTS
PARTS = (768, 768, 768)
STARTS = (0, 768, 1536)
SIDE = 4
CTX = 16
GROUP = HEADS * 8
PACK = GROUP + 32
NORM_EPS = 1e-06
LION_RATE = 0.001
BETA_ONE = 0.9
BETA_TWO = 0.99
WEIGHT_DECAY = 0.1
SCALING = HD ** (-0.5)
BF = jnp.bfloat16
F32 = jnp.float32
I32 = jnp.int32
UNROLL = 6
PER = 9
MESH = pl.DeviceIdType.MESH
STRIDE = (32, 8, 2)
AXES = ((0, 1, 2), (1, 2, 0), (2, 0, 1))


def dot(a, b, dims=((1,), (0,))):
    return lax.dot_general(a, b, (dims, ((), ())), preferred_element_type=F32)


NN = ((1,), (0,))
NT = ((1,), (1,))
TN = ((0,), (0,))


def split(x):
    hi = x.astype(BF)
    return hi, (x - hi.astype(F32)).astype(BF)


def part(i):
    return slice(STARTS[i], STARTS[i] + PARTS[i])


def lanes(i):
    return pl.ds(STARTS[i], PARTS[i])


def half_lanes(i, h):
    return pl.ds(STARTS[i] + h * (PARTS[i] // 2), PARTS[i] // 2)


def iota(shape, dim):
    return lax.broadcasted_iota(I32, shape, dim)


def lower_ones():
    return (iota((TOK, TOK), 0) >= iota((TOK, TOK), 1)).astype(F32).astype(BF)


def segments(starts_ref):
    begin = jnp.broadcast_to(starts_ref[...].astype(F32), (8, TOK)).astype(BF)
    tri = lower_ones()
    row = dot(begin, tri, NT)[0:1]
    col = dot(tri, begin, NT)[:, 0:1]
    return row, col


def head(h):
    return pl.ds(pl.multiple_of(h * HD, HD), HD)


def floor_div(r, by):
    return jnp.floor((r + 0.5) * (1.0 / by))


def digits(r, sizes):
    out = []
    for size in reversed(sizes):
        rest = floor_div(r, size)
        out.append(r - size * rest)
        r = rest
    return [r] + out[::-1]


def mixer(
    og_h, q_h, k_h, v_h, g_h, res_h, router_h, hid_h, w_h, m_h, ids_h, slot_h, starts_h,
    gres_o, state_o, sgrad_o, nw_o, nm_o,
    ids_ref, slot_ref, starts_ref, og, q, k, v, g, res, router, hid, w, m,
    ph1, info, inf, tab, s2, r2, arr, hp,
    f32buf, fsend, frecv, ssend, srecv, state, asend, arecv, bsend, brecv,
    prow, allowed, carried, mixed, qcar, cot, small, wsend, wmid, wrecv, csend, cmid, crecv, gbuf, cum_s,
    in_sem, out_sem, s1_s, s1_r, i1_s, i1_r, s2_s, s2_r, s3_s, s3_r, f_s, f_r, b_s, b_r,
    w1_s, w1_r, w2_s, w2_r, c1_s, c1_r, c2_s, c2_r, a_s, a_r, e_s, e_r,
):
    ctx, ex = lax.axis_index("ctx"), lax.axis_index("exp")
    here = (lax.div(ctx, SIDE), lax.rem(ctx, SIDE), lax.div(ex, 2), lax.rem(ex, 2))

    def at(coords):
        return (coords[0] * SIDE + coords[1], coords[2] * 2 + coords[3])

    def moved(axis, by, flip=False):
        c = list(here)
        c[axis] = lax.rem(c[axis] + by, SIDE)
        if flip:
            c[3] = 1 - c[3]
        return tuple(c)

    def remote(src, dst, ss, rs, device):
        return pltpu.make_async_remote_copy(
            src_ref=src, dst_ref=dst, send_sem=ss, recv_sem=rs, device_id=device, device_id_type=MESH
        )

    barrier = pltpu.get_barrier_semaphore()

    def tell(device):
        pl.semaphore_signal(barrier, inc=1, device_id=device, device_id_type=MESH)

    def tell_ctx(i, _):
        tell((lax.rem(ctx + i, CTX), ex))
        return 0

    def tell_exp(i, _):
        tell((ctx, lax.rem(ex + i, 8)))
        return 0

    lax.fori_loop(1, CTX, tell_ctx, 0)
    lax.fori_loop(1, 8, tell_exp, 0)
    for axis in (0, 1):
        for by in (1, 2, 3):
            tell(at(moved(axis, by, True)))
    loads = []
    for n, (a, b) in enumerate(
        ((ids_h, ids_ref), (slot_h, slot_ref), (starts_h, starts_ref), (og_h, og), (k_h, k), (v_h, v), (g_h, g), (q_h, q), (res_h, res), (router_h, router), (hid_h, hid), (w_h, w), (m_h, m))
    ):
        loads.append(pltpu.make_async_copy(a, b, in_sem.at[n]))
        loads[-1].start()

    small_loads, loads = loads[:3], loads[3:]
    for cp in small_loads:
        cp.wait()
    info[0:TOP] = ids_ref[...].astype(F32)
    info[TOP:2 * TOP] = slot_ref[...].astype(F32)

    pl.semaphore_wait(barrier, CTX - 1 + 7 + 6)

    loads[0].wait()
    sends = []

    def send(src, dst, ss, rs, device):
        cp = remote(src, dst, ss, rs, device)
        cp.start()
        sends.append(cp)

    def rows_of(n, size):
        return pl.ds(pl.multiple_of(n * size, size), size)

    for by in (1, 3, 2):
        for i in range(3):
            send(info, inf.at[i, here[i]], i1_s.at[i, by], i1_r.at[i, here[i]], at(moved(i, by)))
    for h in range(2):
        for by in (1, 3, 2):
            for i in range(3):
                send(og.at[:, half_lanes(i, h)], ph1.at[rows_of(here[i], TOK), half_lanes(i, h)],
                     s1_s.at[i, h, by], s1_r.at[i, h, here[i]], at(moved(i, by)))
    for i in range(3):
        for h in range(2):
            pltpu.make_async_copy(
                og.at[:, half_lanes(i, h)], ph1.at[rows_of(here[i], TOK), half_lanes(i, h)],
                s1_r.at[i, h, here[i]]).start()
        pltpu.make_async_copy(info, inf.at[i, here[i]], i1_r.at[i, here[i]]).start()

    for n in (1, 2, 3):
        loads[n].wait()
    seg_row, seg_col = segments(starts_ref)
    last_seg = seg_row[:, TOK - 1:TOK]
    tri = lower_ones()
    allowed[...] = jnp.where(
        (seg_row == seg_col) & (iota((TOK, TOK), 0) >= iota((TOK, TOK), 1)), 1.0, 0.0)
    carried[...] = jnp.broadcast_to(jnp.where(seg_col == 0.0, 1.0, 0.0), (TOK, TOK))
    tail = jnp.broadcast_to(jnp.where(seg_col == last_seg, 1.0, 0.0), (TOK, TOK))
    unbroken = jnp.where(last_seg == 0.0, 1.0, 0.0)
    prow[...] = jnp.zeros_like(prow)

    def own_state(h, _):
        cum = dot(tri, g[:, head(h)])
        cum_s[:, head(h)] = cum
        last = cum[TOK - 1:TOK]
        key_end = (k[:, head(h)].astype(F32) * jnp.exp(last - cum) * tail).astype(BF)
        fresh = dot(v[:, head(h)], key_end, TN)
        f32buf[:, rows_of(h, 8), :] = fresh.reshape(CTX, 8, HD)
        prow[pl.ds(h, 1), :] = jnp.exp(last) * unbroken
        return 0

    lax.fori_loop(0, HEADS, own_state, 0, unroll=UNROLL)
    passing = prow[...].astype(BF)

    def pack(j, _):
        fsend[j, 0:GROUP, :] = f32buf[j].astype(BF)
        fsend[j, GROUP:PACK, :] = passing
        return 0

    lax.fori_loop(0, CTX, pack, 0, unroll=4)

    def ctx_exchange(src, dst, ss, rs, rows=None):
        def of(ref, n):
            return ref.at[n] if rows is None else ref.at[n, rows]

        def one(i, _):
            i7 = lax.rem(i * 7, CTX)
            t = lax.rem(here[0] + lax.div(i7, SIDE), SIDE) * SIDE + lax.rem(here[1] + lax.rem(i7, SIDE), SIDE)
            remote(of(src, t), of(dst, ctx), ss.at[i], rs.at[ctx], (t, ex)).start()
            return 0

        lax.fori_loop(1, CTX, one, 0)
        pltpu.make_async_copy(of(src, ctx), of(dst, ctx), rs.at[ctx]).start()

    def ctx_arrive(src, dst, ss, rs, rows=None):
        def one(i, _):
            a, b = (src.at[0], dst.at[i]) if rows is None else (src.at[0, rows], dst.at[i, rows])
            pltpu.make_async_copy(a, b, rs.at[i]).wait()
            return 0

        lax.fori_loop(0, CTX, one, 0)

    def ctx_sent(src, dst, ss, rs, rows=None):
        def one(i, _):
            a, b = (src.at[0], dst.at[0]) if rows is None else (src.at[0, rows], dst.at[0, rows])
            pltpu.make_async_copy(a, b, ss.at[i]).wait()
            return 0

        lax.fori_loop(1, CTX, one, 0)

    ctx_exchange(fsend, frecv, f_s, f_r)

    pat_a, pat_s = digits(iota((48, SIDE * TOK), 0).astype(F32), (SLOTS,))
    pattern = jnp.where(pat_a == floor_div(iota((48, SIDE * TOK), 1).astype(F32), TOK), pat_s, -5.0)
    bb, cc, kk = digits(iota((32, TOK), 0).astype(F32), (SIDE, 2))
    for i, (A, B, C) in enumerate(AXES):
        e = bb * STRIDE[B] + cc * STRIDE[C] + kk + (here[A] * STRIDE[A]).astype(F32)
        for a in range(SIDE):
            pltpu.make_async_copy(info, inf.at[i, a], i1_r.at[i, a]).wait()
            found = jnp.full((32, TOK), -1.0, F32)
            for j in range(TOP):
                found = jnp.where(inf[i, a, j:j + 1, :] == e, inf[i, a, TOP + j:TOP + j + 1, :], found)
            tab[i, :, a * TOK:(a + 1) * TOK] = found

    def choose(i, b):
        blocks = []
        for m_ in range(8):
            line = tab[i, pl.ds(b * 8 + m_, 1), :]
            blocks.append(jnp.where(line == pattern, 1.0, 0.0).astype(BF))
        hp[i, rows_of(b, 384)] = jnp.concatenate(blocks, axis=0)

    def half(i, h):
        return slice(STARTS[i] + h * (PARTS[i] // 2), STARTS[i] + (h + 1) * (PARTS[i] // 2))

    def select(i, h, b):
        return dot(hp[i, rows_of(b, 384)], ph1[:, half(i, h)]).astype(BF)

    for h in range(2):
        for by in (1, 3, 2):
            for i, (A, B, C) in enumerate(AXES):
                b = lax.rem(here[B] + by, SIDE)
                if h == 0:
                    choose(i, b)
                if by == 1:
                    for a in range(SIDE):
                        pltpu.make_async_copy(
                            og.at[:, half_lanes(i, h)], ph1.at[pl.ds(a * TOK, TOK), half_lanes(i, h)],
                            s1_r.at[i, h, a]).wait()
                s2[rows_of(b, 384), half(i, h)] = select(i, h, b)
                remote(s2.at[rows_of(b, 384), half_lanes(i, h)], r2.at[rows_of(here[B], 384), half_lanes(i, h)],
                       s2_s.at[i, h, by], s2_r.at[i, h, here[B]], at(moved(B, by))).start()
    for i, (A, B, C) in enumerate(AXES):
        choose(i, here[B])
        for h in range(2):
            r2[rows_of(here[B], 384), half(i, h)] = select(i, h, here[B])

    def onward(b_by):
        for i, (A, B, C) in enumerate(AXES):
            b = lax.rem(here[B] + b_by, SIDE)
            if b_by:
                for h in range(2):
                    pltpu.make_async_copy(
                        s2.at[pl.ds(0, 384), half_lanes(i, h)], r2.at[rows_of(b, 384), half_lanes(i, h)],
                        s2_r.at[i, h, b]).wait()
            slot = here[3] * SIDE + here[C]
            for by in (2, 1, 3, 0):
                for flip in (0, 1):
                    to = moved(C, by, bool(flip))
                    src = r2.at[rows_of(b * 8 + to[C] * 2 + to[3], 48), lanes(i)]
                    dst = arr.at[rows_of(b * 8 + slot, 48), lanes(i)]
                    if by == 0 and flip == 0:
                        pltpu.make_async_copy(src, dst, s3_r.at[i, b]).start()
                    else:
                        send(src, dst, s3_s.at[i, by * 2 + flip, b_by], s3_r.at[i, b], at(to))

    onward(0)

    ctx_arrive(fsend, frecv, f_s, f_r)

    def factor(j, first=0, last=HEADS):
        p = frecv[j, GROUP:PACK, :].astype(F32)
        return jnp.concatenate([jnp.broadcast_to(p[h:h + 1], (8, HD)) for h in range(first, last)], axis=0)

    def forward(j, acc):
        ssend[j] = acc.astype(BF)
        return factor(j) * acc + frecv[j, 0:GROUP, :].astype(F32)

    lax.fori_loop(0, CTX, forward, jnp.zeros((GROUP, HD), F32), unroll=2)
    ctx_exchange(ssend, srecv, b_s, b_r)

    loads[7].wait()
    d = iota((384, 1), 0).astype(F32)
    lanes384 = iota((384, 384), 1)

    def pick_from(where):
        return jnp.where(lanes384 == where.astype(I32), 1.0, 0.0).astype(BF)

    core_, z_, x_, s_ = digits(d, (SIDE, SIDE, SLOTS))
    pick = pick_from(x_ * 96 + z_ * 24 + core_ * 12 + s_)
    for y in range(SIDE):
        block = jnp.concatenate([hid[x * 384 + y * 96:x * 384 + y * 96 + 96, :] for x in range(SIDE)], axis=0)
        hp[0, y * 384:y * 384 + 384] = dot(pick, block).astype(BF)
    z_, core_, y_, s_ = digits(d, (2, SIDE, SLOTS))
    pick = pick_from(y_ * 96 + z_ * 24 + core_ * 12 + s_)
    for x in range(SIDE):
        got = dot(pick, hid[x * 384:x * 384 + 384, :]).astype(BF)
        for n in range(8):
            to = n // 2 * 384 + (n % 2 * SIDE + x) * 48
            hp[1, to:to + 48] = got[n * 48:n * 48 + 48]
    core_, y_, z_, s_ = digits(d, (SIDE, SIDE, SLOTS))
    pick = pick_from(y_ * 96 + z_ * 24 + core_ * 12 + s_)
    for x in range(SIDE):
        hp[2, x * 384:x * 384 + 384] = dot(pick, hid[x * 384:x * 384 + 384, :]).astype(BF)

    onward(1)
    onward(3)
    onward(2)

    for n in (4, 5, 6):
        loads[n].wait()
    ctx_arrive(ssend, srecv, b_s, b_r)

    def widen(j, _):
        f32buf[j] = srecv[j].astype(F32)
        return 0

    lax.fori_loop(0, CTX, widen, 0, unroll=4)

    def attend(h, _):
        cum = cum_s[:, head(h)]
        q_dec = q[:, head(h)].astype(F32) * jnp.exp(cum)
        k_dec = (k[:, head(h)].astype(F32) * jnp.exp(-cum)).astype(BF)
        scores = (dot(q_dec.astype(BF), k_dec, NT) * allowed[...]).astype(BF)
        q_c = (q_dec * carried[...]).astype(BF)
        qcar[:, head(h)] = q_c
        st = f32buf[:, rows_of(h, 8), :].reshape(HD, HD).astype(BF)
        state[h] = st
        out = SCALING * (dot(scores, v[:, head(h)]) + dot(q_c, st, NT))
        mixed[:, head(h)] = res[:, head(h)].astype(F32) + out.astype(BF).astype(F32)
        return 0

    lax.fori_loop(0, HEADS, attend, 0, unroll=UNROLL)
    state_out = pltpu.make_async_copy(state, state_o, out_sem.at[0])
    state_out.start()

    def lane_sum(x):
        acc = x[:, 0:HD]
        for n in range(1, x.shape[1] // HD):
            acc = acc + x[:, n * HD:(n + 1) * HD]
        return jnp.sum(acc, axis=1, keepdims=True)

    sq = sum(lane_sum(mixed[:, part(i)] * mixed[:, part(i)]) for i in range(3))
    inverse = lax.rsqrt(sq * (1.0 / WIDTH) + NORM_EPS)
    logits = sum(dot((mixed[:, part(i)] * inverse).astype(BF), router[part(i), :]) for i in range(3))
    rank_t = jnp.full((EXPERTS, TOK), -1.0, F32)
    for j in range(TOP):
        eq = info[j:j + 1, :] == iota((EXPERTS, TOK), 0).astype(F32)
        rank_t = jnp.where(eq, info[TOP + j:TOP + j + 1, :], rank_t)
    rank = jnp.transpose(rank_t)
    chosen = jnp.where(rank >= 0.0, 1.0, 0.0)
    gate = chosen * jax.nn.sigmoid(logits)
    total = jnp.sum(gate, axis=1, keepdims=True)
    weights = gate / total
    w_round = weights.astype(BF).astype(F32)
    rows_ = []
    for s in range(SLOTS):
        rows_.append(jnp.sum(jnp.where(rank == float(s), w_round, 0.0), axis=0, keepdims=True))
    w_t = jnp.concatenate(rows_ + [jnp.zeros((4, EXPERTS), F32)], axis=0).astype(BF)
    turn_e, turn_c = digits(iota((EXPERTS, EXPERTS), 0).astype(F32), (CTX,))
    turn = jnp.where(turn_c * 8 + turn_e == iota((EXPERTS, EXPERTS), 1).astype(F32), 1.0, 0.0).astype(BF)
    small[...] = jnp.zeros_like(small)
    small[:, 0:16] = dot(turn, w_t, NT)
    wsend[...] = small[...].reshape(8, CTX, EXPERTS)

    def exp_out(src, dst, ss, rs):
        def one(i, _):
            t = lax.rem(ex + i, 8)
            remote(src.at[t], dst.at[:, ex], ss.at[i], rs.at[ex], (ctx, t)).start()
            return 0

        lax.fori_loop(1, 8, one, 0)
        pltpu.make_async_copy(src.at[ex], dst.at[:, ex], rs.at[ex]).start()

    def exp_in(src, dst, ss, rs):
        def one(i, _):
            pltpu.make_async_copy(src.at[0], dst.at[:, i], rs.at[i]).wait()
            return 0

        lax.fori_loop(0, 8, one, 0)

    def exp_sent(src, dst, ss, rs):
        def one(i, _):
            pltpu.make_async_copy(src.at[0], dst.at[:, 0], ss.at[i]).wait()
            return 0

        lax.fori_loop(1, 8, one, 0)

    exp_out(wsend, wmid, w1_s, w1_r)

    for i in range(3):
        for by in (1, 2, 3):
            for h in range(2):
                pltpu.make_async_copy(
                    s2.at[pl.ds(0, 384), half_lanes(i, h)], r2.at[pl.ds(0, 384), half_lanes(i, h)],
                    s2_s.at[i, h, by]).wait()
    loads[8].wait()
    for i in range(3):
        def produce(n, _, i=i):
            s2[rows_of(n, 384), part(i)] = dot(hp[i, rows_of(n, 384)], w[:, part(i)]).astype(BF)
            return 0

        lax.fori_loop(0, SIDE, produce, 0)
    exp_in(wsend, wmid, w1_s, w1_r)
    ctx_exchange(wmid, wrecv, w2_s, w2_r)

    p_core, p_c, p_a, p_s = digits(d, (SIDE, SIDE, SLOTS))
    lanes_r = iota((384, EXPERTS), 1)
    own_slot = lanes_r == p_s.astype(I32)
    small[...] = jnp.zeros_like(small)

    def score_group(b_by):
        for i, (A, B, C) in enumerate(AXES):
            b = lax.rem(here[B] + b_by, SIDE)
            rows = rows_of(b, 384)
            pltpu.make_async_copy(s2.at[pl.ds(0, 384), lanes(i)], arr.at[rows, lanes(i)], s3_r.at[i, b]).wait()
            score = lane_sum(s2[rows, part(i)].astype(F32) * arr[rows, part(i)].astype(F32))
            at_slot = jnp.where(own_slot, score, 0.0)
            coord = [None, None, None]
            coord[A], coord[B], coord[C] = p_a, b.astype(F32), p_c
            to = (coord[2] * 2 + p_core) * CTX + coord[0] * SIDE + coord[1]
            spread = jnp.where(lanes_r == to.astype(I32), 1.0, 0.0).astype(BF)
            hi, lo = split(at_slot)
            small[...] += dot(spread, hi, TN) + dot(spread, lo, TN)

    def grad_group(i, b_by):
        A, B, C = AXES[i]
        b = lax.rem(here[B] + b_by, SIDE)
        src = p_a * STRIDE[A] + b.astype(F32) * STRIDE[B] + p_c * STRIDE[C] + p_core
        pick = jnp.where(lanes_r == src.astype(I32), 1.0, 0.0).astype(BF)
        w_in = wrecv[...].reshape(EXPERTS, EXPERTS).astype(BF)
        col = jnp.sum(jnp.where(own_slot, dot(pick, w_in), 0.0), axis=1, keepdims=True)
        scaled = (arr[rows_of(b, 384), part(i)].astype(F32) * col).astype(BF)
        piece = dot(hp[i, rows_of(b, 384)], scaled, TN)
        if b_by == 0:
            gbuf[:, 0:PARTS[i]] = piece
        else:
            gbuf[:, 0:PARTS[i]] += piece

    grads = []

    def last_grad(i):
        for by in range(SIDE):
            grad_group(i, by)

        def step(n, _):
            r = rows_of(n, 64)
            wf, mf, gf = w[r, part(i)].astype(F32), m[r, part(i)].astype(F32), gbuf[r, 0:PARTS[i]]
            turn = BETA_ONE * mf + (1.0 - BETA_ONE) * gf
            move = jnp.where(turn > 0.0, -LION_RATE, jnp.where(turn < 0.0, LION_RATE, 0.0))
            w[r, part(i)] = (wf * (1.0 - LION_RATE * WEIGHT_DECAY) + move).astype(BF)
            m[r, part(i)] = (BETA_TWO * mf + (1.0 - BETA_TWO) * gf).astype(BF)
            return 0

        lax.fori_loop(0, FF // 64, step, 0)
        for n, (a, b) in enumerate(((w, nw_o), (m, nm_o))):
            cp = pltpu.make_async_copy(a.at[:, lanes(i)], b.at[:, lanes(i)], out_sem.at[3 + 2 * i + n])
            cp.start()
            grads.append(cp)

    score_group(0)
    score_group(1)
    score_group(3)
    score_group(2)
    csend[...] = small[...].reshape(8, CTX, EXPERTS)
    exp_out(csend, cmid, c1_s, c1_r)
    exp_in(csend, cmid, c1_s, c1_r)
    ctx_exchange(cmid, crecv, c2_s, c2_r)
    ctx_arrive(wmid, wrecv, w2_s, w2_r)
    loads[9].wait()
    last_grad(2)
    ctx_arrive(cmid, crecv, c2_s, c2_r)

    back = jnp.transpose(crecv[...].reshape(EXPERTS, EXPERTS))
    prob = jnp.zeros((TOK, EXPERTS), F32)
    for s in range(SLOTS):
        prob = jnp.where(rank == float(s), back[s:s + 1], prob)
    mix = jnp.sum(weights * prob, axis=1, keepdims=True)
    logit_grad = (chosen * ((prob - mix) / total * gate * (1.0 - gate))).astype(BF)
    mean = 0.0
    for i in range(3):
        ng = dot(logit_grad, router[part(i), :], NT)
        cum_s[:, part(i)] = ng
        mean = mean + lane_sum(ng * mixed[:, part(i)])
    pull = inverse * inverse * inverse * (mean * (1.0 / WIDTH))

    def residual(h, _):
        grad = (
            og[:, head(h)].astype(F32) + inverse * cum_s[:, head(h)] - mixed[:, head(h)] * pull
        ).astype(BF)
        cot[:, head(h)] = grad
        adj = SCALING * dot(grad, qcar[:, head(h)], TN)
        f32buf[:, rows_of(h, 8), :] = adj.reshape(CTX, 8, HD)
        return 0

    halves = ((0, 10), (10, HEADS))

    def half_rows(n):
        first, last = halves[n]
        return pl.ds(first * 8, (last - first) * 8)

    for n, (first, last) in enumerate(halves):
        lax.fori_loop(first, last, residual, 0, unroll=last - first)

        def pack_back(j, _, n=n):
            asend[j, half_rows(n), :] = f32buf[j, half_rows(n), :].astype(BF)
            return 0

        lax.fori_loop(0, CTX, pack_back, 0, unroll=4)
        ctx_exchange(asend, arecv, a_s.at[n], a_r.at[n], half_rows(n))
    gres_out = pltpu.make_async_copy(cot, gres_o, out_sem.at[1])
    gres_out.start()
    last_grad(0)
    for n, (first, last) in enumerate(halves):
        ctx_arrive(asend, arecv, a_s.at[n], a_r.at[n], half_rows(n))

        def backward(t, acc, n=n, first=first, last=last):
            j = CTX - 1 - t
            bsend[j, half_rows(n), :] = acc.astype(BF)
            return factor(j, first, last) * acc + arecv[j, half_rows(n), :].astype(F32)

        lax.fori_loop(0, CTX, backward, jnp.zeros(((last - first) * 8, HD), F32), unroll=4)
        ctx_exchange(bsend, brecv, e_s.at[n], e_r.at[n], half_rows(n))
    last_grad(1)
    for n in range(2):
        ctx_arrive(bsend, brecv, e_s.at[n], e_r.at[n], half_rows(n))

    def widen_back(j, _):
        f32buf[j] = brecv[j].astype(F32)
        return 0

    lax.fori_loop(0, CTX, widen_back, 0, unroll=4)
    state_out.wait()

    def gather(h, _):
        state[h] = f32buf[:, rows_of(h, 8), :].reshape(HD, HD).astype(BF)
        return 0

    lax.fori_loop(0, HEADS, gather, 0, unroll=UNROLL)
    sgrad_out = pltpu.make_async_copy(state, sgrad_o, out_sem.at[2])
    sgrad_out.start()

    for cp in sends:
        cp.wait_send()
    ctx_sent(fsend, frecv, f_s, f_r)
    ctx_sent(ssend, srecv, b_s, b_r)
    for n in range(2):
        ctx_sent(asend, arecv, a_s.at[n], a_r.at[n], half_rows(n))
        ctx_sent(bsend, brecv, e_s.at[n], e_r.at[n], half_rows(n))
    exp_sent(wsend, wmid, w1_s, w1_r)
    exp_sent(csend, cmid, c1_s, c1_r)
    ctx_sent(wmid, wrecv, w2_s, w2_r)
    ctx_sent(cmid, crecv, c2_s, c2_r)
    gres_out.wait()
    sgrad_out.wait()
    for cp in grads:
        cp.wait()


def finish(
    q_h, k_h, v_h, g_h, cot_h, state_h, sgrad_h, starts_ref, stepped_h, moment_h,
    dq_h, dk_h, dv_h, dg_h, gres_h, nw_h, nm_h,
    q, k, v, g, cot, state, sgrad, stepped, moment, dq, dk, dv, dg, in_sem, out_sem, pass_sem,
):
    wide = PER * HD
    head_steps = HEADS // PER

    def cols(n):
        return pl.ds(n * wide, wide)

    def loads(n):
        out = [
            pltpu.make_async_copy(a.at[:, cols(n)], b.at[:, cols(n)], in_sem.at[n, j])
            for j, (a, b) in enumerate(((g_h, g), (k_h, k), (q_h, q), (v_h, v), (cot_h, cot)))
        ]
        for j, (a, b) in enumerate(((state_h, state), (sgrad_h, sgrad))):
            out.append(pltpu.make_async_copy(a.at[pl.ds(n * PER, PER)], b.at[pl.ds(n * PER, PER)], in_sem.at[n, 5 + j]))
        return out

    stores = []

    def store(a, b, sem):
        cp = pltpu.make_async_copy(a, b, sem)
        cp.start()
        stores.append(cp)

    order = [loads(n) for n in range(head_steps)]
    for copies in order:
        for cp in copies:
            cp.start()
    through = []
    for j, (a, b) in enumerate(((stepped_h, stepped), (moment_h, moment))):
        through.append(pltpu.make_async_copy(a, b, pass_sem.at[j]))
        through[-1].start()

    seg_row, seg_col = segments(starts_ref)
    last_seg = seg_row[:, TOK - 1:TOK]
    lower = iota((TOK, TOK), 0) >= iota((TOK, TOK), 1)
    upper = iota((TOK, TOK), 0) <= iota((TOK, TOK), 1)
    tri, tri_up = lower.astype(F32).astype(BF), upper.astype(F32).astype(BF)
    same = seg_row == seg_col
    below = jnp.where(same & lower, SCALING, 0.0)
    above = jnp.where(same & upper, SCALING, 0.0)
    carried = jnp.where(seg_col == 0.0, SCALING, 0.0)
    tail = jnp.where(seg_col == last_seg, 1.0, 0.0)
    unbroken = jnp.where(last_seg == 0.0, 1.0, 0.0)

    def heads_step(n):
        at_ = slice(n * wide, (n + 1) * wide)
        store(cot.at[:, cols(n)], gres_h.at[:, cols(n)], out_sem.at[n, 4])
        cum = dot(tri, g[:, at_])
        last = cum[TOK - 1:TOK]
        grow, shrink, to_end = jnp.exp(cum), jnp.exp(-cum), jnp.exp(last - cum) * tail
        kf = k[:, at_].astype(F32)
        q_dec = (q[:, at_].astype(F32) * grow).astype(BF)
        k_dec = (kf * shrink).astype(BF)
        key_end = (kf * to_end).astype(BF)
        d_cums, d_lasts = [], []
        R = range(PER)
        part = [slice(j * HD, (j + 1) * HD) for j in R]
        full = [slice(n * wide + j * HD, n * wide + (j + 1) * HD) for j in R]
        vs, cs = [v[:, c] for c in full], [cot[:, c] for c in full]
        scores_t = [(above * dot(k_dec[:, c], q_dec[:, c], NT)).astype(BF) for c in part]
        d_scores = [(below * dot(cs[j], vs[j], NT)).astype(BF) for j in R]
        d_scores_t = [(above * dot(vs[j], cs[j], NT)).astype(BF) for j in R]
        dq_dec = [dot(d_scores[j], k_dec[:, part[j]]) + carried * dot(cs[j], state[n * PER + j]) for j in R]
        dk_dec = [dot(d_scores_t[j], q_dec[:, part[j]]) for j in R]
        dk_end = [dot(vs[j], sgrad[n * PER + j]) for j in R]
        for j in R:
            c, f, st, sg = part[j], full[j], state[n * PER + j], sgrad[n * PER + j]
            dv[:, f] = (dot(scores_t[j], cs[j]) + dot(key_end[:, c], sg, NT)).astype(BF)
            dq[:, f] = (dq_dec[j] * grow[:, c]).astype(BF)
            dk[:, f] = (dk_dec[j] * shrink[:, c] + dk_end[j] * to_end[:, c]).astype(BF)
            end_term = dk_end[j] * key_end[:, c].astype(F32)
            d_cums.append(dq_dec[j] * q_dec[:, c].astype(F32) - dk_dec[j] * k_dec[:, c].astype(F32) - end_term)
            d_lasts.append(
                jnp.sum(end_term, axis=0, keepdims=True)
                + unbroken * jnp.exp(last[:, c]) * jnp.sum(st.astype(F32) * sg.astype(F32), axis=0, keepdims=True))
        hi, lo = split(jnp.concatenate(d_cums, axis=1))
        dg[:, at_] = (dot(tri_up, hi) + dot(tri_up, lo) + jnp.concatenate(d_lasts, axis=1)).astype(BF)
        for j, (a, b) in enumerate(((dq, dq_h), (dk, dk_h), (dv, dv_h), (dg, dg_h))):
            store(a.at[:, cols(n)], b.at[:, cols(n)], out_sem.at[n, j])

    for n, copies in enumerate(order):
        for cp in copies:
            cp.wait()
        heads_step(n)
        through[n].wait()
        store((stepped, moment)[n], (nw_h, nm_h)[n], pass_sem.at[n + 2])
    for cp in stores:
        cp.wait()


def local(
    queries, key_vectors, values, log_decay, starts, residual_in, out_grad,
    expert_ids, slot_index, router, hidden_saved, w_down, momentum,
):
    any_, vm = pl.BlockSpec(memory_space=pl.ANY), pl.BlockSpec(memory_space=pltpu.VMEM)
    dma = pltpu.SemaphoreType.DMA
    V = pltpu.VMEM
    scratch = [
        V((TOP, TOK), I32), V((TOP, TOK), I32), V((1, TOK), I32),
        *[V((TOK, WIDTH), BF)] * 6, V((WIDTH, EXPERTS), BF), V((CAP, FF), BF), V((FF, WIDTH), BF), V((FF, WIDTH), BF),
        V((SIDE * TOK, WIDTH), BF), V((16, TOK), F32), V((3, SIDE, 16, TOK), F32), V((3, 32, SIDE * TOK), F32),
        *[V((CAP, WIDTH), BF)] * 3,
        V((3, CAP, FF), BF),
        V((CTX, GROUP, HD), F32), V((CTX, PACK, HD), BF), V((CTX, PACK, HD), BF),
        V((CTX, GROUP, HD), BF), V((CTX, GROUP, HD), BF), V((HEADS, HD, HD), BF),
        *[V((CTX, GROUP, HD), BF)] * 4,
        V((32, HD), F32), V((TOK, TOK), F32), V((TOK, TOK), F32), V((TOK, WIDTH), F32),
        V((TOK, WIDTH), BF), V((TOK, WIDTH), BF), V((EXPERTS, EXPERTS), F32),
        V((8, CTX, EXPERTS), F32), V((CTX, 8, EXPERTS), F32), V((CTX, 8, EXPERTS), F32),
        V((8, CTX, EXPERTS), F32), V((CTX, 8, EXPERTS), F32), V((CTX, 8, EXPERTS), F32),
        V((FF, max(PARTS)), F32), V((TOK, WIDTH), F32),
        dma((13,)), dma((9,)),
        dma((3, 2, 4)), dma((3, 2, 4)), dma((3, 4)), dma((3, 4)), dma((3, 2, 4)), dma((3, 2, 4)), dma((3, 8, 4)), dma((3, 4)),
        dma((CTX,)), dma((CTX,)), dma((CTX,)), dma((CTX,)),
        dma((8,)), dma((8,)), dma((CTX,)), dma((CTX,)), dma((8,)), dma((8,)), dma((CTX,)), dma((CTX,)),
        dma((2, CTX)), dma((2, CTX)), dma((2, CTX)), dma((2, CTX)),
    ]
    gres, state, sgrad, stepped, moment = pl.pallas_call(
        mixer,
        name="dispatch_and_scan",
        out_shape=(
            jax.ShapeDtypeStruct((TOK, WIDTH), BF),
            jax.ShapeDtypeStruct((HEADS, HD, HD), BF),
            jax.ShapeDtypeStruct((HEADS, HD, HD), BF),
            jax.ShapeDtypeStruct((FF, WIDTH), BF),
            jax.ShapeDtypeStruct((FF, WIDTH), BF),
        ),
        in_specs=[any_] * 13,
        out_specs=(any_,) * 5,
        scratch_shapes=scratch,
        compiler_params=pltpu.CompilerParams(
            collective_id=0, has_side_effects=True, vmem_limit_bytes=62 * 2**20),
    )(
        out_grad[0], queries[0], key_vectors[0], values[0], log_decay[0], residual_in[0], router,
        hidden_saved[0], w_down[0], momentum[0], expert_ids[0].T, slot_index[0].T, starts,
    )
    tok = V((TOK, WIDTH), BF)
    outs = pl.pallas_call(
        finish,
        name="backward_and_step",
        out_shape=(jax.ShapeDtypeStruct((TOK, WIDTH), BF),) * 5 + (jax.ShapeDtypeStruct((FF, WIDTH), BF),) * 2,
        in_specs=[any_] * 7 + [vm] + [any_] * 2,
        out_specs=(any_,) * 7,
        scratch_shapes=[
            *[tok] * 5, *[V((HEADS, HD, HD), BF)] * 2, *[V((FF, WIDTH), BF)] * 2, *[tok] * 4,
            dma((HEADS // PER, 7)), dma((HEADS // PER, 5)), dma((4,)),
        ],
        compiler_params=pltpu.CompilerParams(vmem_limit_bytes=62 * 2**20),
    )(
        queries[0], key_vectors[0], values[0], log_decay[0], gres, state, sgrad, starts,
        stepped, moment,
    )
    return tuple(x[None] for x in outs)


def solution(mesh):
    tokens = P("exp", "ctx", None)
    owned = P(("ctx", "exp"), None, None)
    in_specs = (tokens,) * 4 + (P("exp", "ctx"),) + (tokens,) * 4 + (P(),) + (owned,) * 3
    out_specs = (tokens,) * 5 + (owned,) * 2
    return jax.shard_map(local, mesh=mesh, in_specs=in_specs, out_specs=out_specs, check_vma=False)
```
